32 devices in a mesh: blk: 8 (over z, core), grp: 4 (over y, x).
Axes of the slice: x: 2, y: 2, z: 4, core: 2. Of those that a mesh axis runs over, the one named last changes fastest.
Arguments:
- ratings: bfloat16 [2, 8, 4, 64, 256, 256], P(None, 'blk', 'grp'), may hold values from -6 to 6
- row_index: int32 [2, 8, 4, 64], P(None, 'blk', 'grp'), may hold values from 0 to 7
- col_index: int32 [2, 8, 4, 64], P(None, 'blk', 'grp'), may hold values from 0 to 63
- row_mask: int32 [2, 8, 4, 64, 256], P(None, 'blk', 'grp'), may hold values 0 or 1
- counts: int32 [2, 8, 4], P(None, 'blk', 'grp'), may hold values from 21 to 64, as said below
- owner_list: int32 [2, 8], P(None, 'blk'), may hold values from 0 to 3
- user_factors: float32 [65536, 128], P(('blk', 'grp'))
- item_factors: float32 [131072, 128], P('blk'), may hold values from -2 to 2
Outputs:
- user_final: float32 [65536, 128], P(('blk', 'grp'))
- item_final: float32 [131072, 128], P(('blk', 'grp'))
The draws below stay inside these ranges and needn't reach their ends.
Inputs may be any that keep to these rules, and one draw needn't show every extreme that they name: `counts`: in every sub-epoch some device has exactly 64 live slots, and every device has at least a third of 64, rounded down.
All inputs are finite; a program needn't handle non-finite values. No bound on the sum of `row_mask` on one device may be relied on, other than what follows from the above.
Results may differ from the reference program's by a relative error of at most 0.02.
Values may be sent and summed in bfloat16 or wider, within the bound.
No kernel may reach another device: no remote copies, remote signals or barrier semaphores. Data moves between devices by JAX's collectives and lax.ppermute only.
A program may use at most 128 MiB of HBM per device.

```python
import jax
import jax.numpy as jnp
from jax import lax

RANK = 128
TILE = 256
UT_DEV = 8
ITEM_BLK = 16384
TMAX = 64
SUB = 2
BLOCKS = 8
MEMBERS = 4
USR_DEV = 2048
USERS = 65536
ITEMS = 131072
COLT = 64


def draw_counts(key, part):
    key = jax.random.fold_in(key, 2)
    first, second = jax.random.split(key)
    values = jax.random.randint(first, (SUB, BLOCKS * MEMBERS), TMAX // 3, TMAX + 1)
    chosen = jax.random.randint(second, (SUB, 1), 0, BLOCKS * MEMBERS)
    places = jnp.arange(BLOCKS * MEMBERS, dtype=jnp.int32)[None, :]
    values = jnp.where(places == chosen, TMAX, values)
    return values.reshape(SUB, BLOCKS, MEMBERS).astype(jnp.int32)


def draw_user_factors(key, part):
    key = jax.random.fold_in(key, 5)
    first, second = jax.random.split(key)
    low_log = jnp.log(0.1)
    high_log = jnp.log(0.8)
    values = jax.random.normal(second, (USERS, RANK), jnp.float32)
    scales = jnp.exp(jax.random.uniform(first, (USERS // TILE, 1, 1), jnp.float32, low_log, high_log))
    values = values.reshape(USERS // TILE, TILE, RANK) * scales
    return values.reshape(USERS, RANK).astype(jnp.float32)


def touch_ends(entries, stream_key, smallest, high):
    dims = entries.shape
    spot = [jax.random.randint(jax.random.fold_in(stream_key, axis), (), 0, dims[axis]) for axis in range(len(dims))]
    entries = entries.at[tuple(spot)].set(smallest)
    longest = dims.index(max(dims))
    spot[longest] = (spot[longest] + 1) % dims[longest]
    return entries.at[tuple(spot)].set(high)


def block_scale(stream_key, extent, cuts, least, high):
    gain = 1.0
    for dim, shards_of in cuts:
        heights = jax.random.uniform(jax.random.fold_in(jax.random.fold_in(stream_key, 6), dim), (shards_of,), jnp.float32, least / len(cuts), high / len(cuts))
        gain = gain * jnp.repeat(jnp.exp(heights), extent[dim] // shards_of).reshape((-1,) + (1,) * (len(extent) - 1 - dim))
    return gain


def gaussian(own_key, dims, width, most, cuts=(), held_as=jnp.bfloat16):
    array = width * jax.random.normal(own_key, dims, jnp.float32)
    if cuts:
        array = array * block_scale(own_key, dims, cuts, -0.22, 0.18)
    return jnp.clip(array, -most, most).astype(held_as)


def setup_inputs(seed: int = 0) -> dict:
    key_of = jax.random.split(jax.random.key(seed), 9)
    return {
        "ratings": gaussian(key_of[0], (SUB, BLOCKS, MEMBERS, TMAX, TILE, TILE), 1.0, 6.0, ((1, 8), (2, 4))),
        "row_index": touch_ends(jax.random.randint(key_of[1], (SUB, BLOCKS, MEMBERS, TMAX), 0, UT_DEV), jax.random.fold_in(key_of[1], 1), 0, UT_DEV - 1).astype(jnp.int32),
        "col_index": touch_ends(jax.random.randint(key_of[2], (SUB, BLOCKS, MEMBERS, TMAX), 0, COLT), jax.random.fold_in(key_of[2], 1), 0, COLT - 1).astype(jnp.int32),
        "row_mask": touch_ends((jax.random.randint(key_of[3], (SUB, BLOCKS, MEMBERS, TMAX, TILE), 0, 8) < 7).astype(jnp.int32), jax.random.fold_in(key_of[3], 1), 0, 1),
        "counts": draw_counts(jax.random.fold_in(key_of[8], 71), 0),
        "owner_list": touch_ends(jax.random.randint(key_of[5], (SUB, BLOCKS), 0, MEMBERS), jax.random.fold_in(key_of[5], 1), 0, MEMBERS - 1).astype(jnp.int32),
        "user_factors": draw_user_factors(jax.random.fold_in(key_of[8], 71), 0),
        "item_factors": gaussian(key_of[7], (ITEMS, RANK), 0.3, 2.0, ((0, 8),), jnp.float32),
    }


LEARN = 0.004
GRAM = 256.0
RIDGE = 1.0


def device_grads(user_tiles, item_tiles, tile_vals, rows_in, cols_in, mask_in, live_count):
    zero_user = jnp.zeros((UT_DEV, TILE, RANK), jnp.float32)
    zero_item = jnp.zeros((COLT, TILE, RANK), jnp.float32)

    def tile_step(carry, slot):
        grad_user, grad_item = carry
        row_tile = rows_in[slot]
        col_tile = cols_in[slot]
        user_part = user_tiles[row_tile]
        item_part = item_tiles[col_tile]
        predicted = jnp.dot(user_part, item_part.T, preferred_element_type=jnp.float32)
        weights = mask_in[slot].astype(jnp.float32)[:, None]
        errors = (weights * (predicted - tile_vals[slot].astype(jnp.float32))).astype(jnp.bfloat16)
        live = (slot < live_count).astype(jnp.float32)
        grad_user = grad_user.at[row_tile].add(live * jnp.dot(errors, item_part, preferred_element_type=jnp.float32))
        grad_item = grad_item.at[col_tile].add(live * jnp.dot(errors.T, user_part, preferred_element_type=jnp.float32))
        return (grad_user, grad_item), None

    (grad_user, grad_item), _ = lax.scan(tile_step, (zero_user, zero_item), jnp.arange(TMAX, dtype=jnp.int32))
    return grad_user, grad_item


def reference(ratings, row_index, col_index, row_mask, counts, owner_list, user_factors, item_factors):
    user_state = user_factors.reshape(BLOCKS, MEMBERS, USR_DEV, RANK)
    item_state = item_factors.reshape(BLOCKS, ITEM_BLK, RANK)
    identity = jnp.eye(RANK, dtype=jnp.float32)
    for epoch in range(SUB):
        current = jnp.roll(item_state, epoch, axis=0)

        def per_block(block_id):
            user_blk = user_state[block_id]
            item_blk = current[block_id]
            item_bf = item_blk.astype(jnp.bfloat16)
            user_bf = user_blk.astype(jnp.bfloat16)
            item_tiles = item_bf.reshape(COLT, TILE, RANK)

            def per_member(member):
                grad_user, grad_item = device_grads(
                    user_bf[member].reshape(UT_DEV, TILE, RANK), item_tiles,
                    ratings[epoch, block_id, member], row_index[epoch, block_id, member],
                    col_index[epoch, block_id, member], row_mask[epoch, block_id, member],
                    counts[epoch, block_id, member])
                return grad_user.reshape(USR_DEV, RANK), grad_item.reshape(ITEM_BLK, RANK).astype(jnp.bfloat16)

            user_grads, item_parts = lax.map(per_member, jnp.arange(MEMBERS, dtype=jnp.int32))
            owner_rows = user_bf[owner_list[epoch, block_id]]
            owner_gram = jnp.dot(owner_rows.T, owner_rows, preferred_element_type=jnp.float32) * (GRAM / USR_DEV) + RIDGE * identity
            item_gram = jnp.dot(item_bf.T, item_bf, preferred_element_type=jnp.float32) * (GRAM / ITEM_BLK) + RIDGE * identity
            user_pull = jnp.einsum("mur,rq->muq", user_blk, item_gram, precision=lax.Precision.HIGHEST)
            new_user = user_blk - LEARN * (user_grads + user_pull)
            item_grad = jnp.sum(item_parts.astype(jnp.float32), axis=0)
            item_pull = jnp.dot(item_blk, owner_gram, precision=lax.Precision.HIGHEST)
            new_item = item_blk - LEARN * (item_grad + item_pull)
            return new_user, new_item

        user_state, current = lax.map(per_block, jnp.arange(BLOCKS, dtype=jnp.int32))
        item_state = jnp.roll(current, -epoch, axis=0)
    user_final = user_state.reshape(USERS, RANK)
    item_final = jnp.roll(item_state, SUB, axis=0).reshape(ITEMS, RANK)
    return user_final, item_final
```

```python
import functools

import jax
import jax.numpy as jnp
from jax import lax
from jax.experimental import pallas as pl
from jax.experimental.pallas import tpu as pltpu
from jax.sharding import PartitionSpec as P

SUB = 2
LEARN = 0.004
GRAM = 256.0
RIDGE = 1.0
CHUNKS = 4
F32 = jnp.float32
BF16 = jnp.bfloat16

ANY = pl.BlockSpec(memory_space=pl.ANY)
SMEM = pl.BlockSpec(memory_space=pltpu.SMEM)
VMEM = pl.BlockSpec(memory_space=pltpu.VMEM)


def params(mib):
    return pltpu.CompilerParams(vmem_limit_bytes=mib * 1024 * 1024)


def gram_of(matrix):
    return lax.dot_general(matrix, matrix, (((0,), (0,)), ((), ())), preferred_element_type=F32)


def owned_gram(users_bf, owner, me):
    rank = users_bf.shape[1]
    eye = (
        lax.broadcasted_iota(jnp.int32, (rank, rank), 0)
        == lax.broadcasted_iota(jnp.int32, (rank, rank), 1)
    )
    own = gram_of(users_bf) * (GRAM / users_bf.shape[0]) + jnp.where(eye, RIDGE, 0.0)
    return jnp.where(owner == me, own, 0.0).astype(BF16)


def tile_kernel(epoch, chunk, members, shard_tiles, tile, pieces, first, *refs):
    me_ref, row_ref, col_ref, count_ref, owner_ref, ratings, mask_ref, users = refs[:8]
    sources = refs[8:8 + pieces]
    refs = refs[8 + pieces:]
    if not first:
        grad_in, gram_in = refs[:2]
        refs = refs[2:]
    send_a, keep_a, send_b, keep_b, grad_user, gram_item = refs[:6]
    refs = refs[6:]
    if first and epoch == 0:
        own_gram = refs[0]
        refs = refs[1:]
    users_f, items, items_f, parts, held, slots, sem_tile, sem_item, sem_user, sem_prev = refs

    me = me_ref[0]
    chunk_tiles = shard_tiles // CHUNKS
    rows = chunk_tiles * tile
    half = rows // 2
    top = members // 2

    user_copy = pltpu.make_async_copy(users, users_f, sem_user)
    user_copy.start()
    copies = []
    if epoch == 0:
        for r in range(members):
            start = (me ^ r) * (shard_tiles * tile) + chunk * rows
            start = pl.multiple_of(start, rows)
            copies.append(
                pltpu.make_async_copy(
                    sources[0].at[pl.ds(start, rows)], items_f.at[pl.ds(r * rows, rows)], sem_item.at[r]
                )
            )
    else:
        at = 0
        for i, source in enumerate(sources):
            copies.append(
                pltpu.make_async_copy(source, items.at[pl.ds(at, source.shape[0])], sem_item.at[i])
            )
            at += source.shape[0]
    for copy in copies:
        copy.start()

    def pick(t, found):
        slots[found] = t
        here = lax.rem(col_ref[epoch, 0, 0, t], shard_tiles) // chunk_tiles == chunk
        live = t < count_ref[epoch, 0, 0]
        return found + jnp.where(here & live, 1, 0).astype(jnp.int32)

    total = lax.fori_loop(0, col_ref.shape[3], pick, jnp.int32(0))

    def fetch(i):
        return pltpu.make_async_copy(ratings.at[epoch, 0, 0, slots[i]], held.at[i], sem_tile.at[i])

    def begin(i, _):
        fetch(i).start()
        return 0

    lax.fori_loop(0, total, begin, 0)

    parts[...] = jnp.zeros_like(parts)
    if first:
        grad_user[...] = jnp.zeros_like(grad_user)
        gram_item[...] = jnp.zeros_like(gram_item)
    else:
        prev = pltpu.make_async_copy(grad_in, grad_user, sem_prev)
        prev.start()
        gram_item[...] = gram_in[...]
    user_copy.wait()
    if epoch == 0:
        for r in range(members):
            copies[r].wait()
            items[pl.ds(r * rows, rows)] = items_f[pl.ds(r * rows, rows)].astype(BF16)
    else:
        for copy in copies:
            copy.wait()
    if not first:
        prev.wait()

    def one(i, valid):
        t = slots[i]
        row = pl.multiple_of(row_ref[epoch, 0, 0, t] * tile, tile)
        col = col_ref[epoch, 0, 0, t]
        place = ((col // shard_tiles) ^ me) * chunk_tiles + lax.rem(col, chunk_tiles)
        place = pl.multiple_of(place * tile, tile)
        user_part = users_f[pl.ds(row, tile)].astype(BF16)
        item_part = items[pl.ds(place, tile)]
        predicted = lax.dot_general(
            user_part, item_part, (((1,), (1,)), ((), ())), preferred_element_type=F32
        )
        weight = mask_ref[epoch, 0, 0, pl.ds(t, 1), :].astype(F32)
        weight = jnp.where(valid, weight, 0.0)
        weight = jnp.broadcast_to(weight, (128, tile)).T
        weight = jnp.concatenate([weight] * (tile // 128), axis=1)
        error = jnp.where(weight > 0.5, predicted - held[i].astype(F32), 0.0).astype(BF16)
        user_add = jnp.dot(error, item_part, preferred_element_type=F32)
        item_add = lax.dot_general(
            error, user_part, (((0,), (0,)), ((), ())), preferred_element_type=F32
        )
        return row, place, user_add, item_add

    def pair(j, _):
        i = 2 * j
        valid = i + 1 < total
        other = jnp.where(valid, i + 1, i)
        fetch(i).wait()

        @pl.when(valid)
        def _():
            fetch(other).wait()

        first_out = one(i, True)
        second_out = one(other, valid)
        for row, place, user_add, item_add in (first_out, second_out):
            grad_user[pl.ds(row, tile)] += user_add
            parts[pl.ds(place, tile)] += item_add
        return 0

    lax.fori_loop(0, (total + 1) // 2, pair, 0)

    spot_sa = spot_ka = spot_sb = spot_kb = 0
    for r in range(members):
        upper = parts[pl.ds(r * rows, half)].astype(BF16)
        lower = parts[pl.ds(r * rows + half, rows - half)].astype(BF16)
        if r & 1:
            send_a[spot_sa] = upper
            spot_sa += 1
        else:
            keep_a[spot_ka] = upper
            spot_ka += 1
        if r & top:
            send_b[spot_sb] = lower
            spot_sb += 1
        else:
            keep_b[spot_kb] = lower
            spot_kb += 1

    def add_gram(j, _):
        gram_item[...] += gram_of(items[pl.ds(pl.multiple_of(j * tile, tile), tile)])
        return 0

    lax.fori_loop(0, members * chunk_tiles, add_gram, 0)
    if first and epoch == 0:
        own_gram[...] = owned_gram(users_f[...].astype(BF16), owner_ref[epoch, 0], me)


def tile_call(epoch, chunk, members, scalars, ratings, row_mask, users, sources, carried):
    tile = ratings.shape[-1]
    slots = ratings.shape[3]
    user_rows, rank = users.shape
    first = carried is None
    if epoch == 0:
        block_rows = sources[0].shape[0]
    else:
        block_rows = sum(s.shape[0] for s in sources) * CHUNKS
    shard_tiles = block_rows // members // tile
    rows = shard_tiles // CHUNKS * tile
    half = rows // 2
    sd = jax.ShapeDtypeStruct
    out_shape = [sd((members // 2, half, rank), BF16)] * 2 + [sd((members // 2, rows - half, rank), BF16)] * 2
    out_shape += [sd((user_rows, rank), F32), sd((rank, rank), F32)]
    if first and epoch == 0:
        out_shape.append(sd((rank, rank), BF16))
    in_specs = [SMEM] * 5 + [ANY, VMEM, ANY] + [ANY] * len(sources)
    operands = [*scalars, ratings, row_mask, users, *sources]
    if not first:
        in_specs += [ANY, VMEM]
        operands += list(carried)
    flops = slots * tile * tile * rank * 6 // CHUNKS
    return pl.pallas_call(
        functools.partial(
            tile_kernel, epoch, chunk, members, shard_tiles, tile, len(sources), first
        ),
        out_shape=out_shape,
        in_specs=in_specs,
        out_specs=[VMEM] * len(out_shape),
        scratch_shapes=[
            pltpu.VMEM((user_rows, rank), F32),
            pltpu.VMEM((members * rows, rank), BF16),
            pltpu.VMEM((members * rows if epoch == 0 else 8, rank), F32),
            pltpu.VMEM((members * rows, rank), F32),
            pltpu.VMEM((slots, tile, tile), BF16),
            pltpu.SMEM((slots + 1,), jnp.int32),
            pltpu.SemaphoreType.DMA((slots,)),
            pltpu.SemaphoreType.DMA((max(members, len(sources)),)),
            pltpu.SemaphoreType.DMA,
            pltpu.SemaphoreType.DMA,
        ],
        compiler_params=params(32),
        cost_estimate=pl.CostEstimate(flops=flops, bytes_accessed=4 << 20, transcendentals=0),
        name=f"tiles_{epoch}_{chunk}",
    )(*operands)


def user_kernel(epoch, block_rows, me_ref, owner_ref, users, grad, gram, *outs):
    rank = users.shape[1]
    eye = (
        lax.broadcasted_iota(jnp.int32, (rank, rank), 0)
        == lax.broadcasted_iota(jnp.int32, (rank, rank), 1)
    )
    full = gram[...] * (GRAM / block_rows) + jnp.where(eye, RIDGE, 0.0)
    pull = jnp.dot(users[...], full, precision=lax.Precision.HIGHEST, preferred_element_type=F32)
    new = users[...] - LEARN * (grad[...] + pull)
    outs[0][...] = new
    if len(outs) > 1:
        outs[1][...] = owned_gram(new.astype(BF16), owner_ref[epoch + 1, 0], me_ref[0])


def user_call(epoch, block_rows, me, owner_list, users, grad, gram):
    rank = users.shape[1]
    out_shape = [jax.ShapeDtypeStruct(users.shape, F32)]
    if epoch + 1 < SUB:
        out_shape.append(jax.ShapeDtypeStruct((rank, rank), BF16))
    return pl.pallas_call(
        functools.partial(user_kernel, epoch, block_rows),
        out_shape=out_shape,
        in_specs=[SMEM, SMEM, VMEM, VMEM, VMEM],
        out_specs=[VMEM] * len(out_shape),
        compiler_params=params(24),
        cost_estimate=pl.CostEstimate(
            flops=users.shape[0] * rank * rank * 14, bytes_accessed=4 << 20, transcendentals=0
        ),
        name=f"users_{epoch}",
    )(me, owner_list, users, grad, gram)


def item_kernel(epoch, chunk, count, shard_rows, me_ref, gram, items, *refs):
    terms_a = refs[:count]
    terms_b = refs[count:2 * count]
    out, held, sem = refs[2 * count:]
    rows = out.shape[0]
    if epoch == 0:
        start = pl.multiple_of(me_ref[0] * shard_rows + chunk * rows, rows)
        copy = pltpu.make_async_copy(items.at[pl.ds(start, rows)], held, sem)
        copy.start()
        copy.wait()
        old = held[...]
        high = old.astype(BF16)
        low = (old - high.astype(F32)).astype(BF16)
        pull = jnp.dot(high, gram[...], preferred_element_type=F32)
        pull += jnp.dot(low, gram[...], preferred_element_type=F32)
    else:
        old = items[...].astype(F32)
        pull = jnp.dot(items[...], gram[...], preferred_element_type=F32)
    sums = []
    for terms in (terms_a, terms_b):
        total = terms[0][0].astype(F32)
        for term in terms[1:]:
            total += term[0].astype(F32)
        sums.append(total)
    grad = jnp.concatenate(sums, axis=0)
    out[...] = (old - LEARN * (grad + pull)).astype(BF16)


def item_call(epoch, chunk, shard_rows, me, gram, items, terms_a, terms_b):
    rank = gram.shape[1]
    rows = shard_rows // CHUNKS
    return pl.pallas_call(
        functools.partial(item_kernel, epoch, chunk, len(terms_a), shard_rows),
        out_shape=jax.ShapeDtypeStruct((rows, rank), BF16),
        in_specs=[SMEM, VMEM, ANY if epoch == 0 else VMEM] + [VMEM] * (2 * len(terms_a)),
        out_specs=VMEM,
        scratch_shapes=[pltpu.VMEM((rows if epoch == 0 else 8, rank), F32), pltpu.SemaphoreType.DMA],
        compiler_params=params(24),
        cost_estimate=pl.CostEstimate(
            flops=rows * rank * rank * 4, bytes_accessed=2 << 20, transcendentals=0
        ),
        name=f"items_{epoch}_{chunk}",
    )(me, gram, items, *terms_a, *terms_b)


def swapped(value, bit):
    length = lax.axis_size("grp")
    return lax.ppermute(value, "grp", [(i, i ^ bit) for i in range(length)])


def moved(value, bit):
    length, blocks = lax.axis_size("grp"), lax.axis_size("blk")
    pairs = [
        (b * length + i, (b + 1) % blocks * length + (i ^ bit))
        for b in range(blocks)
        for i in range(length)
    ]
    return lax.ppermute(value, ("blk", "grp"), pairs)


def summed_over(value):
    length = lax.axis_size("grp")
    bit = 1
    while bit < length:
        value = value + swapped(value, bit)
        bit *= 2
    return value


def scattered(send, keep, order):
    length = lax.axis_size("grp")
    names = [r for r in range(length) if not r & order[0]]
    terms = [keep]
    arrived = swapped(send, order[0])
    for bit in order[1:]:
        terms.append(arrived)
        current = terms[0].astype(F32)
        for term in terms[1:]:
            current = current + term.astype(F32)
        going = [p for p, r in enumerate(names) if r & bit]
        staying = [p for p, r in enumerate(names) if not r & bit]
        send = jnp.stack([current[p] for p in going]).astype(BF16)
        if len(staying) < len(names):
            terms = [jnp.stack([t[p] for p in staying]) if len(staying) > 1 else t for t in terms]
        names = [names[p] for p in staying]
        arrived = swapped(send, bit)
    terms.append(arrived)
    return terms


def gathered(shard):
    length = lax.axis_size("grp")
    half = shard.shape[0] // 2
    known = {0: [moved(shard, 0)]}
    bit = 1
    while bit < length:
        known[bit] = [moved(shard, bit)]
        bit *= 2

    def cut(r, lower):
        pieces = known[r]
        if len(pieces) == 1:
            return pieces[0][half:] if lower else pieces[0][:half]
        return pieces[1] if lower else pieces[0]

    for r in range(1, length):
        if r in known:
            continue
        low = r & -r
        high = 1 << (r.bit_length() - 1)
        known[r] = [swapped(cut(r ^ high, False), high), swapped(cut(r ^ low, True), low)]
    return [piece for r in range(length) for piece in known[r]]


def local(ratings, row_index, col_index, row_mask, counts, owner_list, user_factors, item_factors):
    members = lax.axis_size("grp")
    block_rows = item_factors.shape[0]
    shard_rows = block_rows // members
    me = lax.axis_index("grp").astype(jnp.int32).reshape(1)
    scalars = (me, row_index, col_index, counts, owner_list)
    bits = [1 << i for i in range(members.bit_length() - 1)]
    users = user_factors
    chunks = [[item_factors]] * CHUNKS
    own_gram = None
    for epoch in range(SUB):
        carried = None
        outs = []
        for c in range(CHUNKS):
            out = tile_call(
                epoch, c, members, scalars, ratings, row_mask, users, chunks[c], carried
            )
            carried = out[4:6]
            if epoch == 0 and c == 0:
                own_gram = out[6]
            outs.append(out)
        owner_gram = summed_over(own_gram)
        new_users = user_call(epoch, block_rows, me, owner_list, users, *carried)
        shards = []
        for c in range(CHUNKS):
            send_a, keep_a, send_b, keep_b = outs[c][:4]
            terms_a = scattered(send_a, keep_a, bits)
            terms_b = scattered(send_b, keep_b, bits[::-1])
            shards.append(
                item_call(
                    epoch, c, shard_rows, me, owner_gram, chunks[c][0], terms_a, terms_b
                )
            )
        users = new_users[0]
        if epoch + 1 < SUB:
            own_gram = new_users[1]
            chunks = [gathered(shard) for shard in shards]
        else:
            chunks = [moved(shard, 0) for shard in shards]
    return users, jnp.concatenate(chunks, axis=0).astype(F32)


def solution(mesh):
    in_specs = (
        P(None, "blk", "grp", None, None, None),
        P(None, "blk", "grp", None),
        P(None, "blk", "grp", None),
        P(None, "blk", "grp", None, None),
        P(None, "blk", "grp"),
        P(None, "blk"),
        P(("blk", "grp"), None),
        P("blk", None),
    )
    out_specs = (P(("blk", "grp"), None), P(("blk", "grp"), None))
    return jax.shard_map(local, mesh=mesh, in_specs=in_specs, out_specs=out_specs, check_vma=False)
```

```python
import functools

import jax
import jax.numpy as jnp
from jax import lax
from jax.experimental import pallas as pl
from jax.experimental.pallas import tpu as pltpu
from jax.sharding import PartitionSpec as P

SUB = 2
LEARN = 0.004
GRAM = 256.0
RIDGE = 1.0
CHUNKS = 2
F32 = jnp.float32
BF16 = jnp.bfloat16
BIG = float(jnp.finfo(jnp.bfloat16).max)

ANY = pl.BlockSpec(memory_space=pl.ANY)
HBM = pl.BlockSpec(memory_space=pltpu.HBM)
VMEM = pl.BlockSpec(memory_space=pltpu.VMEM)


def params(mib):
    return pltpu.CompilerParams(vmem_limit_bytes=mib * 1024 * 1024)


def cost(flops, bytes_accessed):
    return pl.CostEstimate(flops=flops, bytes_accessed=bytes_accessed, transcendentals=0)


def over_rows(a, b):
    return lax.dot_general(a, b, (((1,), (1,)), ((), ())), preferred_element_type=F32)


def over_columns(a, b):
    return lax.dot_general(a, b, (((0,), (0,)), ((), ())), preferred_element_type=F32)


def ridge(rank):
    down = lax.broadcasted_iota(jnp.int32, (rank, rank), 0)
    across = lax.broadcasted_iota(jnp.int32, (rank, rank), 1)
    return jnp.where(down == across, RIDGE, 0.0)


def owned(gram, rows, owner):
    full = gram * (GRAM / rows) + ridge(gram.shape[0])
    return jnp.where(owner == lax.axis_index("grp"), full, 0.0).astype(BF16)


def without(members, bit):
    return [r for r in range(members) if not r & bit]


def tile_kernel(epoch, chunk, members, shard_tiles, tile, pieces, first, *refs):
    row_hbm, col_hbm, count_hbm, owner_hbm, ratings, mask_hbm, users = refs[:7]
    sources = refs[7:7 + pieces]
    refs = refs[7 + pieces:]
    if not first:
        grad_in, gram_in = refs[:2]
        refs = refs[2:]
    elif epoch > 0:
        own_in = refs[0]
        refs = refs[1:]
    send_a, keep_a, send_b, keep_b, grad_user, gram_item = refs[:6]
    (row_ref, col_ref, count_ref, owner_ref, mask, users_f, user_bf, user_t, items, items_f, parts,
     held, errors, slots, slot_row, slot_place, sem_tile, sem_item, sem_small) = refs[6:]

    me = lax.axis_index("grp")
    chunk_tiles = shard_tiles // CHUNKS
    rows = chunk_tiles * tile
    half = rows // 2
    bits_tile = chunk_tiles.bit_length() - 1
    bits_shard = shard_tiles.bit_length() - 1

    small = [
        pltpu.make_async_copy(src, dst, sem_small.at[i])
        for i, (src, dst) in enumerate(
            [(row_hbm, row_ref), (col_hbm, col_ref), (count_hbm, count_ref), (owner_hbm, owner_ref),
             (mask_hbm.at[epoch, 0, 0], mask), (users, users_f)]
        )
    ]
    for copy in small:
        copy.start()
    if not first:
        prev = pltpu.make_async_copy(grad_in, grad_user, sem_small.at[6])
        prev.start()
    copies = []
    if epoch == 0:
        for r in range(members):
            start = pl.multiple_of((me ^ r) * (shard_tiles * tile) + chunk * rows, rows)
            copies.append(
                pltpu.make_async_copy(
                    sources[0].at[pl.ds(start, rows)], items_f.at[pl.ds(r * rows, rows)], sem_item.at[r]
                )
            )
    else:
        at = 0
        for i, source in enumerate(sources):
            width = source.shape[1]
            copies.append(
                pltpu.make_async_copy(source, items.at[:, pl.ds(at, width)], sem_item.at[i])
            )
            at += width
    for copy in copies:
        copy.start()
    for copy in small[:4]:
        copy.wait()

    count = count_ref[epoch, 0, 0]

    def pick(t, found):
        col = col_ref[epoch, 0, 0, t]
        slots[found] = t
        slot_row[found] = row_ref[epoch, 0, 0, t]
        slot_place[found] = ((col >> bits_shard) ^ me) * chunk_tiles + (col & (chunk_tiles - 1))
        here = ((col >> bits_tile) & (CHUNKS - 1)) == chunk
        return found + jnp.where(here & (t < count), 1, 0).astype(jnp.int32)

    total = lax.fori_loop(0, col_ref.shape[3], pick, jnp.int32(0), unroll=8)

    def fetch(i):
        return pltpu.make_async_copy(ratings.at[epoch, 0, 0, slots[i]], held.at[i], sem_tile.at[i])

    def begin(i, _):
        fetch(i).start()
        return 0

    lax.fori_loop(0, total, begin, 0)

    parts[...] = jnp.zeros_like(parts)
    if first:
        grad_user[...] = jnp.zeros_like(grad_user)
    for copy in small[4:]:
        copy.wait()

    def user_tile(j, _):
        spot = pl.ds(pl.multiple_of(j * tile, tile), tile)
        part = users_f[spot]
        user_bf[spot] = part.astype(BF16)
        user_t[:, spot] = part.T
        return 0

    lax.fori_loop(0, users_f.shape[0] // tile, user_tile, 0, unroll=2)

    def item_tile(j, _):
        spot = pl.ds(pl.multiple_of(j * tile, tile), tile)
        items[:, spot] = items_f[spot].T.astype(BF16)
        return 0

    for i, copy in enumerate(copies):
        copy.wait()
        if epoch == 0:
            lax.fori_loop(i * chunk_tiles, (i + 1) * chunk_tiles, item_tile, 0, unroll=2)
    if not first:
        prev.wait()

    def spots(i):
        row = pl.multiple_of(slot_row[i] * tile, tile)
        place = pl.multiple_of(slot_place[i] * tile, tile)
        return pl.ds(row, tile), pl.ds(place, tile)

    def front(j):
        buffer = 2 * (j & 1)
        for k in range(2):
            i = 2 * j + k

            @pl.when(i < total)
            def _():
                fetch(i).wait()

        for k in range(2):
            i = jnp.minimum(2 * j + k, total - 1)
            row, place = spots(i)
            predicted = jnp.dot(user_bf[row], items[:, place], preferred_element_type=F32)
            error = (predicted - held[i].astype(F32)).astype(BF16)
            errors[buffer + k] = jnp.clip(error, -BIG, BIG)

    def back(j):
        buffer = 2 * (j & 1)
        adds = []
        for k in range(2):
            valid = 2 * j + k < total
            i = jnp.minimum(2 * j + k, total - 1)
            row, place = spots(i)
            weight = mask[pl.ds(slots[i], 1), :].astype(F32)
            weight = jnp.where(valid, weight, 0.0)
            error = errors[buffer + k]
            user_add = over_rows(items[:, place], error)
            item_add = jnp.dot(
                (user_t[:, row] * weight).astype(BF16), error, preferred_element_type=F32
            )
            adds.append((row, place, jnp.where(weight > 0.5, user_add, 0.0), item_add))
        for row, place, user_add, item_add in adds:
            grad_user[:, row] += user_add
            parts[:, place] += item_add

    pairs = (total + 1) // 2

    @pl.when(total > 0)
    def _():
        front(0)

    def step(j, _):
        front(jnp.minimum(j + 1, pairs))
        back(j)
        return 0

    lax.fori_loop(0, pairs, step, 0)

    for bit, send, keep, start, width in (
        (1, send_a, keep_a, 0, half), (members // 2, send_b, keep_b, half, rows - half)
    ):
        for k, r in enumerate(without(members, bit)):
            keep[:, k * width:(k + 1) * width] = parts[:, pl.ds(r * rows + start, width)].astype(BF16)
            r = r | bit
            send[:, k * width:(k + 1) * width] = parts[:, pl.ds(r * rows + start, width)].astype(BF16)
    gram = over_rows(items[...], items[...])
    if first:
        gram_item[...] = gram
        if epoch == 0:
            own = owned(
                over_columns(user_bf[...], user_bf[...]), users_f.shape[0], owner_ref[epoch, 0]
            )
        else:
            own = own_in[...]
        send_a[:, members // 2 * half:] = own
    else:
        gram_item[...] = gram_in[...] + gram


def tile_call(epoch, chunk, members, scalars, ratings, row_mask, users, sources, carried, own):
    tile = ratings.shape[-1]
    slots = ratings.shape[3]
    user_rows, rank = users.shape
    first = chunk == 0
    if epoch == 0:
        block_rows = sources[0].shape[0]
    else:
        block_rows = sum(s.shape[1] for s in sources) * CHUNKS
    shard_tiles = block_rows // members // tile
    rows = shard_tiles // CHUNKS * tile
    half = rows // 2
    sd = jax.ShapeDtypeStruct
    wide_a, wide_b = members // 2 * half, members // 2 * (rows - half)
    extra = rank if first else 0
    out_shape = [
        sd((rank, wide_a + extra), BF16), sd((rank, wide_a), BF16),
        sd((rank, wide_b), BF16), sd((rank, wide_b), BF16),
        sd((rank, user_rows), F32), sd((rank, rank), F32),
    ]
    in_specs = [HBM] * 7 + [HBM if epoch == 0 else ANY] * len(sources)
    operands = [*scalars, ratings, row_mask, users, *sources]
    if not first:
        in_specs += [ANY, VMEM]
        operands += list(carried)
    elif epoch > 0:
        in_specs += [VMEM]
        operands += [own]
    return pl.pallas_call(
        functools.partial(
            tile_kernel, epoch, chunk, members, shard_tiles, tile, len(sources), first
        ),
        out_shape=out_shape,
        in_specs=in_specs,
        out_specs=[VMEM] * len(out_shape),
        scratch_shapes=[
            *[pltpu.SMEM(s.shape, jnp.int32) for s in scalars],
            pltpu.VMEM((slots, tile), jnp.int32),
            pltpu.VMEM((user_rows, rank), F32),
            pltpu.VMEM((user_rows, rank), BF16),
            pltpu.VMEM((rank, user_rows), F32),
            pltpu.VMEM((rank, members * rows), BF16),
            pltpu.VMEM((members * rows if epoch == 0 else 8, rank), F32),
            pltpu.VMEM((rank, members * rows), F32),
            pltpu.VMEM((slots, tile, tile), BF16),
            pltpu.VMEM((4, tile, tile), BF16),
            *[pltpu.SMEM((slots + 1,), jnp.int32)] * 3,
            pltpu.SemaphoreType.DMA((slots,)),
            pltpu.SemaphoreType.DMA((max(members, len(sources)),)),
            pltpu.SemaphoreType.DMA((7,)),
        ],
        compiler_params=params(44),
        cost_estimate=cost(1 << 20, 1 << 16),
        name=f"tiles_{epoch}_{chunk}",
    )(*operands)


def user_kernel(epoch, block_rows, owner_ref, users, grad, gram, *outs):
    full = gram[...] * (GRAM / block_rows) + ridge(users.shape[1])
    pull = jnp.dot(users[...], full, precision=lax.Precision.HIGHEST, preferred_element_type=F32)
    new = users[...] - LEARN * (grad[...].T + pull)
    outs[0][...] = new
    if len(outs) > 1:
        new = new.astype(BF16)
        outs[1][...] = owned(over_columns(new, new), users.shape[0], owner_ref[epoch + 1, 0])


def user_call(epoch, block_rows, owner_list, users, grad, gram):
    rank = users.shape[1]
    out_shape = [jax.ShapeDtypeStruct(users.shape, F32)]
    if epoch + 1 < SUB:
        out_shape.append(jax.ShapeDtypeStruct((rank, rank), BF16))
    return pl.pallas_call(
        functools.partial(user_kernel, epoch, block_rows),
        out_shape=out_shape,
        in_specs=[pl.BlockSpec(memory_space=pltpu.SMEM), VMEM, VMEM, VMEM],
        out_specs=[VMEM] * len(out_shape),
        compiler_params=params(44),
        cost_estimate=cost(1 << 20, 1 << 16),
        name=f"users_{epoch}",
    )(owner_list, users, grad, gram)


def summed(refs, names, r, width):
    total = None
    for ref, order in zip(refs, names):
        k = order.index(r)
        term = ref[:, k * width:(k + 1) * width].astype(F32)
        total = term if total is None else total + term
    return total


def mid_kernel(paths, grams, *refs):
    at = 0
    outs = refs[sum(len(names) for names, _, _ in paths) + grams:]
    gram_refs = refs[len(refs) - len(paths) - grams:len(refs) - len(paths)]
    for (names, going, width), out in zip(paths, outs):
        terms = refs[at:at + len(names)]
        at += len(names)
        for k, r in enumerate(going):
            out[:, k * width:(k + 1) * width] = summed(terms, names, r, width).astype(BF16)
    if grams:
        rank = outs[0].shape[0]
        total = gram_refs[0][:, gram_refs[0].shape[1] - rank:].astype(F32)
        for ref in gram_refs[1:]:
            total += ref[:, ref.shape[1] - rank:].astype(F32)
        outs[0][:, outs[0].shape[1] - rank:] = total.astype(BF16)


def mid_call(epoch, chunk, step, paths, grams):
    rank = paths[0][0][0][0].shape[0]
    specs, operands, out_shape = [], [], []
    for terms, going, width in paths:
        specs.append(([names for _, names in terms], going, width))
        operands += [array for array, _ in terms]
        extra = rank if grams and not out_shape else 0
        out_shape.append(jax.ShapeDtypeStruct((rank, len(going) * width + extra), BF16))
    operands += grams
    return pl.pallas_call(
        functools.partial(mid_kernel, specs, len(grams)),
        out_shape=out_shape,
        in_specs=[VMEM] * len(operands),
        out_specs=[VMEM] * len(out_shape),
        compiler_params=params(44),
        cost_estimate=cost(1 << 16, 1 << 16),
        name=f"mid_{epoch}_{chunk}_{step}",
    )(*operands)


def item_kernel(epoch, chunk, count, shard_rows, width, grams, items, *refs):
    terms_a, terms_b = refs[:count], refs[count:2 * count]
    gram_refs = refs[2 * count:2 * count + grams]
    refs = refs[2 * count + grams:]
    out = refs[0]
    rank = gram_refs[0].shape[0]
    gram = gram_refs[0][:, gram_refs[0].shape[1] - rank:]
    for ref in gram_refs[1:]:
        gram = (gram.astype(F32) + ref[:, ref.shape[1] - rank:].astype(F32)).astype(BF16)
    if grams > 1:
        refs[1][...] = gram
    rows = shard_rows // CHUNKS
    zero = [[0]] * count
    grad = jnp.concatenate(
        [summed(terms_a, zero, 0, width), summed(terms_b, zero, 0, rows - width)], axis=1
    )
    if epoch == 0:
        held, sem = refs[-2:]
        start = pl.multiple_of(lax.axis_index("grp") * shard_rows + chunk * rows, rows)
        copy = pltpu.make_async_copy(items.at[pl.ds(start, rows)], held, sem)
        copy.start()
        copy.wait()
        old = held[...]
        high = old.astype(BF16)
        low = (old - high.astype(F32)).astype(BF16)
        pull = jnp.dot(high, gram, preferred_element_type=F32)
        pull += jnp.dot(low, gram, preferred_element_type=F32)
        out[...] = (old - LEARN * (grad.T + pull)).T.astype(BF16)
    else:
        pull = over_columns(gram, items[...])
        out[...] = (items[...].astype(F32) - LEARN * (grad + pull)).T.astype(BF16)


def item_call(epoch, chunk, shard_rows, items, terms_a, terms_b, grams):
    rank = grams[0].shape[0]
    rows = shard_rows // CHUNKS
    last = epoch + 1 == SUB
    out_shape = [jax.ShapeDtypeStruct((rows, rank) if last else (rank, rows), BF16)]
    if len(grams) > 1:
        out_shape.append(jax.ShapeDtypeStruct((rank, rank), BF16))
    scratch = [pltpu.VMEM((rows, rank), F32), pltpu.SemaphoreType.DMA] if epoch == 0 else []
    out = pl.pallas_call(
        functools.partial(
            item_kernel, epoch, chunk, len(terms_a), shard_rows, rows // 2, len(grams)
        ),
        out_shape=out_shape,
        in_specs=[HBM if epoch == 0 else VMEM] + [VMEM] * (2 * len(terms_a) + len(grams)),
        out_specs=[VMEM] * len(out_shape),
        scratch_shapes=scratch,
        compiler_params=params(44),
        cost_estimate=cost(1 << 16, 1 << 16),
        name=f"items_{epoch}_{chunk}",
    )(items, *terms_a, *terms_b, *grams)
    return out[0], out[-1]


def swapped(value, bit):
    length = lax.axis_size("grp")
    return lax.ppermute(value, "grp", [(i, i ^ bit) for i in range(length)])


def moved(value, bit):
    length, blocks = lax.axis_size("grp"), lax.axis_size("blk")
    pairs = [
        (b * length + i, (b + 1) % blocks * length + (i ^ bit))
        for b in range(blocks)
        for i in range(length)
    ]
    return lax.ppermute(value, ("blk", "grp"), pairs)


def scattered(epoch, chunk, out, members, width_a, width_b):
    send_a, keep_a, send_b, keep_b = out[:4]
    bits = [1 << i for i in range(members.bit_length() - 1)]
    orders = (bits, bits[::-1])
    widths = (width_a, width_b)
    sends = [send_a, send_b]
    names = [without(members, order[0]) for order in orders]
    terms = [[(keep_a, names[0])], [(keep_b, names[1])]]
    grams = [send_a] if chunk == 0 else []
    for step in range(len(bits)):
        for p in range(2):
            arrived = swapped(sends[p], orders[p][step])
            terms[p].append((arrived, names[p]))
            if p == 0 and grams:
                grams.append(arrived)
        if step + 1 == len(bits):
            break
        paths = []
        for p in range(2):
            bit = orders[p][step + 1]
            paths.append((terms[p], [r for r in names[p] if r & bit], widths[p]))
            names[p] = [r for r in names[p] if not r & bit]
        sends = mid_call(epoch, chunk, step, paths, grams)
    return [a for a, _ in terms[0]], [a for a, _ in terms[1]], grams


def gathered(shard):
    length = lax.axis_size("grp")
    half = shard.shape[1] // 2
    known = {0: [moved(shard, 0)]}
    bit = 1
    while bit < length:
        known[bit] = [moved(shard, bit)]
        bit *= 2

    def cut(r, lower):
        pieces = known[r]
        if len(pieces) == 1:
            return pieces[0][:, half:] if lower else pieces[0][:, :half]
        return pieces[1] if lower else pieces[0]

    for r in range(1, length):
        if r in known:
            continue
        low = r & -r
        high = 1 << (r.bit_length() - 1)
        known[r] = [swapped(cut(r ^ high, False), high), swapped(cut(r ^ low, True), low)]
    return [piece for r in range(length) for piece in known[r]]


def local(ratings, row_index, col_index, row_mask, counts, owner_list, user_factors, item_factors):
    members = lax.axis_size("grp")
    block_rows = item_factors.shape[0]
    shard_rows = block_rows // members
    rows = shard_rows // CHUNKS
    scalars = (row_index, col_index, counts, owner_list)
    users = user_factors
    chunks = [[item_factors]] * CHUNKS
    own_gram = None
    for epoch in range(SUB):
        carried = None
        outs = []
        for c in range(CHUNKS):
            out = tile_call(
                epoch, c, members, scalars, ratings, row_mask, users, chunks[c], carried, own_gram
            )
            carried = out[4:6]
            outs.append(out)
        new_users = user_call(epoch, block_rows, owner_list, users, *carried)
        shards = []
        grams = None
        for c in range(CHUNKS):
            terms_a, terms_b, found = scattered(
                epoch, c, outs[c], members, rows // 2, rows - rows // 2
            )
            shard, gram = item_call(
                epoch, c, shard_rows, chunks[c][0], terms_a, terms_b, found or grams
            )
            if found:
                grams = [gram]
            shards.append(shard)
        users = new_users[0]
        if epoch + 1 < SUB:
            own_gram = new_users[1]
            chunks = [gathered(shard) for shard in shards]
        else:
            chunks = [moved(shard, 0) for shard in shards]
    return users, jnp.concatenate(chunks, axis=0).astype(F32)


def solution(mesh):
    in_specs = (
        P(None, "blk", "grp", None, None, None),
        P(None, "blk", "grp", None),
        P(None, "blk", "grp", None),
        P(None, "blk", "grp", None, None),
        P(None, "blk", "grp"),
        P(None, "blk"),
        P(("blk", "grp"), None),
        P("blk", None),
    )
    out_specs = (P(("blk", "grp"), None), P(("blk", "grp"), None))
    return jax.shard_map(local, mesh=mesh, in_specs=in_specs, out_specs=out_specs, check_vma=False)
```

```python
import functools

import jax
import jax.numpy as jnp
from jax import lax
from jax.experimental import pallas as pl
from jax.experimental.pallas import tpu as pltpu
from jax.sharding import PartitionSpec as P

SUB = 2
LEARN = 0.004
GRAM = 256.0
RIDGE = 1.0
CHUNKS = 2
START_MIB = 54
F32 = jnp.float32
BF16 = jnp.bfloat16
BIG = float(jnp.finfo(jnp.bfloat16).max)

ANY = pl.BlockSpec(memory_space=pl.ANY)
HBM = pl.BlockSpec(memory_space=pltpu.HBM)
VMEM = pl.BlockSpec(memory_space=pltpu.VMEM)


def params(mib):
    return pltpu.CompilerParams(vmem_limit_bytes=mib * 1024 * 1024)


def cost(flops, bytes_accessed):
    return pl.CostEstimate(flops=flops, bytes_accessed=bytes_accessed, transcendentals=0)


def over_rows(a, b):
    return lax.dot_general(a, b, (((1,), (1,)), ((), ())), preferred_element_type=F32)


def over_columns(a, b):
    return lax.dot_general(a, b, (((0,), (0,)), ((), ())), preferred_element_type=F32)


def ridge(rank):
    down = lax.broadcasted_iota(jnp.int32, (rank, rank), 0)
    across = lax.broadcasted_iota(jnp.int32, (rank, rank), 1)
    return jnp.where(down == across, RIDGE, 0.0)


def owned(gram, rows, owner):
    full = gram * (GRAM / rows) + ridge(gram.shape[0])
    return jnp.where(owner == lax.axis_index("grp"), full, 0.0).astype(BF16)


def without(members, bit):
    return [r for r in range(members) if not r & bit]


def tile_kernel(epoch, chunk, members, shard_tiles, tile, pieces, *refs):
    start_up = epoch == 0 and chunk == 0
    first = chunk == 0
    refs = list(refs)

    def take(n):
        out, refs[:n] = refs[:n], []
        return out

    row_hbm, col_hbm, count_hbm, owner_hbm, ratings, mask_hbm = take(6)
    users = take(1) if start_up else take(2)
    sources = take(pieces)
    grad_in = take(0 if first else 1)
    own_in = take(1 if first and epoch > 0 else 0)
    send_a, keep_a, send_b, keep_b, grad_user = take(5)
    if epoch == 0:
        items, old = take(2)
    if start_up:
        user_bf, user_t = take(2)
    else:
        user_bf, user_t = users
    (row_ref, col_ref, count_ref, owner_ref, mask, parts, held, error_0, error_1,
     slots, slot_row, slot_place, sem_tile, sem_item, sem_small) = take(15)
    if epoch == 0:
        items_f, = take(1)
    else:
        items, = take(1)
    if start_up:
        users_f, = take(1)
    errors = (error_0, error_1)

    me = lax.axis_index("grp")
    chunk_tiles = shard_tiles // CHUNKS
    rows = chunk_tiles * tile
    half = rows // 2
    bits_tile = chunk_tiles.bit_length() - 1
    bits_shard = shard_tiles.bit_length() - 1

    pairs = [(row_hbm, row_ref), (col_hbm, col_ref), (count_hbm, count_ref),
             (owner_hbm, owner_ref), (mask_hbm.at[epoch, 0, 0], mask)]
    if not first:
        pairs.append((grad_in[0], grad_user))
    if start_up:
        pairs.append((users[0], users_f))
    small = [
        pltpu.make_async_copy(src, dst, sem_small.at[i]) for i, (src, dst) in enumerate(pairs)
    ]
    for copy in small:
        copy.start()
    copies = []
    if epoch == 0:
        for r in range(members):
            start = pl.multiple_of((me ^ r) * (shard_tiles * tile) + chunk * rows, rows)
            copies.append(
                pltpu.make_async_copy(
                    sources[0].at[pl.ds(start, rows)], items_f.at[pl.ds(r * rows, rows)], sem_item.at[r]
                )
            )
    else:
        at = 0
        for i, source in enumerate(sources):
            width = source.shape[1]
            copies.append(
                pltpu.make_async_copy(source, items.at[:, pl.ds(at, width)], sem_item.at[i])
            )
            at += width
    for copy in copies:
        copy.start()
    for copy in small[:4]:
        copy.wait()

    count = count_ref[epoch, 0, 0]

    def pick(t, found):
        col = col_ref[epoch, 0, 0, t]
        slots[found] = t
        slot_row[found] = row_ref[epoch, 0, 0, t]
        slot_place[found] = ((col >> bits_shard) ^ me) * chunk_tiles + (col & (chunk_tiles - 1))
        here = ((col >> bits_tile) & (CHUNKS - 1)) == chunk
        return found + jnp.where(here & (t < count), 1, 0).astype(jnp.int32)

    total = lax.fori_loop(0, col_ref.shape[3], pick, jnp.int32(0), unroll=8)

    def fetch(i):
        return pltpu.make_async_copy(ratings.at[epoch, 0, 0, slots[i]], held.at[i], sem_tile.at[i])

    def begin(i, _):
        fetch(i).start()
        return 0

    lax.fori_loop(0, total, begin, 0)

    parts[...] = jnp.zeros_like(parts)
    if first:
        grad_user[...] = jnp.zeros_like(grad_user)
    for copy in small[4:]:
        copy.wait()

    def user_tile(j, _):
        spot = pl.ds(pl.multiple_of(j * tile, tile), tile)
        part = users_f[spot]
        user_bf[spot] = part.astype(BF16)
        user_t[:, spot] = part.T.astype(BF16)
        return 0

    if start_up:
        lax.fori_loop(0, users_f.shape[0] // tile, user_tile, 0, unroll=2)

    def item_tile(own, j, _):
        spot = pl.ds(pl.multiple_of(j * tile, tile), tile)
        turned = items_f[spot].T
        items[:, spot] = turned.astype(BF16)
        if own:
            old[:, spot] = turned
        return 0

    for r, copy in enumerate(copies):
        copy.wait()
        if epoch == 0:
            lax.fori_loop(
                r * chunk_tiles, (r + 1) * chunk_tiles, functools.partial(item_tile, r == 0), 0,
                unroll=2,
            )

    def spots(i):
        row = pl.multiple_of(slot_row[i] * tile, tile)
        place = pl.multiple_of(slot_place[i] * tile, tile)
        return pl.ds(row, tile), pl.ds(place, tile)

    def ready(j):
        for k in range(2):
            i = 2 * j + k

            @pl.when(i < total)
            def _():
                fetch(i).wait()

    def front(j):
        for k in range(2):
            i = jnp.minimum(2 * j + k, total - 1)
            row, place = spots(i)
            predicted = jnp.dot(user_bf[row], items[:, place], preferred_element_type=F32)
            error = (predicted - held[i].astype(F32)).astype(BF16)
            errors[k][j & 1] = jnp.clip(error, -BIG, BIG)

    def back(j):
        adds = []
        for k in range(2):
            valid = 2 * j + k < total
            i = jnp.minimum(2 * j + k, total - 1)
            row, place = spots(i)
            weight = mask[pl.ds(slots[i], 1), :].astype(F32)
            weight = jnp.where(valid, weight, 0.0)
            error = errors[k][j & 1]
            user_add = over_rows(items[:, place], error)
            item_add = jnp.dot(
                user_t[:, row] * weight.astype(BF16), error, preferred_element_type=F32
            )
            adds.append((row, place, jnp.where(weight > 0.5, user_add, 0.0), item_add))
        return adds

    def add(adds):
        for row, place, user_add, item_add in adds:
            grad_user[:, row] += user_add
            parts[:, place] += item_add

    twos = (total + 1) // 2

    @pl.when(total > 0)
    def _():
        ready(0)
        front(0)

    def step(j, _):
        ready(j + 1)
        adds = back(j)
        front(j + 1)
        add(adds)
        return 0

    lax.fori_loop(0, twos, step, 0)

    for bit, send, keep, start, width in (
        (1, send_a, keep_a, 0, half), (members // 2, send_b, keep_b, half, rows - half)
    ):
        for k, r in enumerate(without(members, bit)):
            keep[:, k * width:(k + 1) * width] = parts[:, pl.ds(r * rows + start, width)].astype(BF16)
            r = r | bit
            send[:, k * width:(k + 1) * width] = parts[:, pl.ds(r * rows + start, width)].astype(BF16)
    if start_up:
        own = jnp.dot(user_t[...], user_bf[...], preferred_element_type=F32)
        own = owned(own, users_f.shape[0], owner_ref[epoch, 0])
    elif first:
        own = own_in[0][...]
    if first:
        send_a[:, members // 2 * half:] = own


def tile_call(epoch, chunk, members, scalars, ratings, row_mask, users, sources, carried, own):
    tile = ratings.shape[-1]
    slots = ratings.shape[3]
    start_up = epoch == 0 and chunk == 0
    first = chunk == 0
    user_rows, rank = users[0].shape
    if epoch == 0:
        block_rows = sources[0].shape[0]
    else:
        block_rows = sum(s.shape[1] for s in sources) * CHUNKS
    shard_tiles = block_rows // members // tile
    rows = shard_tiles // CHUNKS * tile
    half = rows // 2
    sd = jax.ShapeDtypeStruct
    wide_a, wide_b = members // 2 * half, members // 2 * (rows - half)
    extra = rank if first else 0
    out_shape = [
        sd((rank, wide_a + extra), BF16), sd((rank, wide_a), BF16),
        sd((rank, wide_b), BF16), sd((rank, wide_b), BF16), sd((rank, user_rows), F32),
    ]
    if epoch == 0:
        out_shape += [sd((rank, members * rows), BF16), sd((rank, rows), F32)]
    if start_up:
        out_shape += [sd((user_rows, rank), BF16), sd((rank, user_rows), BF16)]
    in_specs = [HBM] * 6 + ([HBM] if start_up else [VMEM] * 2)
    in_specs += [HBM if epoch == 0 else ANY] * len(sources)
    operands = [*scalars, ratings, row_mask, *users, *sources]
    if not first:
        in_specs += [ANY]
        operands += [carried]
    elif epoch > 0:
        in_specs += [VMEM]
        operands += [own]
    scratch = [
        *[pltpu.SMEM(s.shape, jnp.int32) for s in scalars],
        pltpu.VMEM((slots, tile), jnp.int32),
        pltpu.VMEM((rank, members * rows), F32),
        pltpu.VMEM((slots, tile, tile), BF16),
        *[pltpu.VMEM((2, tile, tile), BF16)] * 2,
        *[pltpu.SMEM((slots + 1,), jnp.int32)] * 3,
        pltpu.SemaphoreType.DMA((slots,)),
        pltpu.SemaphoreType.DMA((max(members, len(sources)),)),
        pltpu.SemaphoreType.DMA((7,)),
    ]
    if epoch == 0:
        scratch.append(pltpu.VMEM((members * rows, rank), F32))
    else:
        scratch.append(pltpu.VMEM((rank, members * rows), BF16))
    if start_up:
        scratch.append(pltpu.VMEM((user_rows, rank), F32))
    return pl.pallas_call(
        functools.partial(tile_kernel, epoch, chunk, members, shard_tiles, tile, len(sources)),
        out_shape=out_shape,
        in_specs=in_specs,
        out_specs=[VMEM] * len(out_shape),
        scratch_shapes=scratch,
        compiler_params=params(START_MIB if start_up else 40),
        cost_estimate=cost(1 << 20, 1 << 16),
        name=f"tiles_{epoch}_{chunk}",
    )(*operands)


def user_kernel(epoch, block_rows, owner_ref, users, grad, *refs):
    outs = 4 if epoch + 1 < SUB else 1
    pieces, outs = refs[:-outs], refs[-outs:]
    gram = over_rows(pieces[0][...], pieces[0][...])
    for piece in pieces[1:]:
        gram += over_rows(piece[...], piece[...])
    full = gram * (GRAM / block_rows) + ridge(users.shape[1])
    pull = jnp.dot(users[...], full, precision=lax.Precision.HIGHEST, preferred_element_type=F32)
    new = users[...] - LEARN * (grad[...].T + pull)
    outs[0][...] = new
    if len(outs) > 1:
        plain = new.astype(BF16)
        turned = new.T.astype(BF16)
        outs[1][...] = plain
        outs[2][...] = turned
        own = jnp.dot(turned, plain, preferred_element_type=F32)
        outs[3][...] = owned(own, users.shape[0], owner_ref[epoch + 1, 0])


def user_call(epoch, block_rows, owner_list, users, grad, pieces):
    rows, rank = users.shape
    sd = jax.ShapeDtypeStruct
    out_shape = [sd(users.shape, F32)]
    if epoch + 1 < SUB:
        out_shape += [sd((rows, rank), BF16), sd((rank, rows), BF16), sd((rank, rank), BF16)]
    return pl.pallas_call(
        functools.partial(user_kernel, epoch, block_rows),
        out_shape=out_shape,
        in_specs=[pl.BlockSpec(memory_space=pltpu.SMEM)] + [VMEM] * (2 + len(pieces)),
        out_specs=[VMEM] * len(out_shape),
        compiler_params=params(40),
        cost_estimate=cost(1 << 20, 1 << 16),
        name=f"users_{epoch}",
    )(owner_list, users, grad, *pieces)


def summed(refs, names, r, width):
    total = None
    for ref, order in zip(refs, names):
        k = order.index(r)
        term = ref[:, k * width:(k + 1) * width].astype(F32)
        total = term if total is None else total + term
    return total


def mid_kernel(paths, grams, *refs):
    at = 0
    outs = refs[sum(len(names) for names, _, _ in paths) + grams:]
    gram_refs = refs[len(refs) - len(paths) - grams:len(refs) - len(paths)]
    for (names, going, width), out in zip(paths, outs):
        terms = refs[at:at + len(names)]
        at += len(names)
        for k, r in enumerate(going):
            out[:, k * width:(k + 1) * width] = summed(terms, names, r, width).astype(BF16)
    if grams:
        rank = outs[0].shape[0]
        total = gram_refs[0][:, gram_refs[0].shape[1] - rank:].astype(F32)
        for ref in gram_refs[1:]:
            total += ref[:, ref.shape[1] - rank:].astype(F32)
        outs[0][:, outs[0].shape[1] - rank:] = total.astype(BF16)


def mid_call(epoch, chunk, step, paths, grams):
    rank = paths[0][0][0][0].shape[0]
    specs, operands, out_shape = [], [], []
    for terms, going, width in paths:
        specs.append(([names for _, names in terms], going, width))
        operands += [array for array, _ in terms]
        extra = rank if grams and not out_shape else 0
        out_shape.append(jax.ShapeDtypeStruct((rank, len(going) * width + extra), BF16))
    operands += grams
    return pl.pallas_call(
        functools.partial(mid_kernel, specs, len(grams)),
        out_shape=out_shape,
        in_specs=[VMEM] * len(operands),
        out_specs=[VMEM] * len(out_shape),
        compiler_params=params(40),
        cost_estimate=cost(1 << 16, 1 << 16),
        name=f"mid_{epoch}_{chunk}_{step}",
    )(*operands)


def item_kernel(epoch, count, rows, width, grams, items, *refs):
    terms_a, terms_b = refs[:count], refs[count:2 * count]
    gram_refs = refs[2 * count:2 * count + grams]
    refs = refs[2 * count + grams:]
    out = refs[0]
    rank = gram_refs[0].shape[0]
    gram = gram_refs[0][:, gram_refs[0].shape[1] - rank:]
    for ref in gram_refs[1:]:
        gram = (gram.astype(F32) + ref[:, ref.shape[1] - rank:].astype(F32)).astype(BF16)
    if grams > 1:
        refs[1][...] = gram
    zero = [[0]] * count
    grad = jnp.concatenate(
        [summed(terms_a, zero, 0, width), summed(terms_b, zero, 0, rows - width)], axis=1
    )
    if epoch == 0:
        high = items[...].astype(BF16)
        low = (items[...] - high.astype(F32)).astype(BF16)
        pull = over_columns(gram, high) + over_columns(gram, low)
    else:
        pull = over_columns(gram, items[...])
    new = items[...].astype(F32) - LEARN * (grad + pull)
    out[...] = (new if epoch + 1 < SUB else new.T).astype(BF16)


def item_call(epoch, chunk, shard_rows, items, terms_a, terms_b, grams):
    rank = grams[0].shape[0]
    rows = shard_rows // CHUNKS
    last = epoch + 1 == SUB
    out_shape = [jax.ShapeDtypeStruct((rows, rank) if last else (rank, rows), BF16)]
    if len(grams) > 1:
        out_shape.append(jax.ShapeDtypeStruct((rank, rank), BF16))
    out = pl.pallas_call(
        functools.partial(
            item_kernel, epoch, len(terms_a), rows, rows // 2, len(grams)
        ),
        out_shape=out_shape,
        in_specs=[VMEM] * (1 + 2 * len(terms_a) + len(grams)),
        out_specs=[VMEM] * len(out_shape),
        compiler_params=params(40),
        cost_estimate=cost(1 << 16, 1 << 16),
        name=f"items_{epoch}_{chunk}",
    )(items, *terms_a, *terms_b, *grams)
    return out[0], out[-1]


def swapped(value, bit):
    length = lax.axis_size("grp")
    return lax.ppermute(value, "grp", [(i, i ^ bit) for i in range(length)])


def moved(value, bit):
    length, blocks = lax.axis_size("grp"), lax.axis_size("blk")
    pairs = [
        (b * length + i, (b + 1) % blocks * length + (i ^ bit))
        for b in range(blocks)
        for i in range(length)
    ]
    return lax.ppermute(value, ("blk", "grp"), pairs)


def scattered(epoch, chunk, out, members, width_a, width_b, after):
    send_a, keep_a, send_b, keep_b = out[:4]
    bits = [1 << i for i in range(members.bit_length() - 1)]
    orders = (bits, bits[::-1])
    widths = (width_a, width_b)
    sends = [send_a, send_b]
    names = [without(members, order[0]) for order in orders]
    terms = [[(keep_a, names[0])], [(keep_b, names[1])]]
    grams = [send_a] if chunk == 0 else []
    for step in range(len(bits)):
        for p in range(2):
            arrived = swapped(sends[p], orders[p][step])
            if step == 0:
                arrived = tied(arrived, after)
            terms[p].append((arrived, names[p]))
            if p == 0 and grams:
                grams.append(arrived)
        if step + 1 == len(bits):
            break
        paths = []
        for p in range(2):
            bit = orders[p][step + 1]
            paths.append((terms[p], [r for r in names[p] if r & bit], widths[p]))
            names[p] = [r for r in names[p] if not r & bit]
        sends = mid_call(epoch, chunk, step, paths, grams)
    return [a for a, _ in terms[0]], [a for a, _ in terms[1]], grams


def tied(value, *others):
    return lax.optimization_barrier((value, *others))[0]


def gather_start(shard):
    known = {0: moved(shard, 0)}
    bit = 1
    while bit < lax.axis_size("grp"):
        known[bit] = moved(shard, bit)
        bit *= 2
    return known


def gather_finish(known, after):
    length = lax.axis_size("grp")
    known = {r: [tied(piece, *after)] for r, piece in known.items()}

    def cut(r, lower):
        pieces = known[r]
        if len(pieces) == 1:
            half = pieces[0].shape[1] // 2
            return pieces[0][:, half:] if lower else pieces[0][:, :half]
        return pieces[1] if lower else pieces[0]

    for r in range(1, length):
        if r in known:
            continue
        low = r & -r
        high = 1 << (r.bit_length() - 1)
        known[r] = [swapped(cut(r ^ high, False), high), swapped(cut(r ^ low, True), low)]
    return [piece for r in range(length) for piece in known[r]]


def local(ratings, row_index, col_index, row_mask, counts, owner_list, user_factors, item_factors):
    members = lax.axis_size("grp")
    block_rows = item_factors.shape[0]
    shard_rows = block_rows // members
    rows = shard_rows // CHUNKS
    scalars = (row_index, col_index, counts, owner_list)
    full_users = user_factors
    users = [user_factors]
    own_gram = None
    known = []
    for epoch in range(SUB):
        grad_user = None
        outs, olds, pieces = [], [], []
        for c in range(CHUNKS):
            if epoch == 0:
                sources = [item_factors]
            else:
                sources = gather_finish(known[c], [] if c == 0 else [grad_user])
            out = tile_call(
                epoch, c, members, scalars, ratings, row_mask, users, sources, grad_user, own_gram
            )
            grad_user = out[4]
            outs.append(out)
            if epoch == 0:
                pieces.append(out[5])
                olds.append(out[6])
                if c == 0:
                    users = out[7:9]
            else:
                pieces += sources
                olds.append(sources[0])
        new_users = user_call(epoch, block_rows, owner_list, full_users, grad_user, pieces)
        full_users = new_users[0]
        shards = []
        grams = None
        for c in range(CHUNKS):
            terms_a, terms_b, found = scattered(
                epoch, c, outs[c], members, rows // 2, rows - rows // 2,
                outs[min(c + 1, CHUNKS - 1)][4],
            )
            if found:
                found[0] = tied(found[0], full_users)
            shard, gram = item_call(epoch, c, shard_rows, olds[c], terms_a, terms_b, found or grams)
            if found:
                grams = [gram]
            shards.append(shard)
        if epoch + 1 < SUB:
            users, own_gram = new_users[1:3], new_users[3]
            known = []
            for shard in shards:
                early = [piece for r, piece in known[-1].items() if r] if known else []
                known.append(gather_start(tied(shard, *early)))
    finals = [moved(shard, 0) for shard in shards]
    return full_users, jnp.concatenate(finals, axis=0).astype(F32)


def solution(mesh):
    in_specs = (
        P(None, "blk", "grp", None, None, None),
        P(None, "blk", "grp", None),
        P(None, "blk", "grp", None),
        P(None, "blk", "grp", None, None),
        P(None, "blk", "grp"),
        P(None, "blk"),
        P(("blk", "grp"), None),
        P("blk", None),
    )
    out_specs = (P(("blk", "grp"), None), P(("blk", "grp"), None))
    return jax.shard_map(local, mesh=mesh, in_specs=in_specs, out_specs=out_specs, check_vma=False)
```

```python
import functools

import jax
import jax.numpy as jnp
from jax import lax
from jax.experimental import pallas as pl
from jax.experimental.pallas import tpu as pltpu
from jax.sharding import PartitionSpec as P

SUB = 2
LEARN = 0.004
GRAM = 256.0
RIDGE = 1.0
CHUNKS = 2
F32 = jnp.float32
BF16 = jnp.bfloat16
BIG = float(jnp.finfo(jnp.bfloat16).max)

ANY = pl.BlockSpec(memory_space=pl.ANY)
HBM = pl.BlockSpec(memory_space=pltpu.HBM)
VMEM = pl.BlockSpec(memory_space=pltpu.VMEM)


def params(mib):
    return pltpu.CompilerParams(vmem_limit_bytes=mib * 1024 * 1024)


def cost(flops, bytes_accessed):
    return pl.CostEstimate(flops=flops, bytes_accessed=bytes_accessed, transcendentals=0)


def over_rows(a, b):
    return lax.dot_general(a, b, (((1,), (1,)), ((), ())), preferred_element_type=F32)


def over_columns(a, b):
    return lax.dot_general(a, b, (((0,), (0,)), ((), ())), preferred_element_type=F32)


def ridge(rank):
    down = lax.broadcasted_iota(jnp.int32, (rank, rank), 0)
    across = lax.broadcasted_iota(jnp.int32, (rank, rank), 1)
    return jnp.where(down == across, RIDGE, 0.0)


def owned(gram, rows, owner):
    full = gram * (GRAM / rows) + ridge(gram.shape[0])
    return jnp.where(owner == lax.axis_index("grp"), full, 0.0).astype(BF16)


def without(members, bit):
    return [r for r in range(members) if not r & bit]


def tile_kernel(epoch, chunk, members, shard_tiles, tile, pieces, *refs):
    start_up = epoch == 0 and chunk == 0
    first = chunk == 0
    refs = list(refs)

    def take(n):
        out, refs[:n] = refs[:n], []
        return out

    row_hbm, col_hbm, plan_hbm, ratings, mask_hbm = take(5)
    users = take(1) if start_up else take(2)
    sources = take(pieces)
    grad_in = take(0 if first else 1)
    own_in = take(1 if first and epoch > 0 else 0)
    send_a, keep_a, send_b, keep_b, grad_user = take(5)
    if epoch == 0:
        items, old = take(2)
    if start_up:
        user_bf, user_t = take(2)
    else:
        user_bf, user_t = users
    (row_ref, col_ref, plan_ref, mask, parts, held, error_0, error_1,
     slots, slot_row, slot_place, sem_tile, sem_item, sem_small) = take(14)
    if epoch == 0:
        items_f, = take(1)
    else:
        items, = take(1)
    if start_up:
        users_f, = take(1)
    errors = (error_0, error_1)

    me = lax.axis_index("grp")
    chunk_tiles = shard_tiles // CHUNKS
    rows = chunk_tiles * tile
    half = rows // 2
    bits_tile = chunk_tiles.bit_length() - 1
    bits_shard = shard_tiles.bit_length() - 1

    pairs = [(row_hbm, row_ref), (col_hbm, col_ref), (plan_hbm, plan_ref),
             (mask_hbm.at[epoch, 0, 0], mask)]
    if not first:
        pairs.append((grad_in[0], grad_user))
    if start_up:
        pairs.append((users[0], users_f))
    small = [
        pltpu.make_async_copy(src, dst, sem_small.at[i]) for i, (src, dst) in enumerate(pairs)
    ]
    for copy in small:
        copy.start()
    copies = []
    if epoch == 0:
        for r in range(members):
            start = pl.multiple_of((me ^ r) * (shard_tiles * tile) + chunk * rows, rows)
            copies.append(
                pltpu.make_async_copy(
                    sources[0].at[pl.ds(start, rows)], items_f.at[pl.ds(r * rows, rows)], sem_item.at[r]
                )
            )
    else:
        at = 0
        for i, source in enumerate(sources):
            width = source.shape[1]
            copies.append(
                pltpu.make_async_copy(source, items.at[:, pl.ds(at, width)], sem_item.at[i])
            )
            at += width
    for copy in copies:
        copy.start()
    for copy in small[:3]:
        copy.wait()

    count = plan_ref[0, epoch]

    def pick(t, found):
        col = col_ref[epoch, 0, 0, t]
        slots[found] = t
        slot_row[found] = row_ref[epoch, 0, 0, t]
        slot_place[found] = ((col >> bits_shard) ^ me) * chunk_tiles + (col & (chunk_tiles - 1))
        here = ((col >> bits_tile) & (CHUNKS - 1)) == chunk
        return found + jnp.where(here & (t < count), 1, 0).astype(jnp.int32)

    total = lax.fori_loop(0, col_ref.shape[3], pick, jnp.int32(0), unroll=8)

    def fetch(i):
        return pltpu.make_async_copy(ratings.at[epoch, 0, 0, slots[i]], held.at[i], sem_tile.at[i])

    def begin(i, _):
        fetch(i).start()
        return 0

    lax.fori_loop(0, total, begin, 0)

    parts[...] = jnp.zeros_like(parts)
    if first:
        grad_user[...] = jnp.zeros_like(grad_user)
    for copy in small[3:]:
        copy.wait()

    def user_tile(j, _):
        spot = pl.ds(pl.multiple_of(j * tile, tile), tile)
        part = users_f[spot]
        user_bf[spot] = part.astype(BF16)
        user_t[:, spot] = part.T.astype(BF16)
        return 0

    if start_up:
        lax.fori_loop(0, users_f.shape[0] // tile, user_tile, 0, unroll=2)

    def item_tile(own, j, _):
        spot = pl.ds(pl.multiple_of(j * tile, tile), tile)
        turned = items_f[spot].T
        items[:, spot] = turned.astype(BF16)
        if own:
            old[:, spot] = turned
        return 0

    for r, copy in enumerate(copies):
        copy.wait()
        if epoch == 0:
            lax.fori_loop(
                r * chunk_tiles, (r + 1) * chunk_tiles, functools.partial(item_tile, r == 0), 0,
                unroll=2,
            )

    def spots(i):
        row = pl.multiple_of(slot_row[i] * tile, tile)
        place = pl.multiple_of(slot_place[i] * tile, tile)
        return pl.ds(row, tile), pl.ds(place, tile)

    def ready(j):
        for k in range(2):
            i = 2 * j + k

            @pl.when(i < total)
            def _():
                fetch(i).wait()

    def front(j):
        for k in range(2):
            i = jnp.minimum(2 * j + k, total - 1)
            row, place = spots(i)
            predicted = jnp.dot(user_bf[row], items[:, place], preferred_element_type=F32)
            error = (predicted - held[i].astype(F32)).astype(BF16)
            errors[k][j & 1] = jnp.clip(error, -BIG, BIG)

    def back(j):
        adds = []
        for k in range(2):
            valid = 2 * j + k < total
            i = jnp.minimum(2 * j + k, total - 1)
            row, place = spots(i)
            weight = mask[pl.ds(slots[i], 1), :].astype(F32)
            weight = jnp.where(valid, weight, 0.0)
            error = errors[k][j & 1]
            user_add = over_rows(items[:, place], error)
            item_add = jnp.dot(
                user_t[:, row] * weight.astype(BF16), error, preferred_element_type=F32
            )
            adds.append((row, place, jnp.where(weight > 0.5, user_add, 0.0), item_add))
        return adds

    def add(adds):
        for row, place, user_add, item_add in adds:
            grad_user[:, row] += user_add
            parts[:, place] += item_add

    twos = (total + 1) // 2

    @pl.when(total > 0)
    def _():
        ready(0)
        front(0)

    def step(j, _):
        ready(j + 1)
        adds = back(j)
        front(j + 1)
        add(adds)
        return 0

    lax.fori_loop(0, twos, step, 0)

    for bit, send, keep, start, width in (
        (1, send_a, keep_a, 0, half), (members // 2, send_b, keep_b, half, rows - half)
    ):
        for k, r in enumerate(without(members, bit)):
            keep[:, k * width:(k + 1) * width] = parts[:, pl.ds(r * rows + start, width)].astype(BF16)
            r = r | bit
            send[:, k * width:(k + 1) * width] = parts[:, pl.ds(r * rows + start, width)].astype(BF16)
    if start_up:
        own = jnp.dot(user_t[...], user_bf[...], preferred_element_type=F32)
        own = owned(own, users_f.shape[0], plan_ref[1, epoch])
    elif first:
        own = own_in[0][...]
    if first:
        send_a[:, members // 2 * half:] = own


def tile_call(epoch, chunk, members, scalars, ratings, row_mask, users, sources, carried, own):
    tile = ratings.shape[-1]
    slots = ratings.shape[3]
    start_up = epoch == 0 and chunk == 0
    first = chunk == 0
    user_rows, rank = users[0].shape
    if epoch == 0:
        block_rows = sources[0].shape[0]
    else:
        block_rows = sum(s.shape[1] for s in sources) * CHUNKS
    shard_tiles = block_rows // members // tile
    rows = shard_tiles // CHUNKS * tile
    half = rows // 2
    sd = jax.ShapeDtypeStruct
    wide_a, wide_b = members // 2 * half, members // 2 * (rows - half)
    extra = rank if first else 0
    out_shape = [
        sd((rank, wide_a + extra), BF16), sd((rank, wide_a), BF16),
        sd((rank, wide_b), BF16), sd((rank, wide_b), BF16), sd((rank, user_rows), F32),
    ]
    if epoch == 0:
        out_shape += [sd((rank, members * rows), BF16), sd((rank, rows), F32)]
    if start_up:
        out_shape += [sd((user_rows, rank), BF16), sd((rank, user_rows), BF16)]
    in_specs = [HBM] * 5 + ([HBM] if start_up else [VMEM] * 2)
    in_specs += [HBM if epoch == 0 else ANY] * len(sources)
    operands = [*scalars, ratings, row_mask, *users, *sources]
    if not first:
        in_specs += [ANY]
        operands += [carried]
    elif epoch > 0:
        in_specs += [VMEM]
        operands += [own]
    scratch = [
        *[pltpu.SMEM(s.shape, jnp.int32) for s in scalars],
        pltpu.VMEM((slots, tile), jnp.int32),
        pltpu.VMEM((rank, members * rows), F32),
        pltpu.VMEM((slots, tile, tile), BF16),
        *[pltpu.VMEM((2, tile, tile), BF16)] * 2,
        *[pltpu.SMEM((slots + 1,), jnp.int32)] * 3,
        pltpu.SemaphoreType.DMA((slots,)),
        pltpu.SemaphoreType.DMA((max(members, len(sources)),)),
        pltpu.SemaphoreType.DMA((6,)),
    ]
    if epoch == 0:
        scratch.append(pltpu.VMEM((members * rows, rank), F32))
    else:
        scratch.append(pltpu.VMEM((rank, members * rows), BF16))
    if start_up:
        scratch.append(pltpu.VMEM((user_rows, rank), F32))
    return pl.pallas_call(
        functools.partial(tile_kernel, epoch, chunk, members, shard_tiles, tile, len(sources)),
        out_shape=out_shape,
        in_specs=in_specs,
        out_specs=[VMEM] * len(out_shape),
        scratch_shapes=scratch,
        compiler_params=params(40),
        cost_estimate=cost(1 << 20, 1 << 16),
        name=f"tiles_{epoch}_{chunk}",
    )(*operands)


def user_kernel(epoch, block_rows, plan_ref, users, grad, *refs):
    outs = 4 if epoch + 1 < SUB else 1
    pieces, outs = refs[:-outs], refs[-outs:]
    gram = over_rows(pieces[0][...], pieces[0][...])
    for piece in pieces[1:]:
        gram += over_rows(piece[...], piece[...])
    full = gram * (GRAM / block_rows) + ridge(users.shape[1])
    pull = jnp.dot(users[...], full, precision=lax.Precision.HIGHEST, preferred_element_type=F32)
    new = users[...] - LEARN * (grad[...].T + pull)
    outs[0][...] = new
    if len(outs) > 1:
        plain = new.astype(BF16)
        turned = new.T.astype(BF16)
        outs[1][...] = plain
        outs[2][...] = turned
        own = jnp.dot(turned, plain, preferred_element_type=F32)
        outs[3][...] = owned(own, users.shape[0], plan_ref[1, epoch + 1])


def user_call(epoch, block_rows, plan, users, grad, pieces):
    rows, rank = users.shape
    sd = jax.ShapeDtypeStruct
    out_shape = [sd(users.shape, F32)]
    if epoch + 1 < SUB:
        out_shape += [sd((rows, rank), BF16), sd((rank, rows), BF16), sd((rank, rank), BF16)]
    return pl.pallas_call(
        functools.partial(user_kernel, epoch, block_rows),
        out_shape=out_shape,
        in_specs=[pl.BlockSpec(memory_space=pltpu.SMEM)] + [VMEM] * (2 + len(pieces)),
        out_specs=[VMEM] * len(out_shape),
        compiler_params=params(40),
        cost_estimate=cost(1 << 20, 1 << 16),
        name=f"users_{epoch}",
    )(plan, users, grad, *pieces)


def summed(refs, names, r, width):
    total = None
    for ref, order in zip(refs, names):
        k = order.index(r)
        term = ref[:, k * width:(k + 1) * width].astype(F32)
        total = term if total is None else total + term
    return total


def mid_kernel(paths, grams, *refs):
    at = 0
    outs = refs[sum(len(names) for names, _, _ in paths) + grams:]
    gram_refs = refs[len(refs) - len(paths) - grams:len(refs) - len(paths)]
    for (names, going, width), out in zip(paths, outs):
        terms = refs[at:at + len(names)]
        at += len(names)
        for k, r in enumerate(going):
            out[:, k * width:(k + 1) * width] = summed(terms, names, r, width).astype(BF16)
    if grams:
        rank = outs[0].shape[0]
        total = gram_refs[0][:, gram_refs[0].shape[1] - rank:].astype(F32)
        for ref in gram_refs[1:]:
            total += ref[:, ref.shape[1] - rank:].astype(F32)
        outs[0][:, outs[0].shape[1] - rank:] = total.astype(BF16)


def mid_call(epoch, chunk, step, paths, grams):
    rank = paths[0][0][0][0].shape[0]
    specs, operands, out_shape = [], [], []
    for terms, going, width in paths:
        specs.append(([names for _, names in terms], going, width))
        operands += [array for array, _ in terms]
        extra = rank if grams and not out_shape else 0
        out_shape.append(jax.ShapeDtypeStruct((rank, len(going) * width + extra), BF16))
    operands += grams
    return pl.pallas_call(
        functools.partial(mid_kernel, specs, len(grams)),
        out_shape=out_shape,
        in_specs=[VMEM] * len(operands),
        out_specs=[VMEM] * len(out_shape),
        compiler_params=params(40),
        cost_estimate=cost(1 << 16, 1 << 16),
        name=f"mid_{epoch}_{chunk}_{step}",
    )(*operands)


def item_kernel(epoch, count, rows, width, grams, items, *refs):
    terms_a, terms_b = refs[:count], refs[count:2 * count]
    gram_refs = refs[2 * count:2 * count + grams]
    refs = refs[2 * count + grams:]
    out = refs[0]
    rank = gram_refs[0].shape[0]
    gram = gram_refs[0][:, gram_refs[0].shape[1] - rank:]
    for ref in gram_refs[1:]:
        gram = (gram.astype(F32) + ref[:, ref.shape[1] - rank:].astype(F32)).astype(BF16)
    if grams > 1:
        refs[1][...] = gram
    zero = [[0]] * count
    grad = jnp.concatenate(
        [summed(terms_a, zero, 0, width), summed(terms_b, zero, 0, rows - width)], axis=1
    )
    if epoch == 0:
        high = items[...].astype(BF16)
        low = (items[...] - high.astype(F32)).astype(BF16)
        pull = over_columns(gram, high) + over_columns(gram, low)
    else:
        pull = over_columns(gram, items[...])
    new = items[...].astype(F32) - LEARN * (grad + pull)
    out[...] = (new if epoch + 1 < SUB else new.T).astype(BF16)


def item_call(epoch, chunk, shard_rows, items, terms_a, terms_b, grams):
    rank = grams[0].shape[0]
    rows = shard_rows // CHUNKS
    last = epoch + 1 == SUB
    out_shape = [jax.ShapeDtypeStruct((rows, rank) if last else (rank, rows), BF16)]
    if len(grams) > 1:
        out_shape.append(jax.ShapeDtypeStruct((rank, rank), BF16))
    out = pl.pallas_call(
        functools.partial(
            item_kernel, epoch, len(terms_a), rows, rows // 2, len(grams)
        ),
        out_shape=out_shape,
        in_specs=[VMEM] * (1 + 2 * len(terms_a) + len(grams)),
        out_specs=[VMEM] * len(out_shape),
        compiler_params=params(40),
        cost_estimate=cost(1 << 16, 1 << 16),
        name=f"items_{epoch}_{chunk}",
    )(items, *terms_a, *terms_b, *grams)
    return out[0], out[-1]


def swapped(value, bit):
    length = lax.axis_size("grp")
    return lax.ppermute(value, "grp", [(i, i ^ bit) for i in range(length)])


def moved(value, bit):
    length, blocks = lax.axis_size("grp"), lax.axis_size("blk")
    pairs = [
        (b * length + i, (b + 1) % blocks * length + (i ^ bit))
        for b in range(blocks)
        for i in range(length)
    ]
    return lax.ppermute(value, ("blk", "grp"), pairs)


def scattered(epoch, chunk, out, members, width_a, width_b, after):
    send_a, keep_a, send_b, keep_b = out[:4]
    bits = [1 << i for i in range(members.bit_length() - 1)]
    orders = (bits, bits[::-1])
    widths = (width_a, width_b)
    sends = [send_a, send_b]
    names = [without(members, order[0]) for order in orders]
    terms = [[(keep_a, names[0])], [(keep_b, names[1])]]
    grams = [send_a] if chunk == 0 else []
    for step in range(len(bits)):
        for p in range(2):
            arrived = swapped(sends[p], orders[p][step])
            if step == 0:
                arrived = tied(arrived, after)
            terms[p].append((arrived, names[p]))
            if p == 0 and grams:
                grams.append(arrived)
        if step + 1 == len(bits):
            break
        paths = []
        for p in range(2):
            bit = orders[p][step + 1]
            paths.append((terms[p], [r for r in names[p] if r & bit], widths[p]))
            names[p] = [r for r in names[p] if not r & bit]
        sends = mid_call(epoch, chunk, step, paths, grams)
    return [a for a, _ in terms[0]], [a for a, _ in terms[1]], grams


def tied(value, *others):
    return lax.optimization_barrier((value, *others))[0]


def gather_start(shard):
    known = {0: moved(shard, 0)}
    bit = 1
    while bit < lax.axis_size("grp"):
        known[bit] = moved(shard, bit)
        bit *= 2
    return known


def gather_finish(known, after):
    length = lax.axis_size("grp")
    known = {r: [tied(piece, *after)] for r, piece in known.items()}

    def cut(r, lower):
        pieces = known[r]
        if len(pieces) == 1:
            half = pieces[0].shape[1] // 2
            return pieces[0][:, half:] if lower else pieces[0][:, :half]
        return pieces[1] if lower else pieces[0]

    for r in range(1, length):
        if r in known:
            continue
        low = r & -r
        high = 1 << (r.bit_length() - 1)
        known[r] = [swapped(cut(r ^ high, False), high), swapped(cut(r ^ low, True), low)]
    return [piece for r in range(length) for piece in known[r]]


def local(ratings, row_index, col_index, row_mask, counts, owner_list, user_factors, item_factors):
    members = lax.axis_size("grp")
    block_rows = item_factors.shape[0]
    shard_rows = block_rows // members
    rows = shard_rows // CHUNKS
    plan = jnp.stack([counts[:, 0, 0], owner_list[:, 0]])
    row_index, col_index, plan_hbm, row_mask, first_users, ratings, item_factors = (
        pltpu.with_memory_space_constraint(array, pltpu.HBM)
        for array in (
            row_index, col_index, plan, row_mask, user_factors, ratings, item_factors
        )
    )
    scalars = (row_index, col_index, plan_hbm)
    full_users = user_factors
    users = [first_users]
    own_gram = None
    gathers = []
    for epoch in range(SUB):
        grad_user = None
        outs, olds, pieces = [], [], []
        for c in range(CHUNKS):
            if epoch == 0:
                sources = [item_factors]
            else:
                known, sources = gathers[c]
                sources = sources or gather_finish(known, [grad_user])
            out = tile_call(
                epoch, c, members, scalars, ratings, row_mask, users, sources, grad_user, own_gram
            )
            grad_user = out[4]
            outs.append(out)
            if epoch == 0:
                pieces.append(out[5])
                olds.append(out[6])
                if c == 0:
                    users = out[7:9]
            else:
                pieces += sources
                olds.append(sources[0])
        last = epoch + 1 == SUB
        if not last:
            new_users = user_call(epoch, block_rows, plan, full_users, grad_user, pieces)
            full_users = new_users[0]
        shards = []
        grams = None
        for c in range(CHUNKS):
            terms_a, terms_b, found = scattered(
                epoch, c, outs[c], members, rows // 2, rows - rows // 2,
                outs[min(c + 1, CHUNKS - 1)][4],
            )
            if found and not last:
                found[0] = tied(found[0], full_users)
            shard, gram = item_call(epoch, c, shard_rows, olds[c], terms_a, terms_b, found or grams)
            if found:
                grams = [gram]
            shards.append(shard)
        if last:
            grad_user = tied(grad_user, *shards)
            full_users = user_call(epoch, block_rows, plan, full_users, grad_user, pieces)[0]
        else:
            users, own_gram = new_users[1:3], new_users[3]
            gathers = []
            for shard in shards:
                known = gather_start(tied(shard, *early) if gathers else shard)
                if gathers:
                    gathers.append((known, None))
                else:
                    gathers.append((known, gather_finish(known, [])))
                early = [piece for r, piece in enumerate(gathers[0][1]) if r > 2]
    finals = [moved(shard, 0) for shard in shards]
    return full_users, jnp.concatenate(finals, axis=0).astype(F32)


def solution(mesh):
    in_specs = (
        P(None, "blk", "grp", None, None, None),
        P(None, "blk", "grp", None),
        P(None, "blk", "grp", None),
        P(None, "blk", "grp", None, None),
        P(None, "blk", "grp"),
        P(None, "blk"),
        P(("blk", "grp"), None),
        P("blk", None),
    )
    out_specs = (P(("blk", "grp"), None), P(("blk", "grp"), None))
    return jax.shard_map(local, mesh=mesh, in_specs=in_specs, out_specs=out_specs, check_vma=False)
```

```python
import functools

import jax
import jax.numpy as jnp
from jax import lax
from jax.experimental import pallas as pl
from jax.experimental.pallas import tpu as pltpu
from jax.sharding import PartitionSpec as P

SUB = 2
LEARN = 0.004
GRAM = 256.0
RIDGE = 1.0
CHUNKS = 2
WIDE = 4
F32 = jnp.float32
BF16 = jnp.bfloat16
BIG = float(jnp.finfo(jnp.bfloat16).max)

ANY = pl.BlockSpec(memory_space=pl.ANY)
HBM = pl.BlockSpec(memory_space=pltpu.HBM)
VMEM = pl.BlockSpec(memory_space=pltpu.VMEM)


def params(mib):
    return pltpu.CompilerParams(vmem_limit_bytes=mib * 1024 * 1024)


def cost(flops, bytes_accessed):
    return pl.CostEstimate(flops=flops, bytes_accessed=bytes_accessed, transcendentals=0)


def over_rows(a, b):
    return lax.dot_general(a, b, (((1,), (1,)), ((), ())), preferred_element_type=F32)


def over_columns(a, b):
    return lax.dot_general(a, b, (((0,), (0,)), ((), ())), preferred_element_type=F32)


def ridge(rank):
    down = lax.broadcasted_iota(jnp.int32, (rank, rank), 0)
    across = lax.broadcasted_iota(jnp.int32, (rank, rank), 1)
    return jnp.where(down == across, RIDGE, 0.0)


def owned(gram, rows, owner):
    full = gram * (GRAM / rows) + ridge(gram.shape[0])
    return jnp.where(owner == lax.axis_index("grp"), full, 0.0).astype(BF16)


def without(members, bit):
    return [r for r in range(members) if not r & bit]


def tile_kernel(epoch, chunk, members, shard_tiles, tile, pieces, *refs):
    start_up = epoch == 0 and chunk == 0
    first = chunk == 0
    refs = list(refs)

    def take(n):
        out, refs[:n] = refs[:n], []
        return out

    row_hbm, col_hbm, count_hbm, owner_hbm, ratings, mask_hbm = take(6)
    users = take(1) if start_up else take(2)
    sources = take(pieces)
    grad_in = take(0 if first else 1)
    own_in = take(1 if first and epoch > 0 else 0)
    send_a, keep_a, send_b, keep_b, grad_user = take(5)
    if epoch == 0:
        items, old = take(2)
    if start_up:
        user_bf, user_t = take(2)
    else:
        user_bf, user_t = users
    (row_ref, col_ref, count_ref, owner_ref, mask, parts, held, slots, slot_row, slot_place,
     sem_tile, sem_item, sem_small) = take(13)
    errors = take(WIDE)
    if epoch == 0:
        items_f, = take(1)
    else:
        items, = take(1)
    if start_up:
        users_f, = take(1)

    me = lax.axis_index("grp")
    chunk_tiles = shard_tiles // CHUNKS
    rows = chunk_tiles * tile
    half = rows // 2
    bits_tile = chunk_tiles.bit_length() - 1
    bits_shard = shard_tiles.bit_length() - 1

    pairs = [(row_hbm, row_ref), (col_hbm, col_ref), (count_hbm, count_ref),
             (owner_hbm, owner_ref), (mask_hbm.at[epoch, 0, 0], mask)]
    if not first:
        pairs.append((grad_in[0], grad_user))
    if start_up:
        pairs.append((users[0], users_f))
    small = [
        pltpu.make_async_copy(src, dst, sem_small.at[i]) for i, (src, dst) in enumerate(pairs)
    ]
    for copy in small:
        copy.start()
    copies = []
    if epoch == 0:
        for r in range(members):
            start = pl.multiple_of((me ^ r) * (shard_tiles * tile) + chunk * rows, rows)
            copies.append(
                pltpu.make_async_copy(
                    sources[0].at[pl.ds(start, rows)], items_f.at[pl.ds(r * rows, rows)], sem_item.at[r]
                )
            )
    else:
        at = 0
        for i, source in enumerate(sources):
            width = source.shape[1]
            copies.append(
                pltpu.make_async_copy(source, items.at[:, pl.ds(at, width)], sem_item.at[i])
            )
            at += width
    for copy in copies:
        copy.start()
    for copy in small[:4]:
        copy.wait()

    count = count_ref[0, epoch]

    def pick(t, found):
        col = col_ref[epoch, 0, 0, t]
        slots[found] = t
        slot_row[found] = row_ref[epoch, 0, 0, t]
        slot_place[found] = ((col >> bits_shard) ^ me) * chunk_tiles + (col & (chunk_tiles - 1))
        here = ((col >> bits_tile) & (CHUNKS - 1)) == chunk
        return found + jnp.where(here & (t < count), 1, 0).astype(jnp.int32)

    total = lax.fori_loop(0, col_ref.shape[3], pick, jnp.int32(0), unroll=8)

    def fetch(i):
        return pltpu.make_async_copy(ratings.at[epoch, 0, 0, slots[i]], held.at[i], sem_tile.at[i])

    def begin(i, _):
        fetch(i).start()
        return 0

    lax.fori_loop(0, total, begin, 0)

    parts[...] = jnp.zeros_like(parts)
    if first:
        grad_user[...] = jnp.zeros_like(grad_user)
    for copy in small[4:]:
        copy.wait()

    def user_tile(j, _):
        spot = pl.ds(pl.multiple_of(j * tile, tile), tile)
        part = users_f[spot].astype(BF16)
        user_bf[spot] = part
        user_t[:, spot] = part.T
        return 0

    if start_up:
        lax.fori_loop(0, users_f.shape[0] // tile, user_tile, 0, unroll=2)

    def item_tile(own, j, _):
        spot = pl.ds(pl.multiple_of(j * tile, tile), tile)
        items[:, spot] = items_f[spot].astype(BF16).T
        if own:
            old[:, spot] = items_f[spot].T
        return 0

    for r, copy in enumerate(copies):
        copy.wait()
        if epoch == 0:
            lax.fori_loop(
                r * chunk_tiles, (r + 1) * chunk_tiles, functools.partial(item_tile, r == 0), 0,
                unroll=2,
            )

    def spots(i):
        row = pl.multiple_of(slot_row[i] * tile, tile)
        place = pl.multiple_of(slot_place[i] * tile, tile)
        return pl.ds(row, tile), pl.ds(place, tile)

    def ready(j):
        for k in range(WIDE):
            i = WIDE * j + k

            @pl.when(i < total)
            def _():
                fetch(i).wait()

    def front(j):
        for k in range(WIDE):
            i = jnp.minimum(WIDE * j + k, total - 1)
            row, place = spots(i)
            predicted = jnp.dot(user_bf[row], items[:, place], preferred_element_type=F32)
            error = (predicted - held[i].astype(F32)).astype(BF16)
            errors[k][j & 1] = jnp.clip(error, -BIG, BIG)

    def back(j):
        adds = []
        for k in range(WIDE):
            valid = WIDE * j + k < total
            i = jnp.minimum(WIDE * j + k, total - 1)
            row, place = spots(i)
            weight = mask[pl.ds(slots[i], 1), :].astype(F32)
            weight = jnp.where(valid, weight, 0.0)
            error = errors[k][j & 1]
            user_add = over_rows(items[:, place], error)
            item_add = jnp.dot(
                user_t[:, row] * weight.astype(BF16), error, preferred_element_type=F32
            )
            adds.append((row, place, jnp.where(weight > 0.5, user_add, 0.0), item_add))
        return adds

    def add(adds):
        for row, place, user_add, item_add in adds:
            grad_user[:, row] += user_add
            parts[:, place] += item_add

    groups = (total + WIDE - 1) // WIDE

    @pl.when(total > 0)
    def _():
        ready(0)
        front(0)

    def step(j, _):
        ready(j + 1)
        adds = back(j)
        front(j + 1)
        add(adds)
        return 0

    lax.fori_loop(0, groups, step, 0)

    for bit, send, keep, start, width in (
        (1, send_a, keep_a, 0, half), (members // 2, send_b, keep_b, half, rows - half)
    ):
        for k, r in enumerate(without(members, bit)):
            keep[:, k * width:(k + 1) * width] = parts[:, pl.ds(r * rows + start, width)].astype(BF16)
            r = r | bit
            send[:, k * width:(k + 1) * width] = parts[:, pl.ds(r * rows + start, width)].astype(BF16)
    if start_up:
        own = jnp.dot(user_t[...], user_bf[...], preferred_element_type=F32)
        own = owned(own, users_f.shape[0], owner_ref[0, epoch])
    elif first:
        own = own_in[0][...]
    if first:
        send_a[:, members // 2 * half:] = own


def tile_call(epoch, chunk, members, scalars, ratings, row_mask, users, sources, carried, own):
    tile = ratings.shape[-1]
    slots = ratings.shape[3]
    start_up = epoch == 0 and chunk == 0
    first = chunk == 0
    user_rows, rank = users[0].shape
    if epoch == 0:
        block_rows = sources[0].shape[0]
    else:
        block_rows = sum(s.shape[1] for s in sources) * CHUNKS
    shard_tiles = block_rows // members // tile
    rows = shard_tiles // CHUNKS * tile
    half = rows // 2
    sd = jax.ShapeDtypeStruct
    wide_a, wide_b = members // 2 * half, members // 2 * (rows - half)
    extra = rank if first else 0
    out_shape = [
        sd((rank, wide_a + extra), BF16), sd((rank, wide_a), BF16),
        sd((rank, wide_b), BF16), sd((rank, wide_b), BF16), sd((rank, user_rows), F32),
    ]
    if epoch == 0:
        out_shape += [sd((rank, members * rows), BF16), sd((rank, rows), F32)]
    if start_up:
        out_shape += [sd((user_rows, rank), BF16), sd((rank, user_rows), BF16)]
    in_specs = [HBM] * 6 + ([HBM] if start_up else [VMEM] * 2)
    in_specs += [HBM if epoch == 0 else ANY] * len(sources)
    operands = [*scalars, ratings, row_mask, *users, *sources]
    if not first:
        in_specs += [ANY]
        operands += [carried]
    elif epoch > 0:
        in_specs += [VMEM]
        operands += [own]
    scratch = [
        *[pltpu.SMEM(s.shape, jnp.int32) for s in scalars],
        pltpu.VMEM((slots, tile), jnp.int32),
        pltpu.VMEM((rank, members * rows), F32),
        pltpu.VMEM((slots, tile, tile), BF16),
        *[pltpu.SMEM((slots + 1,), jnp.int32)] * 3,
        pltpu.SemaphoreType.DMA((slots,)),
        pltpu.SemaphoreType.DMA((max(members, len(sources)),)),
        pltpu.SemaphoreType.DMA((7,)),
        *[pltpu.VMEM((2, tile, tile), BF16)] * WIDE,
    ]
    if epoch == 0:
        scratch.append(pltpu.VMEM((members * rows, rank), F32))
    else:
        scratch.append(pltpu.VMEM((rank, members * rows), BF16))
    if start_up:
        scratch.append(pltpu.VMEM((user_rows, rank), F32))
    return pl.pallas_call(
        functools.partial(tile_kernel, epoch, chunk, members, shard_tiles, tile, len(sources)),
        out_shape=out_shape,
        in_specs=in_specs,
        out_specs=[VMEM] * len(out_shape),
        scratch_shapes=scratch,
        compiler_params=params(40),
        cost_estimate=cost(1 << 20, 1 << 16),
        name=f"tiles_{epoch}_{chunk}",
    )(*operands)


def user_kernel(epoch, block_rows, owner_ref, users, grad, *refs):
    outs = 4 if epoch + 1 < SUB else 1
    pieces, outs = refs[:-outs], refs[-outs:]
    gram = over_rows(pieces[0][...], pieces[0][...])
    for piece in pieces[1:]:
        gram += over_rows(piece[...], piece[...])
    full = gram * (GRAM / block_rows) + ridge(users.shape[1])
    pull = jnp.dot(users[...], full, precision=lax.Precision.HIGHEST, preferred_element_type=F32)
    new = users[...] - LEARN * (grad[...].T + pull)
    outs[0][...] = new
    if len(outs) > 1:
        plain = new.astype(BF16)
        turned = new.T.astype(BF16)
        outs[1][...] = plain
        outs[2][...] = turned
        own = jnp.dot(turned, plain, preferred_element_type=F32)
        outs[3][...] = owned(own, users.shape[0], owner_ref[0, epoch + 1])


def user_call(epoch, block_rows, owners, users, grad, pieces):
    rows, rank = users.shape
    sd = jax.ShapeDtypeStruct
    out_shape = [sd(users.shape, F32)]
    if epoch + 1 < SUB:
        out_shape += [sd((rows, rank), BF16), sd((rank, rows), BF16), sd((rank, rank), BF16)]
    return pl.pallas_call(
        functools.partial(user_kernel, epoch, block_rows),
        out_shape=out_shape,
        in_specs=[pl.BlockSpec(memory_space=pltpu.SMEM)] + [VMEM] * (2 + len(pieces)),
        out_specs=[VMEM] * len(out_shape),
        compiler_params=params(40),
        cost_estimate=cost(1 << 20, 1 << 16),
        name=f"users_{epoch}",
    )(owners, users, grad, *pieces)


def summed(refs, names, r, width):
    total = None
    for ref, order in zip(refs, names):
        k = order.index(r)
        term = ref[:, k * width:(k + 1) * width].astype(F32)
        total = term if total is None else total + term
    return total


def mid_kernel(paths, grams, *refs):
    at = 0
    outs = refs[sum(len(names) for names, _, _ in paths) + grams:]
    gram_refs = refs[len(refs) - len(paths) - grams:len(refs) - len(paths)]
    for (names, going, width), out in zip(paths, outs):
        terms = refs[at:at + len(names)]
        at += len(names)
        for k, r in enumerate(going):
            out[:, k * width:(k + 1) * width] = summed(terms, names, r, width).astype(BF16)
    if grams:
        rank = outs[0].shape[0]
        total = gram_refs[0][:, gram_refs[0].shape[1] - rank:].astype(F32)
        for ref in gram_refs[1:]:
            total += ref[:, ref.shape[1] - rank:].astype(F32)
        outs[0][:, outs[0].shape[1] - rank:] = total.astype(BF16)


def mid_call(epoch, chunk, step, paths, grams):
    rank = paths[0][0][0][0].shape[0]
    specs, operands, out_shape = [], [], []
    for terms, going, width in paths:
        specs.append(([names for _, names in terms], going, width))
        operands += [array for array, _ in terms]
        extra = rank if grams and not out_shape else 0
        out_shape.append(jax.ShapeDtypeStruct((rank, len(going) * width + extra), BF16))
    operands += grams
    return pl.pallas_call(
        functools.partial(mid_kernel, specs, len(grams)),
        out_shape=out_shape,
        in_specs=[VMEM] * len(operands),
        out_specs=[VMEM] * len(out_shape),
        compiler_params=params(40),
        cost_estimate=cost(1 << 16, 1 << 16),
        name=f"mid_{epoch}_{chunk}_{step}",
    )(*operands)


def item_kernel(epoch, count, rows, width, grams, items, *refs):
    terms_a, terms_b = refs[:count], refs[count:2 * count]
    gram_refs = refs[2 * count:2 * count + grams]
    refs = refs[2 * count + grams:]
    out = refs[0]
    rank = gram_refs[0].shape[0]
    gram = gram_refs[0][:, gram_refs[0].shape[1] - rank:]
    for ref in gram_refs[1:]:
        gram = (gram.astype(F32) + ref[:, ref.shape[1] - rank:].astype(F32)).astype(BF16)
    if grams > 1:
        refs[1][...] = gram
    zero = [[0]] * count
    grad = jnp.concatenate(
        [summed(terms_a, zero, 0, width), summed(terms_b, zero, 0, rows - width)], axis=1
    )
    if epoch == 0:
        high = items[...].astype(BF16)
        low = (items[...] - high.astype(F32)).astype(BF16)
        pull = over_columns(gram, high) + over_columns(gram, low)
    else:
        pull = over_columns(gram, items[...])
    new = items[...].astype(F32) - LEARN * (grad + pull)
    out[...] = (new if epoch + 1 < SUB else new.T).astype(BF16)


def item_call(epoch, chunk, shard_rows, items, terms_a, terms_b, grams):
    rank = grams[0].shape[0]
    rows = shard_rows // CHUNKS
    last = epoch + 1 == SUB
    out_shape = [jax.ShapeDtypeStruct((rows, rank) if last else (rank, rows), BF16)]
    if len(grams) > 1:
        out_shape.append(jax.ShapeDtypeStruct((rank, rank), BF16))
    out = pl.pallas_call(
        functools.partial(
            item_kernel, epoch, len(terms_a), rows, rows // 2, len(grams)
        ),
        out_shape=out_shape,
        in_specs=[VMEM] * (1 + 2 * len(terms_a) + len(grams)),
        out_specs=[VMEM] * len(out_shape),
        compiler_params=params(40),
        cost_estimate=cost(1 << 16, 1 << 16),
        name=f"items_{epoch}_{chunk}",
    )(items, *terms_a, *terms_b, *grams)
    return out[0], out[-1]


def swapped(value, bit):
    length = lax.axis_size("grp")
    return lax.ppermute(value, "grp", [(i, i ^ bit) for i in range(length)])


def moved(value, bit):
    length, blocks = lax.axis_size("grp"), lax.axis_size("blk")
    pairs = [
        (b * length + i, (b + 1) % blocks * length + (i ^ bit))
        for b in range(blocks)
        for i in range(length)
    ]
    return lax.ppermute(value, ("blk", "grp"), pairs)


def orders_of(members):
    bits = [1 << i for i in range(members.bit_length() - 1)]
    return bits, bits[::-1]


def exchanged(out, members):
    return [swapped(send, order[0]) for send, order in zip((out[0], out[2]), orders_of(members))]


def scattered(epoch, chunk, out, arrived, members, widths):
    send_a, keep_a, _, keep_b = out[:4]
    orders = orders_of(members)
    names = [without(members, order[0]) for order in orders]
    terms = [[(keep_a, names[0])], [(keep_b, names[1])]]
    grams = [send_a] if chunk == 0 else []
    for step in range(len(orders[0])):
        for p in range(2):
            terms[p].append((arrived[p], names[p]))
        if grams:
            grams.append(arrived[0])
        if step + 1 == len(orders[0]):
            break
        paths = []
        for p in range(2):
            bit = orders[p][step + 1]
            paths.append((terms[p], [r for r in names[p] if r & bit], widths[p]))
            names[p] = [r for r in names[p] if not r & bit]
        sends = mid_call(epoch, chunk, step, paths, grams)
        arrived = [swapped(sends[p], orders[p][step + 1]) for p in range(2)]
    return [a for a, _ in terms[0]], [a for a, _ in terms[1]], grams


def tied(value, *others):
    return lax.optimization_barrier((value, *others))[0]


def gather_start(shard):
    known = {0: moved(shard, 0)}
    bit = 1
    while bit < lax.axis_size("grp"):
        known[bit] = moved(shard, bit)
        bit *= 2
    return known


def gather_finish(known, after):
    length = lax.axis_size("grp")
    known = {r: [tied(piece, *after)] for r, piece in known.items()}

    def cut(r, lower):
        pieces = known[r]
        if len(pieces) == 1:
            half = pieces[0].shape[1] // 2
            return pieces[0][:, half:] if lower else pieces[0][:, :half]
        return pieces[1] if lower else pieces[0]

    for r in range(1, length):
        if r in known:
            continue
        low = r & -r
        high = 1 << (r.bit_length() - 1)
        known[r] = [swapped(cut(r ^ high, False), high), swapped(cut(r ^ low, True), low)]
    return [piece for r in range(length) for piece in known[r]]


def local(ratings, row_index, col_index, row_mask, counts, owner_list, user_factors, item_factors):
    members = lax.axis_size("grp")
    block_rows = item_factors.shape[0]
    shard_rows = block_rows // members
    rows = shard_rows // CHUNKS
    owners = owner_list.reshape(1, -1)
    row_index, col_index, counts, owner_hbm, row_mask, first_users, ratings, item_factors = (
        pltpu.with_memory_space_constraint(array, pltpu.HBM)
        for array in (
            row_index, col_index, counts.reshape(1, -1), owners, row_mask, user_factors, ratings,
            item_factors,
        )
    )
    scalars = (row_index, col_index, counts, owner_hbm)
    full_users = user_factors
    users = [first_users]
    own_gram = None
    gathers = []
    for epoch in range(SUB):
        grad_user = None
        outs, olds, pieces = [], [], []
        for c in range(CHUNKS):
            if epoch == 0:
                sources = [item_factors]
            else:
                known, sources = gathers[c]
                sources = sources or gather_finish(known, [grad_user])
            out = tile_call(
                epoch, c, members, scalars, ratings, row_mask, users, sources, grad_user, own_gram
            )
            grad_user = out[4]
            outs.append(out)
            if epoch == 0:
                pieces.append(out[5])
                olds.append(out[6])
                if c == 0:
                    users = out[7:9]
            else:
                pieces += sources
                olds.append(sources[0])
        last = epoch + 1 == SUB
        if not last:
            new_users = user_call(epoch, block_rows, owners, full_users, grad_user, pieces)
            full_users = new_users[0]
        shards = []
        grams = None
        firsts = [exchanged(out, members) for out in outs]
        for c in range(CHUNKS):
            following = min(c + 1, CHUNKS - 1)
            arrived = [tied(array, outs[following][4]) for array in firsts[c]]
            terms_a, terms_b, found = scattered(
                epoch, c, outs[c], arrived, members, (rows // 2, rows - rows // 2)
            )
            old = olds[c]
            if not last:
                old = tied(old, full_users, *firsts[following])
            shard, gram = item_call(epoch, c, shard_rows, old, terms_a, terms_b, found or grams)
            if found:
                grams = [gram]
            shards.append(shard)
        if last:
            grad_user = tied(grad_user, *shards)
            full_users = user_call(epoch, block_rows, owners, full_users, grad_user, pieces)[0]
        else:
            users, own_gram = new_users[1:3], new_users[3]
            gathers = []
            for shard in shards:
                known = gather_start(tied(shard, *early) if gathers else shard)
                if gathers:
                    gathers.append((known, None))
                else:
                    gathers.append((known, gather_finish(known, [])))
                early = [piece for r, piece in enumerate(gathers[0][1]) if r > 2]
    finals = [moved(shard, 0) for shard in shards]
    return full_users, jnp.concatenate(finals, axis=0).astype(F32)


def solution(mesh):
    in_specs = (
        P(None, "blk", "grp", None, None, None),
        P(None, "blk", "grp", None),
        P(None, "blk", "grp", None),
        P(None, "blk", "grp", None, None),
        P(None, "blk", "grp"),
        P(None, "blk"),
        P(("blk", "grp"), None),
        P("blk", None),
    )
    out_specs = (P(("blk", "grp"), None), P(("blk", "grp"), None))
    return jax.shard_map(local, mesh=mesh, in_specs=in_specs, out_specs=out_specs, check_vma=False)
```

```python
import functools

import jax
import jax.numpy as jnp
from jax import lax
from jax.experimental import pallas as pl
from jax.experimental.pallas import tpu as pltpu
from jax.sharding import PartitionSpec as P

SUB = 2
LEARN = 0.004
GRAM = 256.0
RIDGE = 1.0
CHUNKS = 2
WIDE = 4
F32 = jnp.float32
BF16 = jnp.bfloat16
BIG = float(jnp.finfo(jnp.bfloat16).max)

ANY = pl.BlockSpec(memory_space=pl.ANY)
HBM = pl.BlockSpec(memory_space=pltpu.HBM)
VMEM = pl.BlockSpec(memory_space=pltpu.VMEM)


def params(mib):
    return pltpu.CompilerParams(vmem_limit_bytes=mib * 1024 * 1024)


def declared(name):
    flops = {"tiles": 16e9, "users": 10e9, "items": 1.2e9, "mid": 0.2e9}[name.split("_")[0]]
    return pl.CostEstimate(flops=int(flops), bytes_accessed=1 << 16, transcendentals=0)


def over_rows(a, b):
    return lax.dot_general(a, b, (((1,), (1,)), ((), ())), preferred_element_type=F32)


def over_columns(a, b):
    return lax.dot_general(a, b, (((0,), (0,)), ((), ())), preferred_element_type=F32)


def ridge(rank):
    down = lax.broadcasted_iota(jnp.int32, (rank, rank), 0)
    across = lax.broadcasted_iota(jnp.int32, (rank, rank), 1)
    return jnp.where(down == across, RIDGE, 0.0)


def owned(gram, rows, owner):
    full = gram * (GRAM / rows) + ridge(gram.shape[0])
    return jnp.where(owner == lax.axis_index("grp"), full, 0.0).astype(BF16)


def without(members, bit):
    return [r for r in range(members) if not r & bit]


def chunk_columns(members, rows, direct):
    half = rows // 2
    found = []
    alone = []
    for bit, start, width in ((1, 0, half), (members // 2, half, rows - half)):
        names = [r for r in without(members, bit) if r or not direct]
        found.append([(r | bit, start, width) for r in names])
        found.append([(r, start, width) for r in names])
        alone.append([(bit, start, width)])
    return found + [*alone, [(0, 0, rows)]] if direct else found


def tile_kernel(epoch, chunk, direct, members, shard_tiles, tile, pieces, *refs):
    start_up = epoch == 0 and chunk == 0
    first = chunk == 0
    refs = list(refs)

    def take(n):
        out, refs[:n] = refs[:n], []
        return out

    row_hbm, col_hbm, count_hbm, owner_hbm, ratings, mask_hbm = take(6)
    users = take(1) if start_up else take(2)
    sources = take(len(pieces))
    grad_in = take(0 if first else 1)
    own_in = take(1 if first and epoch > 0 else 0)
    outs = take(7 if direct else 4)
    grad_user, = take(1)
    if epoch == 0:
        items, old = take(2)
    if start_up:
        user_bf, user_t = take(2)
    else:
        user_bf, user_t = users
    (row_ref, col_ref, count_ref, owner_ref, mask, parts, held, slots, slot_row, slot_place,
     sem_tile, sem_item, sem_small) = take(13)
    errors = take(WIDE)
    if epoch == 0:
        items_f, = take(1)
    else:
        items, = take(1)
    if start_up:
        users_f, = take(1)

    me = lax.axis_index("grp")
    chunk_tiles = shard_tiles // CHUNKS
    rows = chunk_tiles * tile
    half = rows // 2
    bits_tile = chunk_tiles.bit_length() - 1
    bits_shard = shard_tiles.bit_length() - 1

    pairs = [(row_hbm, row_ref), (col_hbm, col_ref), (count_hbm, count_ref),
             (owner_hbm, owner_ref), (mask_hbm.at[epoch, 0, 0], mask)]
    if not first:
        pairs.append((grad_in[0], grad_user))
    if start_up:
        pairs.append((users[0], users_f))
    small = [
        pltpu.make_async_copy(src, dst, sem_small.at[i]) for i, (src, dst) in enumerate(pairs)
    ]
    for copy in small:
        copy.start()
    copies = []
    if epoch == 0:
        for r in range(members):
            start = pl.multiple_of((me ^ r) * (shard_tiles * tile) + chunk * rows, rows)
            copies.append(
                pltpu.make_async_copy(
                    sources[0].at[pl.ds(start, rows)], items_f.at[pl.ds(r * rows, rows)], sem_item.at[r]
                )
            )
    else:
        for source, columns in zip(sources, pieces):
            at = 0
            for r, start, width in columns:
                copies.append(
                    pltpu.make_async_copy(
                        source.at[:, pl.ds(at, width)], items.at[:, pl.ds(r * rows + start, width)],
                        sem_item.at[len(copies)],
                    )
                )
                at += width
    for copy in copies:
        copy.start()
    for copy in small[:4]:
        copy.wait()

    count = count_ref[0, epoch]

    def pick(t, found):
        col = col_ref[epoch, 0, 0, t]
        slots[found] = t
        slot_row[found] = row_ref[epoch, 0, 0, t]
        slot_place[found] = ((col >> bits_shard) ^ me) * chunk_tiles + (col & (chunk_tiles - 1))
        here = ((col >> bits_tile) & (CHUNKS - 1)) == chunk
        return found + jnp.where(here & (t < count), 1, 0).astype(jnp.int32)

    total = lax.fori_loop(0, col_ref.shape[3], pick, jnp.int32(0), unroll=8)

    def fetch(i):
        return pltpu.make_async_copy(ratings.at[epoch, 0, 0, slots[i]], held.at[i], sem_tile.at[i])

    def begin(i, _):
        fetch(i).start()
        return 0

    lax.fori_loop(0, total, begin, 0)

    parts[...] = jnp.zeros_like(parts)
    if first:
        grad_user[...] = jnp.zeros_like(grad_user)
    for copy in small[4:]:
        copy.wait()

    def user_tile(j, _):
        spot = pl.ds(pl.multiple_of(j * tile, tile), tile)
        part = users_f[spot].astype(BF16)
        user_bf[spot] = part
        user_t[:, spot] = part.T
        return 0

    if start_up:
        lax.fori_loop(0, users_f.shape[0] // tile, user_tile, 0, unroll=2)

    def item_tile(own, j, _):
        spot = pl.ds(pl.multiple_of(j * tile, tile), tile)
        items[:, spot] = items_f[spot].astype(BF16).T
        if own:
            old[:, spot] = items_f[spot].T
        return 0

    for r, copy in enumerate(copies):
        copy.wait()
        if epoch == 0:
            lax.fori_loop(
                r * chunk_tiles, (r + 1) * chunk_tiles, functools.partial(item_tile, r == 0), 0,
                unroll=2,
            )

    def spots(i):
        row = pl.multiple_of(slot_row[i] * tile, tile)
        place = pl.multiple_of(slot_place[i] * tile, tile)
        return pl.ds(row, tile), pl.ds(place, tile)

    def ready(j):
        for k in range(WIDE):
            i = WIDE * j + k

            @pl.when(i < total)
            def _():
                fetch(i).wait()

    def front(j):
        for k in range(WIDE):
            i = jnp.minimum(WIDE * j + k, total - 1)
            row, place = spots(i)
            predicted = jnp.dot(user_bf[row], items[:, place], preferred_element_type=F32)
            error = (predicted - held[i].astype(F32)).astype(BF16)
            errors[k][j & 1] = jnp.clip(error, -BIG, BIG)

    def back(j):
        adds = []
        for k in range(WIDE):
            valid = WIDE * j + k < total
            i = jnp.minimum(WIDE * j + k, total - 1)
            row, place = spots(i)
            weight = mask[pl.ds(slots[i], 1), :].astype(F32)
            weight = jnp.where(valid, weight, 0.0)
            error = errors[k][j & 1]
            user_add = over_rows(items[:, place], error)
            item_add = jnp.dot(
                user_t[:, row] * weight.astype(BF16), error, preferred_element_type=F32
            )
            adds.append((row, place, jnp.where(weight > 0.5, user_add, 0.0), item_add))
        return adds

    def add(adds):
        for row, place, user_add, item_add in adds:
            grad_user[:, row] += user_add
            parts[:, place] += item_add

    groups = (total + WIDE - 1) // WIDE

    @pl.when(total > 0)
    def _():
        ready(0)
        front(0)

    def step(j, _):
        ready(j + 1)
        adds = back(j)
        front(j + 1)
        add(adds)
        return 0

    lax.fori_loop(0, groups, step, 0)

    for out, columns in zip(outs, chunk_columns(members, rows, direct)):
        at = 0
        for r, start, width in columns:
            out[:, at:at + width] = parts[:, pl.ds(r * rows + start, width)].astype(BF16)
            at += width
    if start_up:
        own = jnp.dot(user_t[...], user_bf[...], preferred_element_type=F32)
        own = owned(own, users_f.shape[0], owner_ref[0, epoch])
    elif first:
        own = own_in[0][...]
    if first:
        outs[0][:, members // 2 * half:] = own


def tile_call(
    epoch, chunk, direct, members, scalars, ratings, row_mask, users, sources, carried, own
):
    tile = ratings.shape[-1]
    slots = ratings.shape[3]
    start_up = epoch == 0 and chunk == 0
    first = chunk == 0
    user_rows, rank = users[0].shape
    pieces = [columns for _, columns in sources]
    sources = [array for array, _ in sources]
    if epoch == 0:
        block_rows = sources[0].shape[0]
    else:
        block_rows = sum(s.shape[1] for s in sources) * CHUNKS
    shard_tiles = block_rows // members // tile
    rows = shard_tiles // CHUNKS * tile
    sd = jax.ShapeDtypeStruct
    widths = [sum(w for _, _, w in columns) for columns in chunk_columns(members, rows, direct)]
    widths[0] += rank if first else 0
    out_shape = [sd((rank, width), BF16) for width in widths] + [sd((rank, user_rows), F32)]
    if epoch == 0:
        out_shape += [sd((rank, members * rows), BF16), sd((rank, rows), F32)]
    if start_up:
        out_shape += [sd((user_rows, rank), BF16), sd((rank, user_rows), BF16)]
    in_specs = [HBM] * 6 + ([HBM] if start_up else [VMEM] * 2)
    in_specs += [HBM if epoch == 0 else ANY] * len(sources)
    operands = [*scalars, ratings, row_mask, *users, *sources]
    if not first:
        in_specs += [ANY]
        operands += [carried]
    elif epoch > 0:
        in_specs += [VMEM]
        operands += [own]
    scratch = [
        *[pltpu.SMEM(s.shape, jnp.int32) for s in scalars],
        pltpu.VMEM((slots, tile), jnp.int32),
        pltpu.VMEM((rank, members * rows), F32),
        pltpu.VMEM((slots, tile, tile), BF16),
        *[pltpu.SMEM((slots + 1,), jnp.int32)] * 3,
        pltpu.SemaphoreType.DMA((slots,)),
        pltpu.SemaphoreType.DMA((2 * members,)),
        pltpu.SemaphoreType.DMA((7,)),
        *[pltpu.VMEM((2, tile, tile), BF16)] * WIDE,
    ]
    if epoch == 0:
        scratch.append(pltpu.VMEM((members * rows, rank), F32))
    else:
        scratch.append(pltpu.VMEM((rank, members * rows), BF16))
    if start_up:
        scratch.append(pltpu.VMEM((user_rows, rank), F32))
    return pl.pallas_call(
        functools.partial(
            tile_kernel, epoch, chunk, direct, members, shard_tiles, tile, pieces
        ),
        out_shape=out_shape,
        in_specs=in_specs,
        out_specs=[VMEM] * len(out_shape),
        scratch_shapes=scratch,
        compiler_params=params(40),
        cost_estimate=declared(f"tiles_{epoch}_{chunk}"),
        name=f"tiles_{epoch}_{chunk}",
    )(*operands)


def user_kernel(epoch, block_rows, owner_ref, users, grad, *refs):
    outs = 4 if epoch + 1 < SUB else 1
    pieces, outs = refs[:-outs], refs[-outs:]
    gram = over_rows(pieces[0][...], pieces[0][...])
    for piece in pieces[1:]:
        gram += over_rows(piece[...], piece[...])
    full = gram * (GRAM / block_rows) + ridge(users.shape[1])
    pull = jnp.dot(users[...], full, precision=lax.Precision.HIGHEST, preferred_element_type=F32)
    new = users[...] - LEARN * (grad[...].T + pull)
    outs[0][...] = new
    if len(outs) > 1:
        plain = new.astype(BF16)
        turned = new.T.astype(BF16)
        outs[1][...] = plain
        outs[2][...] = turned
        own = jnp.dot(turned, plain, preferred_element_type=F32)
        outs[3][...] = owned(own, users.shape[0], owner_ref[0, epoch + 1])


def user_call(epoch, block_rows, owners, users, grad, pieces):
    rows, rank = users.shape
    sd = jax.ShapeDtypeStruct
    out_shape = [sd(users.shape, F32)]
    if epoch + 1 < SUB:
        out_shape += [sd((rows, rank), BF16), sd((rank, rows), BF16), sd((rank, rank), BF16)]
    return pl.pallas_call(
        functools.partial(user_kernel, epoch, block_rows),
        out_shape=out_shape,
        in_specs=[pl.BlockSpec(memory_space=pltpu.SMEM)] + [VMEM] * (2 + len(pieces)),
        out_specs=[VMEM] * len(out_shape),
        compiler_params=params(40),
        cost_estimate=declared(f"users_{epoch}"),
        name=f"users_{epoch}",
    )(owners, users, grad, *pieces)


def summed(refs, names, r, width):
    total = None
    for ref, order in zip(refs, names):
        k = order.index(r)
        term = ref[:, k * width:(k + 1) * width].astype(F32)
        total = term if total is None else total + term
    return total


def mid_kernel(paths, grams, *refs):
    at = 0
    outs = refs[sum(len(names) for names, _, _ in paths) + grams:]
    gram_refs = refs[len(refs) - len(paths) - grams:len(refs) - len(paths)]
    for (names, going, width), out in zip(paths, outs):
        terms = refs[at:at + len(names)]
        at += len(names)
        for k, r in enumerate(going):
            out[:, k * width:(k + 1) * width] = summed(terms, names, r, width).astype(BF16)
    if grams:
        rank = outs[0].shape[0]
        total = gram_refs[0][:, gram_refs[0].shape[1] - rank:].astype(F32)
        for ref in gram_refs[1:]:
            total += ref[:, ref.shape[1] - rank:].astype(F32)
        outs[0][:, outs[0].shape[1] - rank:] = total.astype(BF16)


def mid_call(epoch, chunk, step, paths, grams):
    rank = paths[0][0][0][0].shape[0]
    specs, operands, out_shape = [], [], []
    for terms, going, width in paths:
        specs.append(([names for _, names in terms], going, width))
        operands += [array for array, _ in terms]
        extra = rank if grams and not out_shape else 0
        out_shape.append(jax.ShapeDtypeStruct((rank, len(going) * width + extra), BF16))
    operands += grams
    return pl.pallas_call(
        functools.partial(mid_kernel, specs, len(grams)),
        out_shape=out_shape,
        in_specs=[VMEM] * len(operands),
        out_specs=[VMEM] * len(out_shape),
        compiler_params=params(40),
        cost_estimate=declared(f"mid_{epoch}_{chunk}_{step}"),
        name=f"mid_{epoch}_{chunk}_{step}",
    )(*operands)


def item_kernel(epoch, count, rows, width, grams, items, *refs):
    terms_a, terms_b = refs[:count], refs[count:2 * count]
    gram_refs = refs[2 * count:2 * count + grams]
    refs = refs[2 * count + grams:]
    out = refs[0]
    rank = gram_refs[0].shape[0]
    gram = gram_refs[0][:, gram_refs[0].shape[1] - rank:]
    for ref in gram_refs[1:]:
        gram = (gram.astype(F32) + ref[:, ref.shape[1] - rank:].astype(F32)).astype(BF16)
    if grams > 1:
        refs[1][...] = gram
    zero = [[0]] * count
    grad = jnp.concatenate(
        [summed(terms_a, zero, 0, width), summed(terms_b, zero, 0, rows - width)], axis=1
    )
    if epoch == 0:
        high = items[...].astype(BF16)
        low = (items[...] - high.astype(F32)).astype(BF16)
        pull = over_columns(gram, high) + over_columns(gram, low)
    else:
        pull = over_columns(gram, items[...])
    new = items[...].astype(F32) - LEARN * (grad + pull)
    if epoch + 1 < SUB:
        new = new.astype(BF16)
        out[...] = new
        refs[-2][...] = new[:, :width]
        refs[-1][...] = new[:, width:]
    else:
        out[:rows] = new.T.astype(BF16)
        if grams > 1:
            out[rows:] = gram


def item_call(epoch, chunk, shard_rows, items, terms_a, terms_b, grams):
    rank = grams[0].shape[0]
    rows = shard_rows // CHUNKS
    last = epoch + 1 == SUB
    tall = rows + (rank if len(grams) > 1 else 0)
    out_shape = [jax.ShapeDtypeStruct((tall, rank) if last else (rank, rows), BF16)]
    if len(grams) > 1:
        out_shape.append(jax.ShapeDtypeStruct((rank, rank), BF16))
    if not last:
        out_shape += [jax.ShapeDtypeStruct((rank, rows // 2), BF16)]
        out_shape += [jax.ShapeDtypeStruct((rank, rows - rows // 2), BF16)]
    out = pl.pallas_call(
        functools.partial(
            item_kernel, epoch, len(terms_a), rows, rows // 2, len(grams)
        ),
        out_shape=out_shape,
        in_specs=[VMEM] * (1 + 2 * len(terms_a) + len(grams)),
        out_specs=[VMEM] * len(out_shape),
        compiler_params=params(40),
        cost_estimate=declared(f"items_{epoch}_{chunk}"),
        name=f"items_{epoch}_{chunk}",
    )(items, *terms_a, *terms_b, *grams)
    gram = out[1] if len(grams) > 1 else None
    return out[0] if last else (out[0], *out[-2:]), gram


def swapped(value, bit):
    length = lax.axis_size("grp")
    return lax.ppermute(value, "grp", [(i, i ^ bit) for i in range(length)])


def moved(value, bit):
    length, blocks = lax.axis_size("grp"), lax.axis_size("blk")
    pairs = [
        (b * length + i, (b + 1) % blocks * length + (i ^ bit))
        for b in range(blocks)
        for i in range(length)
    ]
    return lax.ppermute(value, ("blk", "grp"), pairs)


def orders_of(members):
    bits = [1 << i for i in range(members.bit_length() - 1)]
    return bits, bits[::-1]


def exchanged(out, members):
    return [swapped(send, order[0]) for send, order in zip((out[0], out[2]), orders_of(members))]


def scattered(epoch, chunk, out, arrived, members, widths):
    send_a, keep_a, _, keep_b = out[:4]
    orders = orders_of(members)
    names = [without(members, order[0]) for order in orders]
    terms = [[(keep_a, names[0])], [(keep_b, names[1])]]
    grams = [send_a] if chunk == 0 else []
    sends = []
    for step in range(len(orders[0])):
        for p in range(2):
            terms[p].append((arrived[p], names[p]))
        if grams:
            grams.append(arrived[0])
        if step + 1 == len(orders[0]):
            break
        paths = []
        for p in range(2):
            bit = orders[p][step + 1]
            paths.append((terms[p], [r for r in names[p] if r & bit], widths[p]))
            names[p] = [r for r in names[p] if not r & bit]
        sends = mid_call(epoch, chunk, step, paths, grams)
        arrived = [swapped(sends[p], orders[p][step + 1]) for p in range(2)]
    return [a for a, _ in terms[0]], [a for a, _ in terms[1]], grams, sends


def scattered_direct(epoch, chunk, out, arrived, members, widths):
    _, keep_a, _, keep_b = out[:4]
    orders = orders_of(members)
    names = [[r for r in without(members, order[0]) if r] for order in orders]
    terms = [[(keep_a, names[0])], [(keep_b, names[1])]]
    ended = [[moved(out[4 + p], orders[p][0])] for p in range(2)]
    own = moved(out[6], 0)
    arrived = [tied(array, own) for array in arrived]
    sends = []
    for step in range(len(orders[0]) - 1):
        paths, kinds = [], []
        for p in range(2):
            terms[p].append((arrived[p], names[p]))
            bit = orders[p][step + 1]
            paths.append((terms[p], [bit], widths[p]))
            kinds.append((p, True))
            going = [r for r in names[p] if r & bit and r != bit]
            names[p] = [r for r in names[p] if not r & bit]
            if going:
                paths.append((terms[p], going, widths[p]))
                kinds.append((p, False))
        sends = mid_call(epoch, chunk, step, paths, [])
        arrived = [None, None]
        for (p, alone), send in zip(kinds, sends):
            bit = orders[p][step + 1]
            if alone:
                ended[p].append(moved(send, bit))
            else:
                arrived[p] = swapped(send, bit)
    return own, ended[0], ended[1], sends


def final_kernel(rows, width, others, count, *refs):
    done, refs = refs[:others], refs[others:]
    items, own = refs[:2]
    sides = refs[2:2 + count], refs[2 + count:2 + 2 * count]
    out = refs[2 + 2 * count]
    for c, ref in enumerate(done):
        out[c * rows:(c + 1) * rows] = ref[:rows].astype(F32)
    gram = done[0][rows:]
    totals = []
    for side, start, size in zip(sides, (0, width), (width, rows - width)):
        total = own[:, start:start + size].astype(F32)
        for ref in side:
            total += ref[...].astype(F32)
        totals.append(total)
    grad = jnp.concatenate(totals, axis=1)
    new = items[...].astype(F32) - LEARN * (grad + over_columns(gram, items[...]))
    out[others * rows:] = new.T


def final_call(done, items, own, side_a, side_b):
    rank, rows = items.shape
    operands = [*done, items, own, *side_a, *side_b]
    return pl.pallas_call(
        functools.partial(final_kernel, rows, rows // 2, len(done), len(side_a)),
        out_shape=jax.ShapeDtypeStruct(((len(done) + 1) * rows, rank), F32),
        in_specs=[VMEM] * len(operands),
        out_specs=VMEM,
        compiler_params=params(40),
        cost_estimate=declared("items_final"),
        name="items_final",
    )(*operands)


def tied(value, *others):
    return lax.optimization_barrier((value, *others))[0]


def gathered(shard, upper, lower, after):
    length = lax.axis_size("grp")
    rows, half = shard.shape[1], upper.shape[1]
    known = {0: [moved(tied(shard, *after), 0)]}
    for bit in orders_of(length)[0]:
        known[bit] = [moved(shard, bit)]
    near = [known[bit][0] for bit in orders_of(length)[0]]

    def cut(r, p):
        pieces = known[r]
        if len(pieces) == 2:
            return pieces[p]
        return pieces[0][:, half:] if p else pieces[0][:, :half]

    for r in range(1, length):
        if r not in known:
            low, high = r & -r, 1 << (r.bit_length() - 1)
            sent = [cut(r ^ high, 0), cut(r ^ low, 1)]
            sent = [tied(piece, *after) for piece in sent]
            known[r] = [swapped(sent[0], high), swapped(sent[1], low)]
    found = []
    for r, pieces in known.items():
        spots = [(0, rows)] if len(pieces) == 1 else [(0, half), (half, rows - half)]
        found += [(piece, [(r, *spot)]) for piece, spot in zip(pieces, spots)]
    return found, near


def local(ratings, row_index, col_index, row_mask, counts, owner_list, user_factors, item_factors):
    members = lax.axis_size("grp")
    block_rows = item_factors.shape[0]
    shard_rows = block_rows // members
    rows = shard_rows // CHUNKS
    owners = owner_list.reshape(1, -1)
    row_index, col_index, counts, owner_hbm, row_mask, first_users, ratings, item_factors = (
        pltpu.with_memory_space_constraint(array, pltpu.HBM)
        for array in (
            row_index, col_index, counts.reshape(1, -1), owners, row_mask, user_factors, ratings,
            item_factors,
        )
    )
    scalars = (row_index, col_index, counts, owner_hbm)
    full_users = user_factors
    users = [first_users]
    own_gram = None
    gathers = []
    for epoch in range(SUB):
        grad_user = None
        outs, olds, pieces = [], [], []
        for c in range(CHUNKS):
            if epoch == 0:
                sources = [(item_factors, None)]
            else:
                sources = gathers[c]
                if epoch + 1 == SUB and c + 1 == CHUNKS:
                    kept = moved(tied(sources[0][0], grad_user), 0)
            direct = epoch + 1 == SUB and c + 1 == CHUNKS
            out = tile_call(
                epoch, c, direct, members, scalars, ratings, row_mask, users, sources, grad_user,
                own_gram,
            )
            grad_user = out[7 if direct else 4]
            outs.append(out)
            if epoch == 0:
                pieces.append(out[5])
                olds.append(out[6])
                if c == 0:
                    users = out[7:9]
            else:
                pieces += [array for array, _ in sources]
                olds.append(sources[0][0])
        last = epoch + 1 == SUB
        if not last:
            new_users = user_call(epoch, block_rows, owners, full_users, grad_user, pieces)
            full_users = new_users[0]
        shards = []
        grams = None
        reduced = []
        ahead = None
        for c in range(CHUNKS):
            arrived = ahead if ahead else exchanged(outs[c], members)
            arrived = [tied(array, grad_user if last else outs[-1][4]) for array in arrived]
            if last:
                if c == 0:
                    ahead = exchanged(outs[1], members)
                    arrived = [tied(array, kept, *ahead) for array in arrived]
                else:
                    arrived = [tied(array, grad_user) for array in ahead]
            reduce = scattered_direct if last and c + 1 == CHUNKS else scattered
            reduced.append(
                reduce(epoch, c, outs[c], arrived, members, (rows // 2, rows - rows // 2))
            )
        for c in range(CHUNKS - 1 if last else CHUNKS):
            terms_a, terms_b, found, sent = reduced[c]
            old = olds[c]
            if not last:
                old = tied(old, *reduced[min(c + 1, CHUNKS - 1)][3])
                old = tied(old, full_users)
            shard, gram = item_call(epoch, c, shard_rows, old, terms_a, terms_b, found or grams)
            if found:
                grams = [gram]
            shards.append(shard)
        if last:
            done = [moved(shard, 0) for shard in shards]
            own, side_a, side_b, sent = reduced[-1]
            grad_user = tied(grad_user, *sent)
            item_final = final_call(done, kept, own, side_a, side_b)
            full_users = user_call(epoch, block_rows, owners, full_users, grad_user, pieces)[0]
        else:
            users, own_gram = new_users[1:3], new_users[3]
            gathers = [gathered(*shard, [shards[-1][0]]) for shard in shards]
            near = gathers[-1][1]
            gathers = [found for found, _ in gathers]
            (array, columns), *rest = gathers[0]
            gathers[0] = [(tied(array, *near), columns), *rest]
    return full_users, item_final


def solution(mesh):
    in_specs = (
        P(None, "blk", "grp", None, None, None),
        P(None, "blk", "grp", None),
        P(None, "blk", "grp", None),
        P(None, "blk", "grp", None, None),
        P(None, "blk", "grp"),
        P(None, "blk"),
        P(("blk", "grp"), None),
        P("blk", None),
    )
    out_specs = (P(("blk", "grp"), None), P(("blk", "grp"), None))
    return jax.shard_map(local, mesh=mesh, in_specs=in_specs, out_specs=out_specs, check_vma=False)
```

```python
import functools

import jax
import jax.numpy as jnp
from jax import lax
from jax.experimental import pallas as pl
from jax.experimental.pallas import tpu as pltpu
from jax.sharding import PartitionSpec as P

SUB = 2
LEARN = 0.004
GRAM = 256.0
RIDGE = 1.0
CHUNKS = 2
WIDE = 4
F32 = jnp.float32
BF16 = jnp.bfloat16
BIG = float(jnp.finfo(jnp.bfloat16).max)

ANY = pl.BlockSpec(memory_space=pl.ANY)
HBM = pl.BlockSpec(memory_space=pltpu.HBM)
VMEM = pl.BlockSpec(memory_space=pltpu.VMEM)


def params(mib):
    return pltpu.CompilerParams(vmem_limit_bytes=mib * 1024 * 1024)


def declared(name):
    costs = {"tiles": 16e9, "users": 10e9, "items": 1.2e9, "mid": 0.2e9, "mid_1_1_0": 1e9}
    flops = costs.get(name, costs[name.split("_")[0]])
    return pl.CostEstimate(flops=int(flops), bytes_accessed=1 << 16, transcendentals=0)


def over_rows(a, b):
    return lax.dot_general(a, b, (((1,), (1,)), ((), ())), preferred_element_type=F32)


def over_columns(a, b):
    return lax.dot_general(a, b, (((0,), (0,)), ((), ())), preferred_element_type=F32)


def ridge(rank):
    down = lax.broadcasted_iota(jnp.int32, (rank, rank), 0)
    across = lax.broadcasted_iota(jnp.int32, (rank, rank), 1)
    return jnp.where(down == across, RIDGE, 0.0)


def owned(gram, rows, owner):
    full = gram * (GRAM / rows) + ridge(gram.shape[0])
    return jnp.where(owner == lax.axis_index("grp"), full, 0.0).astype(BF16)


def without(members, bit):
    return [r for r in range(members) if not r & bit]


def chunk_columns(members, rows, direct):
    half = rows // 2
    found = []
    alone = []
    for bit, start, width in ((1, 0, half), (members // 2, half, rows - half)):
        names = [r for r in without(members, bit) if r or not direct]
        found.append([(r | bit, start, width) for r in names])
        found.append([(r, start, width) for r in names])
        alone.append([(bit, start, width)])
    return found + [*alone, [(0, 0, rows)]] if direct else found


def tile_kernel(epoch, chunk, direct, members, shard_tiles, tile, pieces, *refs):
    start_up = epoch == 0 and chunk == 0
    first = chunk == 0
    refs = list(refs)

    def take(n):
        out, refs[:n] = refs[:n], []
        return out

    row_hbm, col_hbm, count_hbm, owner_hbm, ratings, mask_hbm = take(6)
    users = take(1) if start_up else take(2)
    sources = take(len(pieces))
    grad_in = take(0 if first else 1)
    own_in = take(1 if first and epoch > 0 else 0)
    outs = take(7 if direct else 4)
    grad_user, = take(1)
    if epoch == 0:
        items, old = take(2)
    if start_up:
        user_bf, user_t = take(2)
    else:
        user_bf, user_t = users
    (row_ref, col_ref, count_ref, owner_ref, mask, parts, held, slots, slot_row, slot_place,
     sem_tile, sem_item, sem_small) = take(13)
    errors = take(WIDE)
    if epoch == 0:
        items_f, = take(1)
    else:
        items, = take(1)
    if start_up:
        users_f, = take(1)

    me = lax.axis_index("grp")
    chunk_tiles = shard_tiles // CHUNKS
    rows = chunk_tiles * tile
    half = rows // 2
    bits_tile = chunk_tiles.bit_length() - 1
    bits_shard = shard_tiles.bit_length() - 1

    pairs = [(row_hbm, row_ref), (col_hbm, col_ref), (count_hbm, count_ref),
             (owner_hbm, owner_ref), (mask_hbm.at[epoch, 0, 0], mask)]
    if not first:
        pairs.append((grad_in[0], grad_user))
    if start_up:
        pairs.append((users[0], users_f))
    small = [
        pltpu.make_async_copy(src, dst, sem_small.at[i]) for i, (src, dst) in enumerate(pairs)
    ]
    for copy in small:
        copy.start()
    copies = []
    if epoch == 0:
        for r in range(members):
            start = pl.multiple_of((me ^ r) * (shard_tiles * tile) + chunk * rows, rows)
            copies.append(
                pltpu.make_async_copy(
                    sources[0].at[pl.ds(start, rows)], items_f.at[pl.ds(r * rows, rows)], sem_item.at[r]
                )
            )
    else:
        for source, columns in zip(sources, pieces):
            at = 0
            for r, start, width in columns:
                copies.append(
                    pltpu.make_async_copy(
                        source.at[:, pl.ds(at, width)], items.at[:, pl.ds(r * rows + start, width)],
                        sem_item.at[len(copies)],
                    )
                )
                at += width
    for copy in copies:
        copy.start()
    for copy in small[:4]:
        copy.wait()

    count = count_ref[0, epoch]

    def pick(t, found):
        col = col_ref[epoch, 0, 0, t]
        slots[found] = t
        slot_row[found] = row_ref[epoch, 0, 0, t]
        slot_place[found] = ((col >> bits_shard) ^ me) * chunk_tiles + (col & (chunk_tiles - 1))
        here = ((col >> bits_tile) & (CHUNKS - 1)) == chunk
        return found + jnp.where(here & (t < count), 1, 0).astype(jnp.int32)

    total = lax.fori_loop(0, col_ref.shape[3], pick, jnp.int32(0), unroll=8)

    def fetch(i):
        return pltpu.make_async_copy(ratings.at[epoch, 0, 0, slots[i]], held.at[i], sem_tile.at[i])

    def begin(i, _):
        fetch(i).start()
        return 0

    lax.fori_loop(0, total, begin, 0)

    parts[...] = jnp.zeros_like(parts)
    if first:
        grad_user[...] = jnp.zeros_like(grad_user)
    for copy in small[4:]:
        copy.wait()

    def user_tile(j, _):
        spot = pl.ds(pl.multiple_of(j * tile, tile), tile)
        part = users_f[spot].astype(BF16)
        user_bf[spot] = part
        user_t[:, spot] = part.T
        return 0

    if start_up:
        lax.fori_loop(0, users_f.shape[0] // tile, user_tile, 0, unroll=2)

    def item_tile(own, j, _):
        spot = pl.ds(pl.multiple_of(j * tile, tile), tile)
        items[:, spot] = items_f[spot].astype(BF16).T
        if own:
            old[:, spot] = items_f[spot].T
        return 0

    for r, copy in enumerate(copies):
        copy.wait()
        if epoch == 0:
            lax.fori_loop(
                r * chunk_tiles, (r + 1) * chunk_tiles, functools.partial(item_tile, r == 0), 0,
                unroll=2,
            )

    def spots(i):
        row = pl.multiple_of(slot_row[i] * tile, tile)
        place = pl.multiple_of(slot_place[i] * tile, tile)
        return pl.ds(row, tile), pl.ds(place, tile)

    def ready(j):
        for k in range(WIDE):
            i = WIDE * j + k

            @pl.when(i < total)
            def _():
                fetch(i).wait()

    def front(j):
        for k in range(WIDE):
            i = jnp.minimum(WIDE * j + k, total - 1)
            row, place = spots(i)
            predicted = jnp.dot(user_bf[row], items[:, place], preferred_element_type=F32)
            error = (predicted - held[i].astype(F32)).astype(BF16)
            errors[k][j & 1] = jnp.clip(error, -BIG, BIG)

    def back(j):
        adds = []
        for k in range(WIDE):
            valid = WIDE * j + k < total
            i = jnp.minimum(WIDE * j + k, total - 1)
            row, place = spots(i)
            weight = mask[pl.ds(slots[i], 1), :].astype(F32)
            weight = jnp.where(valid, weight, 0.0)
            error = errors[k][j & 1]
            user_add = over_rows(items[:, place], error)
            item_add = jnp.dot(
                user_t[:, row] * weight.astype(BF16), error, preferred_element_type=F32
            )
            adds.append((row, place, jnp.where(weight > 0.5, user_add, 0.0), item_add))
        return adds

    def add(adds):
        for row, place, user_add, item_add in adds:
            grad_user[:, row] += user_add
            parts[:, place] += item_add

    groups = (total + WIDE - 1) // WIDE

    @pl.when(total > 0)
    def _():
        ready(0)
        front(0)

    def step(j, _):
        ready(j + 1)
        adds = back(j)
        front(j + 1)
        add(adds)
        return 0

    lax.fori_loop(0, groups, step, 0)

    for out, columns in zip(outs, chunk_columns(members, rows, direct)):
        at = 0
        for r, start, width in columns:
            out[:, at:at + width] = parts[:, pl.ds(r * rows + start, width)].astype(BF16)
            at += width
    if start_up:
        own = jnp.dot(user_t[...], user_bf[...], preferred_element_type=F32)
        own = owned(own, users_f.shape[0], owner_ref[0, epoch])
    elif first:
        own = own_in[0][...]
    if first:
        outs[0][:, members // 2 * half:] = own


def tile_call(
    epoch, chunk, direct, members, scalars, ratings, row_mask, users, sources, carried, own
):
    tile = ratings.shape[-1]
    slots = ratings.shape[3]
    start_up = epoch == 0 and chunk == 0
    first = chunk == 0
    user_rows, rank = users[0].shape
    pieces = [columns for _, columns in sources]
    sources = [array for array, _ in sources]
    if epoch == 0:
        block_rows = sources[0].shape[0]
    else:
        block_rows = sum(s.shape[1] for s in sources) * CHUNKS
    shard_tiles = block_rows // members // tile
    rows = shard_tiles // CHUNKS * tile
    sd = jax.ShapeDtypeStruct
    widths = [sum(w for _, _, w in columns) for columns in chunk_columns(members, rows, direct)]
    widths[0] += rank if first else 0
    out_shape = [sd((rank, width), BF16) for width in widths] + [sd((rank, user_rows), F32)]
    if epoch == 0:
        out_shape += [sd((rank, members * rows), BF16), sd((rank, rows), F32)]
    if start_up:
        out_shape += [sd((user_rows, rank), BF16), sd((rank, user_rows), BF16)]
    in_specs = [HBM] * 6 + ([HBM] if start_up else [VMEM] * 2)
    in_specs += [HBM if epoch == 0 else ANY] * len(sources)
    operands = [*scalars, ratings, row_mask, *users, *sources]
    if not first:
        in_specs += [ANY]
        operands += [carried]
    elif epoch > 0:
        in_specs += [VMEM]
        operands += [own]
    scratch = [
        *[pltpu.SMEM(s.shape, jnp.int32) for s in scalars],
        pltpu.VMEM((slots, tile), jnp.int32),
        pltpu.VMEM((rank, members * rows), F32),
        pltpu.VMEM((slots, tile, tile), BF16),
        *[pltpu.SMEM((slots + 1,), jnp.int32)] * 3,
        pltpu.SemaphoreType.DMA((slots,)),
        pltpu.SemaphoreType.DMA((2 * members,)),
        pltpu.SemaphoreType.DMA((7,)),
        *[pltpu.VMEM((2, tile, tile), BF16)] * WIDE,
    ]
    if epoch == 0:
        scratch.append(pltpu.VMEM((members * rows, rank), F32))
    else:
        scratch.append(pltpu.VMEM((rank, members * rows), BF16))
    if start_up:
        scratch.append(pltpu.VMEM((user_rows, rank), F32))
    return pl.pallas_call(
        functools.partial(
            tile_kernel, epoch, chunk, direct, members, shard_tiles, tile, pieces
        ),
        out_shape=out_shape,
        in_specs=in_specs,
        out_specs=[VMEM] * len(out_shape),
        scratch_shapes=scratch,
        compiler_params=params(40),
        cost_estimate=declared(f"tiles_{epoch}_{chunk}"),
        name=f"tiles_{epoch}_{chunk}",
    )(*operands)


def user_kernel(epoch, block_rows, owner_ref, users, grad, *refs):
    outs = 4 if epoch + 1 < SUB else 1
    pieces, outs = refs[:-outs], refs[-outs:]
    gram = over_rows(pieces[0][...], pieces[0][...])
    for piece in pieces[1:]:
        gram += over_rows(piece[...], piece[...])
    full = gram * (GRAM / block_rows) + ridge(users.shape[1])
    pull = jnp.dot(users[...], full, precision=lax.Precision.HIGHEST, preferred_element_type=F32)
    new = users[...] - LEARN * (grad[...].T + pull)
    outs[0][...] = new
    if len(outs) > 1:
        plain = new.astype(BF16)
        turned = new.T.astype(BF16)
        outs[1][...] = plain
        outs[2][...] = turned
        own = jnp.dot(turned, plain, preferred_element_type=F32)
        outs[3][...] = owned(own, users.shape[0], owner_ref[0, epoch + 1])


def user_call(epoch, block_rows, owners, users, grad, pieces):
    rows, rank = users.shape
    sd = jax.ShapeDtypeStruct
    out_shape = [sd(users.shape, F32)]
    if epoch + 1 < SUB:
        out_shape += [sd((rows, rank), BF16), sd((rank, rows), BF16), sd((rank, rank), BF16)]
    return pl.pallas_call(
        functools.partial(user_kernel, epoch, block_rows),
        out_shape=out_shape,
        in_specs=[pl.BlockSpec(memory_space=pltpu.SMEM)] + [VMEM] * (2 + len(pieces)),
        out_specs=[VMEM] * len(out_shape),
        compiler_params=params(40),
        cost_estimate=declared(f"users_{epoch}"),
        name=f"users_{epoch}",
    )(owners, users, grad, *pieces)


def summed(refs, names, r, width):
    total = None
    for ref, order in zip(refs, names):
        k = order.index(r)
        term = ref[:, k * width:(k + 1) * width].astype(F32)
        total = term if total is None else total + term
    return total


def mid_kernel(paths, grams, *refs):
    at = 0
    outs = refs[sum(len(names) for names, _, _ in paths) + grams:]
    gram_refs = refs[len(refs) - len(paths) - grams:len(refs) - len(paths)]
    for (names, going, width), out in zip(paths, outs):
        terms = refs[at:at + len(names)]
        at += len(names)
        for k, r in enumerate(going):
            out[:, k * width:(k + 1) * width] = summed(terms, names, r, width).astype(BF16)
    if grams:
        rank = outs[0].shape[0]
        total = gram_refs[0][:, gram_refs[0].shape[1] - rank:].astype(F32)
        for ref in gram_refs[1:]:
            total += ref[:, ref.shape[1] - rank:].astype(F32)
        outs[0][:, outs[0].shape[1] - rank:] = total.astype(BF16)


def mid_call(epoch, chunk, step, paths, grams):
    rank = paths[0][0][0][0].shape[0]
    specs, operands, out_shape = [], [], []
    for terms, going, width in paths:
        specs.append(([names for _, names in terms], going, width))
        operands += [array for array, _ in terms]
        extra = rank if grams and not out_shape else 0
        out_shape.append(jax.ShapeDtypeStruct((rank, len(going) * width + extra), BF16))
    operands += grams
    return pl.pallas_call(
        functools.partial(mid_kernel, specs, len(grams)),
        out_shape=out_shape,
        in_specs=[VMEM] * len(operands),
        out_specs=[VMEM] * len(out_shape),
        compiler_params=params(40),
        cost_estimate=declared(f"mid_{epoch}_{chunk}_{step}"),
        name=f"mid_{epoch}_{chunk}_{step}",
    )(*operands)


def item_kernel(epoch, count, rows, width, grams, items, *refs):
    terms_a, terms_b = refs[:count], refs[count:2 * count]
    gram_refs = refs[2 * count:2 * count + grams]
    refs = refs[2 * count + grams:]
    out = refs[0]
    rank = gram_refs[0].shape[0]
    gram = gram_refs[0][:, gram_refs[0].shape[1] - rank:]
    for ref in gram_refs[1:]:
        gram = (gram.astype(F32) + ref[:, ref.shape[1] - rank:].astype(F32)).astype(BF16)
    if grams > 1:
        refs[1][...] = gram
    zero = [[0]] * count
    grad = jnp.concatenate(
        [summed(terms_a, zero, 0, width), summed(terms_b, zero, 0, rows - width)], axis=1
    )
    if epoch == 0:
        high = items[...].astype(BF16)
        low = (items[...] - high.astype(F32)).astype(BF16)
        pull = over_columns(gram, high) + over_columns(gram, low)
    else:
        pull = over_columns(gram, items[...])
    new = items[...].astype(F32) - LEARN * (grad + pull)
    if epoch + 1 < SUB:
        new = new.astype(BF16)
        out[...] = new
        refs[-2][...] = new[:, :width]
        refs[-1][...] = new[:, width:]
    else:
        out[:rows] = new.T.astype(BF16)
        if grams > 1:
            out[rows:] = gram


def item_call(epoch, chunk, shard_rows, items, terms_a, terms_b, grams):
    rank = grams[0].shape[0]
    rows = shard_rows // CHUNKS
    last = epoch + 1 == SUB
    tall = rows + (rank if len(grams) > 1 else 0)
    out_shape = [jax.ShapeDtypeStruct((tall, rank) if last else (rank, rows), BF16)]
    if len(grams) > 1:
        out_shape.append(jax.ShapeDtypeStruct((rank, rank), BF16))
    if not last:
        out_shape += [jax.ShapeDtypeStruct((rank, rows // 2), BF16)]
        out_shape += [jax.ShapeDtypeStruct((rank, rows - rows // 2), BF16)]
    out = pl.pallas_call(
        functools.partial(
            item_kernel, epoch, len(terms_a), rows, rows // 2, len(grams)
        ),
        out_shape=out_shape,
        in_specs=[VMEM] * (1 + 2 * len(terms_a) + len(grams)),
        out_specs=[VMEM] * len(out_shape),
        compiler_params=params(40),
        cost_estimate=declared(f"items_{epoch}_{chunk}"),
        name=f"items_{epoch}_{chunk}",
    )(items, *terms_a, *terms_b, *grams)
    gram = out[1] if len(grams) > 1 else None
    return out[0] if last else (out[0], *out[-2:]), gram


def swapped(value, bit):
    length = lax.axis_size("grp")
    return lax.ppermute(value, "grp", [(i, i ^ bit) for i in range(length)])


def moved(value, bit):
    length, blocks = lax.axis_size("grp"), lax.axis_size("blk")
    pairs = [
        (b * length + i, (b + 1) % blocks * length + (i ^ bit))
        for b in range(blocks)
        for i in range(length)
    ]
    return lax.ppermute(value, ("blk", "grp"), pairs)


def orders_of(members):
    bits = [1 << i for i in range(members.bit_length() - 1)]
    return bits, bits[::-1]


def exchanged(out, members):
    return [swapped(send, order[0]) for send, order in zip((out[0], out[2]), orders_of(members))]


def scattered(epoch, chunk, out, arrived, members, widths):
    send_a, keep_a, _, keep_b = out[:4]
    orders = orders_of(members)
    names = [without(members, order[0]) for order in orders]
    terms = [[(keep_a, names[0])], [(keep_b, names[1])]]
    grams = [send_a] if chunk == 0 else []
    sends = []
    for step in range(len(orders[0])):
        for p in range(2):
            terms[p].append((arrived[p], names[p]))
        if grams:
            grams.append(arrived[0])
        if step + 1 == len(orders[0]):
            break
        paths = []
        for p in range(2):
            bit = orders[p][step + 1]
            paths.append((terms[p], [r for r in names[p] if r & bit], widths[p]))
            names[p] = [r for r in names[p] if not r & bit]
        sends = mid_call(epoch, chunk, step, paths, grams)
        arrived = [swapped(sends[p], orders[p][step + 1]) for p in range(2)]
    return [a for a, _ in terms[0]], [a for a, _ in terms[1]], grams, sends


def scattered_direct(epoch, chunk, out, arrived, members, widths):
    _, keep_a, _, keep_b = out[:4]
    orders = orders_of(members)
    names = [[r for r in without(members, order[0]) if r] for order in orders]
    terms = [[(keep_a, names[0])], [(keep_b, names[1])]]
    ended = [[moved(out[4 + p], orders[p][0])] for p in range(2)]
    own = moved(out[6], 0)
    arrived = [tied(array, own) for array in arrived]
    sends = []
    for step in range(len(orders[0]) - 1):
        paths, kinds = [], []
        for p in range(2):
            terms[p].append((arrived[p], names[p]))
            bit = orders[p][step + 1]
            paths.append((terms[p], [bit], widths[p]))
            kinds.append((p, True))
            going = [r for r in names[p] if r & bit and r != bit]
            names[p] = [r for r in names[p] if not r & bit]
            if going:
                paths.append((terms[p], going, widths[p]))
                kinds.append((p, False))
        sends = mid_call(epoch, chunk, step, paths, [])
        arrived = [None, None]
        for (p, alone), send in zip(kinds, sends):
            bit = orders[p][step + 1]
            if alone:
                ended[p].append(moved(send, bit))
            else:
                arrived[p] = swapped(send, bit)
    return own, ended[0], ended[1], sends


def final_kernel(rows, width, others, count, *refs):
    done, refs = refs[:others], refs[others:]
    items, own = refs[:2]
    sides = refs[2:2 + count], refs[2 + count:2 + 2 * count]
    out, held, sem = refs[2 + 2 * count:]

    def leave(c):
        spot = pl.ds(c * rows, rows)
        return pltpu.make_async_copy(held.at[spot], out.at[spot], sem.at[c])

    for c, ref in enumerate(done):
        held[c * rows:(c + 1) * rows] = ref[:rows].astype(F32)
        leave(c).start()
    gram = done[0][rows:]
    totals = []
    for side, start, size in zip(sides, (0, width), (width, rows - width)):
        total = own[:, start:start + size].astype(F32)
        for ref in side:
            total += ref[...].astype(F32)
        totals.append(total)
    grad = jnp.concatenate(totals, axis=1)
    new = items[...].astype(F32) - LEARN * (grad + over_columns(gram, items[...]))
    held[others * rows:] = new.T
    leave(others).start()
    for c in range(others + 1):
        leave(c).wait()


def final_call(done, items, own, side_a, side_b):
    rank, rows = items.shape
    operands = [*done, items, own, *side_a, *side_b]
    return pl.pallas_call(
        functools.partial(final_kernel, rows, rows // 2, len(done), len(side_a)),
        out_shape=jax.ShapeDtypeStruct((CHUNKS * rows, rank), F32),
        in_specs=[VMEM] * len(operands),
        out_specs=HBM,
        scratch_shapes=[
            pltpu.VMEM((CHUNKS * rows, rank), F32), pltpu.SemaphoreType.DMA((CHUNKS,))
        ],
        compiler_params=params(40),
        cost_estimate=declared("items_final"),
        name="items_final",
    )(*operands)


def tied(value, *others):
    return lax.optimization_barrier((value, *others))[0]


def gathered(shard, upper, lower, after):
    length = lax.axis_size("grp")
    rows, half = shard.shape[1], upper.shape[1]
    known = {0: [moved(tied(shard, *after), 0)]}
    for bit in orders_of(length)[0]:
        known[bit] = [moved(shard, bit)]
    near = [known[bit][0] for bit in orders_of(length)[0]]

    def cut(r, p):
        pieces = known[r]
        if len(pieces) == 2:
            return pieces[p]
        return pieces[0][:, half:] if p else pieces[0][:, :half]

    for r in range(1, length):
        if r not in known:
            low, high = r & -r, 1 << (r.bit_length() - 1)
            sent = [cut(r ^ high, 0), cut(r ^ low, 1)]
            sent = [tied(piece, *after) for piece in sent]
            known[r] = [swapped(sent[0], high), swapped(sent[1], low)]
    found = []
    for r, pieces in known.items():
        spots = [(0, rows)] if len(pieces) == 1 else [(0, half), (half, rows - half)]
        found += [(piece, [(r, *spot)]) for piece, spot in zip(pieces, spots)]
    return found, near


def local(ratings, row_index, col_index, row_mask, counts, owner_list, user_factors, item_factors):
    members = lax.axis_size("grp")
    block_rows = item_factors.shape[0]
    shard_rows = block_rows // members
    rows = shard_rows // CHUNKS
    owners = owner_list.reshape(1, -1)
    row_index, col_index, counts, owner_hbm, row_mask, first_users, ratings, item_factors = (
        pltpu.with_memory_space_constraint(array, pltpu.HBM)
        for array in (
            row_index, col_index, counts.reshape(1, -1), owners, row_mask, user_factors, ratings,
            item_factors,
        )
    )
    scalars = (row_index, col_index, counts, owner_hbm)
    full_users = user_factors
    users = [first_users]
    own_gram = None
    gathers = []
    for epoch in range(SUB):
        grad_user = None
        outs, olds, pieces = [], [], []
        for c in range(CHUNKS):
            if epoch == 0:
                sources = [(item_factors, None)]
            else:
                sources = gathers[c]
                if epoch + 1 == SUB and c + 1 == CHUNKS:
                    kept = moved(tied(sources[0][0], grad_user), 0)
            direct = epoch + 1 == SUB and c + 1 == CHUNKS
            out = tile_call(
                epoch, c, direct, members, scalars, ratings, row_mask, users, sources, grad_user,
                own_gram,
            )
            grad_user = out[7 if direct else 4]
            outs.append(out)
            if epoch == 0:
                pieces.append(out[5])
                olds.append(out[6])
                if c == 0:
                    users = out[7:9]
            else:
                pieces += [array for array, _ in sources]
                olds.append(sources[0][0])
        last = epoch + 1 == SUB
        if not last:
            new_users = user_call(epoch, block_rows, owners, full_users, grad_user, pieces)
            full_users = new_users[0]
        shards = []
        grams = None
        reduced = []
        ahead = None
        for c in range(CHUNKS):
            arrived = ahead if ahead else exchanged(outs[c], members)
            arrived = [tied(array, grad_user if last else outs[-1][4]) for array in arrived]
            if last:
                if c == 0:
                    ahead = exchanged(outs[1], members)
                    arrived = [tied(array, kept) for array in arrived]
                else:
                    arrived = [tied(array, grad_user) for array in ahead]
            reduce = scattered_direct if last and c + 1 == CHUNKS else scattered
            reduced.append(
                reduce(epoch, c, outs[c], arrived, members, (rows // 2, rows - rows // 2))
            )
        for c in range(CHUNKS - 1 if last else CHUNKS):
            terms_a, terms_b, found, sent = reduced[c]
            old = olds[c]
            if not last:
                old = tied(old, *reduced[min(c + 1, CHUNKS - 1)][3])
                old = tied(old, full_users)
            shard, gram = item_call(epoch, c, shard_rows, old, terms_a, terms_b, found or grams)
            if found:
                grams = [gram]
            shards.append(shard)
        if last:
            done = [moved(shard, 0) for shard in shards]
            own, side_a, side_b, sent = reduced[-1]
            grad_user = tied(grad_user, *sent)
            item_final = final_call(done, kept, own, side_a, side_b)
            full_users = user_call(epoch, block_rows, owners, full_users, grad_user, pieces)[0]
        else:
            users, own_gram = new_users[1:3], new_users[3]
            gathers = [gathered(*shard, [shards[-1][0]]) for shard in shards]
            near = gathers[-1][1]
            gathers = [found for found, _ in gathers]
            (array, columns), *rest = gathers[0]
            gathers[0] = [(tied(array, *near), columns), *rest]
    return full_users, item_final


def solution(mesh):
    in_specs = (
        P(None, "blk", "grp", None, None, None),
        P(None, "blk", "grp", None),
        P(None, "blk", "grp", None),
        P(None, "blk", "grp", None, None),
        P(None, "blk", "grp"),
        P(None, "blk"),
        P(("blk", "grp"), None),
        P("blk", None),
    )
    out_specs = (P(("blk", "grp"), None), P(("blk", "grp"), None))
    return jax.shard_map(local, mesh=mesh, in_specs=in_specs, out_specs=out_specs, check_vma=False)
```

```python
import functools

import jax
import jax.numpy as jnp
from jax import lax
from jax.experimental import pallas as pl
from jax.experimental.pallas import tpu as pltpu
from jax.sharding import PartitionSpec as P

SUB = 2
LEARN = 0.004
GRAM = 256.0
RIDGE = 1.0
CHUNKS = 2
WIDE = 4
F32 = jnp.float32
BF16 = jnp.bfloat16
BIG = float(jnp.finfo(jnp.bfloat16).max)

ANY = pl.BlockSpec(memory_space=pl.ANY)
HBM = pl.BlockSpec(memory_space=pltpu.HBM)
VMEM = pl.BlockSpec(memory_space=pltpu.VMEM)


def params(mib):
    return pltpu.CompilerParams(vmem_limit_bytes=mib * 1024 * 1024)


def declared(name):
    costs = {"tiles": 16e9, "users": 10e9, "items": 1.2e9, "mid": 0.2e9, "mid_1_1_0": 1e9}
    flops = costs.get(name, costs[name.split("_")[0]])
    return pl.CostEstimate(flops=int(flops), bytes_accessed=1 << 16, transcendentals=0)


def over_rows(a, b):
    return lax.dot_general(a, b, (((1,), (1,)), ((), ())), preferred_element_type=F32)


def over_columns(a, b):
    return lax.dot_general(a, b, (((0,), (0,)), ((), ())), preferred_element_type=F32)


def ridge(rank):
    down = lax.broadcasted_iota(jnp.int32, (rank, rank), 0)
    across = lax.broadcasted_iota(jnp.int32, (rank, rank), 1)
    return jnp.where(down == across, RIDGE, 0.0)


def owned(gram, rows, owner):
    full = gram * (GRAM / rows) + ridge(gram.shape[0])
    return jnp.where(owner == lax.axis_index("grp"), full, 0.0).astype(BF16)


def without(members, bit):
    return [r for r in range(members) if not r & bit]


def chunk_columns(members, rows, direct):
    half = rows // 2
    found = []
    alone = []
    for bit, start, width in ((1, 0, half), (members // 2, half, rows - half)):
        names = [r for r in without(members, bit) if r or not direct]
        found.append([(r | bit, start, width) for r in names])
        found.append([(r, start, width) for r in names])
        alone.append([(bit, start, width)])
    return found + [*alone, [(0, 0, rows)]] if direct else found


def tile_kernel(epoch, chunk, direct, members, shard_tiles, tile, pieces, *refs):
    start_up = epoch == 0 and chunk == 0
    first = chunk == 0
    refs = list(refs)

    def take(n):
        out, refs[:n] = refs[:n], []
        return out

    row_hbm, col_hbm, count_hbm, owner_hbm, ratings, mask_hbm = take(6)
    users = take(1) if start_up else take(2)
    sources = take(len(pieces))
    grad_in = take(0 if first else 1)
    own_in = take(1 if first and epoch > 0 else 0)
    outs = take(7 if direct else 4)
    grad_user, = take(1)
    if epoch == 0:
        items, old = take(2)
    if start_up:
        user_bf, user_t = take(2)
    else:
        user_bf, user_t = users
    (row_ref, col_ref, count_ref, owner_ref, mask, parts, held, slots, slot_row, slot_place,
     sem_tile, sem_item, sem_small) = take(13)
    errors = take(WIDE)
    if epoch == 0:
        items_f, = take(1)
    else:
        items, = take(1)
    if start_up:
        users_f, = take(1)

    me = lax.axis_index("grp")
    chunk_tiles = shard_tiles // CHUNKS
    rows = chunk_tiles * tile
    half = rows // 2
    bits_tile = chunk_tiles.bit_length() - 1
    bits_shard = shard_tiles.bit_length() - 1

    pairs = [(row_hbm, row_ref), (col_hbm, col_ref), (count_hbm, count_ref),
             (owner_hbm, owner_ref), (mask_hbm.at[epoch, 0, 0], mask)]
    if not first:
        pairs.append((grad_in[0], grad_user))
    if start_up:
        pairs.append((users[0], users_f))
    small = [
        pltpu.make_async_copy(src, dst, sem_small.at[i]) for i, (src, dst) in enumerate(pairs)
    ]
    for copy in small:
        copy.start()
    copies = []
    if epoch == 0:
        for r in range(members):
            start = pl.multiple_of((me ^ r) * (shard_tiles * tile) + chunk * rows, rows)
            copies.append(
                pltpu.make_async_copy(
                    sources[0].at[pl.ds(start, rows)], items_f.at[pl.ds(r * rows, rows)], sem_item.at[r]
                )
            )
    else:
        for source, columns in zip(sources, pieces):
            at = 0
            for r, start, width in columns:
                copies.append(
                    pltpu.make_async_copy(
                        source.at[:, pl.ds(at, width)], items.at[:, pl.ds(r * rows + start, width)],
                        sem_item.at[len(copies)],
                    )
                )
                at += width
    for copy in copies:
        copy.start()
    for copy in small[:4]:
        copy.wait()

    count = count_ref[0, epoch]

    def pick(t, found):
        col = col_ref[epoch, 0, 0, t]
        slots[found] = t
        slot_row[found] = row_ref[epoch, 0, 0, t]
        slot_place[found] = ((col >> bits_shard) ^ me) * chunk_tiles + (col & (chunk_tiles - 1))
        here = ((col >> bits_tile) & (CHUNKS - 1)) == chunk
        return found + jnp.where(here & (t < count), 1, 0).astype(jnp.int32)

    total = lax.fori_loop(0, col_ref.shape[3], pick, jnp.int32(0), unroll=8)

    def fetch(i):
        return pltpu.make_async_copy(ratings.at[epoch, 0, 0, slots[i]], held.at[i], sem_tile.at[i])

    def begin(i, _):
        fetch(i).start()
        return 0

    lax.fori_loop(0, total, begin, 0)

    parts[...] = jnp.zeros_like(parts)
    if first:
        grad_user[...] = jnp.zeros_like(grad_user)
    for copy in small[4:]:
        copy.wait()

    def user_tile(j, _):
        spot = pl.ds(pl.multiple_of(j * tile, tile), tile)
        part = users_f[spot].astype(BF16)
        user_bf[spot] = part
        user_t[:, spot] = part.T
        return 0

    if start_up:
        lax.fori_loop(0, users_f.shape[0] // tile, user_tile, 0, unroll=2)

    def item_tile(own, j, _):
        spot = pl.ds(pl.multiple_of(j * tile, tile), tile)
        items[:, spot] = items_f[spot].astype(BF16).T
        if own:
            old[:, spot] = items_f[spot].T
        return 0

    for r, copy in enumerate(copies):
        copy.wait()
        if epoch == 0:
            lax.fori_loop(
                r * chunk_tiles, (r + 1) * chunk_tiles, functools.partial(item_tile, r == 0), 0,
                unroll=2,
            )

    def spots(i):
        row = pl.multiple_of(slot_row[i] * tile, tile)
        place = pl.multiple_of(slot_place[i] * tile, tile)
        return pl.ds(row, tile), pl.ds(place, tile)

    def ready(j):
        for k in range(WIDE):
            i = WIDE * j + k

            @pl.when(i < total)
            def _():
                fetch(i).wait()

    def front(j):
        for k in range(WIDE):
            i = jnp.minimum(WIDE * j + k, total - 1)
            row, place = spots(i)
            predicted = jnp.dot(user_bf[row], items[:, place], preferred_element_type=F32)
            error = (predicted - held[i].astype(F32)).astype(BF16)
            errors[k][j & 1] = jnp.clip(error, -BIG, BIG)

    def back(j):
        adds = []
        for k in range(WIDE):
            valid = WIDE * j + k < total
            i = jnp.minimum(WIDE * j + k, total - 1)
            row, place = spots(i)
            weight = mask[pl.ds(slots[i], 1), :].astype(F32)
            weight = jnp.where(valid, weight, 0.0)
            error = errors[k][j & 1]
            user_add = over_rows(items[:, place], error)
            item_add = jnp.dot(
                user_t[:, row] * weight.astype(BF16), error, preferred_element_type=F32
            )
            adds.append((row, place, jnp.where(weight > 0.5, user_add, 0.0), item_add))
        return adds

    def add(adds):
        for row, place, user_add, item_add in adds:
            grad_user[:, row] += user_add
            parts[:, place] += item_add

    groups = (total + WIDE - 1) // WIDE

    @pl.when(total > 0)
    def _():
        ready(0)
        front(0)

    def step(j, _):
        ready(j + 1)
        adds = back(j)
        front(j + 1)
        add(adds)
        return 0

    lax.fori_loop(0, groups, step, 0)

    for out, columns in zip(outs, chunk_columns(members, rows, direct)):
        at = 0
        for r, start, width in columns:
            out[:, at:at + width] = parts[:, pl.ds(r * rows + start, width)].astype(BF16)
            at += width
    if start_up:
        own = jnp.dot(user_t[...], user_bf[...], preferred_element_type=F32)
        own = owned(own, users_f.shape[0], owner_ref[0, epoch])
    elif first:
        own = own_in[0][...]
    if first:
        outs[0][:, members // 2 * half:] = own


def tile_call(
    epoch, chunk, direct, members, scalars, ratings, row_mask, users, sources, carried, own
):
    tile = ratings.shape[-1]
    slots = ratings.shape[3]
    start_up = epoch == 0 and chunk == 0
    first = chunk == 0
    user_rows, rank = users[0].shape
    pieces = [columns for _, columns in sources]
    sources = [array for array, _ in sources]
    if epoch == 0:
        block_rows = sources[0].shape[0]
    else:
        block_rows = sum(s.shape[1] for s in sources) * CHUNKS
    shard_tiles = block_rows // members // tile
    rows = shard_tiles // CHUNKS * tile
    sd = jax.ShapeDtypeStruct
    widths = [sum(w for _, _, w in columns) for columns in chunk_columns(members, rows, direct)]
    widths[0] += rank if first else 0
    out_shape = [sd((rank, width), BF16) for width in widths] + [sd((rank, user_rows), F32)]
    if epoch == 0:
        out_shape += [sd((rank, members * rows), BF16), sd((rank, rows), F32)]
    if start_up:
        out_shape += [sd((user_rows, rank), BF16), sd((rank, user_rows), BF16)]
    in_specs = [HBM] * 6 + ([HBM] if start_up else [VMEM] * 2)
    in_specs += [HBM if epoch == 0 else ANY] * len(sources)
    operands = [*scalars, ratings, row_mask, *users, *sources]
    if not first:
        in_specs += [ANY]
        operands += [carried]
    elif epoch > 0:
        in_specs += [VMEM]
        operands += [own]
    scratch = [
        *[pltpu.SMEM(s.shape, jnp.int32) for s in scalars],
        pltpu.VMEM((slots, tile), jnp.int32),
        pltpu.VMEM((rank, members * rows), F32),
        pltpu.VMEM((slots, tile, tile), BF16),
        *[pltpu.SMEM((slots + 1,), jnp.int32)] * 3,
        pltpu.SemaphoreType.DMA((slots,)),
        pltpu.SemaphoreType.DMA((2 * members,)),
        pltpu.SemaphoreType.DMA((7,)),
        *[pltpu.VMEM((2, tile, tile), BF16)] * WIDE,
    ]
    if epoch == 0:
        scratch.append(pltpu.VMEM((members * rows, rank), F32))
    else:
        scratch.append(pltpu.VMEM((rank, members * rows), BF16))
    if start_up:
        scratch.append(pltpu.VMEM((user_rows, rank), F32))
    return pl.pallas_call(
        functools.partial(
            tile_kernel, epoch, chunk, direct, members, shard_tiles, tile, pieces
        ),
        out_shape=out_shape,
        in_specs=in_specs,
        out_specs=[VMEM] * len(out_shape),
        scratch_shapes=scratch,
        compiler_params=params(40),
        cost_estimate=declared(f"tiles_{epoch}_{chunk}"),
        name=f"tiles_{epoch}_{chunk}",
    )(*operands)


def user_kernel(epoch, block_rows, owner_ref, users, grad, *refs):
    outs = 4 if epoch + 1 < SUB else 1
    pieces, outs = refs[:-outs], refs[-outs:]
    gram = over_rows(pieces[0][...], pieces[0][...])
    for piece in pieces[1:]:
        gram += over_rows(piece[...], piece[...])
    full = gram * (GRAM / block_rows) + ridge(users.shape[1])
    pull = jnp.dot(users[...], full, precision=lax.Precision.HIGHEST, preferred_element_type=F32)
    new = users[...] - LEARN * (grad[...].T + pull)
    outs[0][...] = new
    if len(outs) > 1:
        plain = new.astype(BF16)
        turned = new.T.astype(BF16)
        outs[1][...] = plain
        outs[2][...] = turned
        own = jnp.dot(turned, plain, preferred_element_type=F32)
        outs[3][...] = owned(own, users.shape[0], owner_ref[0, epoch + 1])


def user_call(epoch, block_rows, owners, users, grad, pieces):
    rows, rank = users.shape
    sd = jax.ShapeDtypeStruct
    out_shape = [sd(users.shape, F32)]
    if epoch + 1 < SUB:
        out_shape += [sd((rows, rank), BF16), sd((rank, rows), BF16), sd((rank, rank), BF16)]
    return pl.pallas_call(
        functools.partial(user_kernel, epoch, block_rows),
        out_shape=out_shape,
        in_specs=[pl.BlockSpec(memory_space=pltpu.SMEM)] + [VMEM] * (2 + len(pieces)),
        out_specs=[VMEM] * len(out_shape),
        compiler_params=params(40),
        cost_estimate=declared(f"users_{epoch}"),
        name=f"users_{epoch}",
    )(owners, users, grad, *pieces)


def summed(refs, names, r, width):
    total = None
    for ref, order in zip(refs, names):
        k = order.index(r)
        term = ref[:, k * width:(k + 1) * width].astype(F32)
        total = term if total is None else total + term
    return total


def mid_kernel(paths, grams, *refs):
    at = 0
    outs = refs[sum(len(names) for names, _, _ in paths) + grams:]
    gram_refs = refs[len(refs) - len(paths) - grams:len(refs) - len(paths)]
    for (names, going, width), out in zip(paths, outs):
        terms = refs[at:at + len(names)]
        at += len(names)
        for k, r in enumerate(going):
            out[:, k * width:(k + 1) * width] = summed(terms, names, r, width).astype(BF16)
    if grams:
        rank = outs[0].shape[0]
        total = gram_refs[0][:, gram_refs[0].shape[1] - rank:].astype(F32)
        for ref in gram_refs[1:]:
            total += ref[:, ref.shape[1] - rank:].astype(F32)
        outs[0][:, outs[0].shape[1] - rank:] = total.astype(BF16)


def mid_call(epoch, chunk, step, paths, grams):
    rank = paths[0][0][0][0].shape[0]
    specs, operands, out_shape = [], [], []
    for terms, going, width in paths:
        specs.append(([names for _, names in terms], going, width))
        operands += [array for array, _ in terms]
        extra = rank if grams and not out_shape else 0
        out_shape.append(jax.ShapeDtypeStruct((rank, len(going) * width + extra), BF16))
    operands += grams
    return pl.pallas_call(
        functools.partial(mid_kernel, specs, len(grams)),
        out_shape=out_shape,
        in_specs=[VMEM] * len(operands),
        out_specs=[VMEM] * len(out_shape),
        compiler_params=params(40),
        cost_estimate=declared(f"mid_{epoch}_{chunk}_{step}"),
        name=f"mid_{epoch}_{chunk}_{step}",
    )(*operands)


def item_kernel(epoch, count, rows, width, grams, items, *refs):
    terms_a, terms_b = refs[:count], refs[count:2 * count]
    gram_refs = refs[2 * count:2 * count + grams]
    refs = refs[2 * count + grams:]
    out = refs[0]
    rank = gram_refs[0].shape[0]
    gram = gram_refs[0][:, gram_refs[0].shape[1] - rank:]
    for ref in gram_refs[1:]:
        gram = (gram.astype(F32) + ref[:, ref.shape[1] - rank:].astype(F32)).astype(BF16)
    if grams > 1:
        refs[1][...] = gram
    zero = [[0]] * count
    grad = jnp.concatenate(
        [summed(terms_a, zero, 0, width), summed(terms_b, zero, 0, rows - width)], axis=1
    )
    if epoch == 0:
        high = items[...].astype(BF16)
        low = (items[...] - high.astype(F32)).astype(BF16)
        pull = over_columns(gram, high) + over_columns(gram, low)
    else:
        pull = over_columns(gram, items[...])
    new = items[...].astype(F32) - LEARN * (grad + pull)
    if epoch + 1 < SUB:
        out[...] = new.astype(BF16)
    else:
        out[:rows] = new.T.astype(BF16)
        if grams > 1:
            out[rows:] = gram


def item_call(epoch, chunk, shard_rows, items, terms_a, terms_b, grams):
    rank = grams[0].shape[0]
    rows = shard_rows // CHUNKS
    last = epoch + 1 == SUB
    tall = rows + (rank if len(grams) > 1 else 0)
    out_shape = [jax.ShapeDtypeStruct((tall, rank) if last else (rank, rows), BF16)]
    if len(grams) > 1:
        out_shape.append(jax.ShapeDtypeStruct((rank, rank), BF16))
    out = pl.pallas_call(
        functools.partial(
            item_kernel, epoch, len(terms_a), rows, rows // 2, len(grams)
        ),
        out_shape=out_shape,
        in_specs=[VMEM] * (1 + 2 * len(terms_a) + len(grams)),
        out_specs=[VMEM] * len(out_shape),
        compiler_params=params(40),
        cost_estimate=declared(f"items_{epoch}_{chunk}"),
        name=f"items_{epoch}_{chunk}",
    )(items, *terms_a, *terms_b, *grams)
    gram = out[1] if len(grams) > 1 else None
    return out[0], gram


def swapped(value, bit):
    length = lax.axis_size("grp")
    return lax.ppermute(value, "grp", [(i, i ^ bit) for i in range(length)])


def moved(value, bit):
    length, blocks = lax.axis_size("grp"), lax.axis_size("blk")
    pairs = [
        (b * length + i, (b + 1) % blocks * length + (i ^ bit))
        for b in range(blocks)
        for i in range(length)
    ]
    return lax.ppermute(value, ("blk", "grp"), pairs)


def orders_of(members):
    bits = [1 << i for i in range(members.bit_length() - 1)]
    return bits, bits[::-1]


def exchanged(out, members):
    return [swapped(send, order[0]) for send, order in zip((out[0], out[2]), orders_of(members))]


def scattered(epoch, chunk, out, arrived, members, widths):
    send_a, keep_a, _, keep_b = out[:4]
    orders = orders_of(members)
    names = [without(members, order[0]) for order in orders]
    terms = [[(keep_a, names[0])], [(keep_b, names[1])]]
    grams = [send_a] if chunk == 0 else []
    sends = []
    for step in range(len(orders[0])):
        for p in range(2):
            terms[p].append((arrived[p], names[p]))
        if grams:
            grams.append(arrived[0])
        if step + 1 == len(orders[0]):
            break
        paths = []
        for p in range(2):
            bit = orders[p][step + 1]
            paths.append((terms[p], [r for r in names[p] if r & bit], widths[p]))
            names[p] = [r for r in names[p] if not r & bit]
        sends = mid_call(epoch, chunk, step, paths, grams)
        arrived = [swapped(sends[p], orders[p][step + 1]) for p in range(2)]
    return [a for a, _ in terms[0]], [a for a, _ in terms[1]], grams, sends


def scattered_direct(epoch, chunk, out, arrived, members, widths):
    _, keep_a, _, keep_b = out[:4]
    orders = orders_of(members)
    names = [[r for r in without(members, order[0]) if r] for order in orders]
    terms = [[(keep_a, names[0])], [(keep_b, names[1])]]
    ended = [[moved(out[4 + p], orders[p][0])] for p in range(2)]
    own = moved(out[6], 0)
    arrived = [tied(array, own) for array in arrived]
    sends = []
    for step in range(len(orders[0]) - 1):
        paths, kinds = [], []
        for p in range(2):
            terms[p].append((arrived[p], names[p]))
            bit = orders[p][step + 1]
            paths.append((terms[p], [bit], widths[p]))
            kinds.append((p, True))
            going = [r for r in names[p] if r & bit and r != bit]
            names[p] = [r for r in names[p] if not r & bit]
            if going:
                paths.append((terms[p], going, widths[p]))
                kinds.append((p, False))
        sends = mid_call(epoch, chunk, step, paths, [])
        arrived = [None, None]
        for (p, alone), send in zip(kinds, sends):
            bit = orders[p][step + 1]
            if alone:
                ended[p].append(moved(send, bit))
            else:
                arrived[p] = swapped(send, bit)
    return own, ended[0], ended[1], sends


def final_kernel(rows, width, others, count, *refs):
    done, refs = refs[:others], refs[others:]
    items, own = refs[:2]
    sides = refs[2:2 + count], refs[2 + count:2 + 2 * count]
    out, held, sem = refs[2 + 2 * count:]

    def leave(c):
        spot = pl.ds(c * rows, rows)
        return pltpu.make_async_copy(held.at[spot], out.at[spot], sem.at[c])

    for c, ref in enumerate(done):
        held[c * rows:(c + 1) * rows] = ref[:rows].astype(F32)
        leave(c).start()
    gram = done[0][rows:]
    totals = []
    for side, start, size in zip(sides, (0, width), (width, rows - width)):
        total = own[:, start:start + size].astype(F32)
        for ref in side:
            total += ref[...].astype(F32)
        totals.append(total)
    grad = jnp.concatenate(totals, axis=1)
    new = items[...].astype(F32) - LEARN * (grad + over_columns(gram, items[...]))
    held[others * rows:] = new.T
    leave(others).start()
    for c in range(others + 1):
        leave(c).wait()


def final_call(done, items, own, side_a, side_b):
    rank, rows = items.shape
    operands = [*done, items, own, *side_a, *side_b]
    return pl.pallas_call(
        functools.partial(final_kernel, rows, rows // 2, len(done), len(side_a)),
        out_shape=jax.ShapeDtypeStruct((CHUNKS * rows, rank), F32),
        in_specs=[VMEM] * len(operands),
        out_specs=HBM,
        scratch_shapes=[
            pltpu.VMEM((CHUNKS * rows, rank), F32), pltpu.SemaphoreType.DMA((CHUNKS,))
        ],
        compiler_params=params(40),
        cost_estimate=declared("items_final"),
        name="items_final",
    )(*operands)


def tied(value, *others):
    return lax.optimization_barrier((value, *others))[0]


def gathered(shard, after):
    length = lax.axis_size("grp")
    rows, half = shard.shape[1], shard.shape[1] // 2
    known = {0: [moved(tied(shard, *after), 0)]}
    for bit in orders_of(length)[0]:
        known[bit] = [moved(shard, bit)]
    near = [known[bit][0] for bit in orders_of(length)[0]]

    def cut(r, p):
        pieces = known[r]
        if len(pieces) == 2:
            return pieces[p]
        return pieces[0][:, half:] if p else pieces[0][:, :half]

    for r in range(1, length):
        if r not in known:
            low, high = r & -r, 1 << (r.bit_length() - 1)
            sent = [cut(r ^ high, 0), cut(r ^ low, 1)]
            sent = [tied(piece, *after) for piece in sent]
            known[r] = [swapped(sent[0], high), swapped(sent[1], low)]
    found = []
    for r, pieces in known.items():
        spots = [(0, rows)] if len(pieces) == 1 else [(0, half), (half, rows - half)]
        found += [(piece, [(r, *spot)]) for piece, spot in zip(pieces, spots)]
    return found, near


def local(ratings, row_index, col_index, row_mask, counts, owner_list, user_factors, item_factors):
    members = lax.axis_size("grp")
    block_rows = item_factors.shape[0]
    shard_rows = block_rows // members
    rows = shard_rows // CHUNKS
    owners = owner_list.reshape(1, -1)
    row_index, col_index, counts, owner_hbm, row_mask, first_users, ratings, item_factors = (
        pltpu.with_memory_space_constraint(array, pltpu.HBM)
        for array in (
            row_index, col_index, counts.reshape(1, -1), owners, row_mask, user_factors, ratings,
            item_factors,
        )
    )
    scalars = (row_index, col_index, counts, owner_hbm)
    full_users = user_factors
    users = [first_users]
    own_gram = None
    gathers = []
    for epoch in range(SUB):
        grad_user = None
        outs, olds, pieces = [], [], []
        for c in range(CHUNKS):
            if epoch == 0:
                sources = [(item_factors, None)]
            else:
                sources = gathers[c]
            direct = epoch + 1 == SUB and c + 1 == CHUNKS
            out = tile_call(
                epoch, c, direct, members, scalars, ratings, row_mask, users, sources, grad_user,
                own_gram,
            )
            grad_user = out[7 if direct else 4]
            outs.append(out)
            if epoch == 0:
                pieces.append(out[5])
                olds.append(out[6])
                if c == 0:
                    users = out[7:9]
            else:
                pieces += [array for array, _ in sources]
                olds.append(sources[0][0])
        last = epoch + 1 == SUB
        if last:
            kept = moved(tied(olds[-1], grad_user), 0)
        if not last:
            new_users = user_call(epoch, block_rows, owners, full_users, grad_user, pieces)
            full_users = new_users[0]
        shards = []
        grams = None
        reduced = []
        ahead = None
        for c in range(CHUNKS):
            arrived = ahead if ahead else exchanged(outs[c], members)
            arrived = [tied(array, grad_user if last else outs[-1][4]) for array in arrived]
            if last:
                if c == 0:
                    ahead = exchanged(outs[1], members)
                    arrived = [tied(array, kept) for array in arrived]
                else:
                    arrived = [tied(array, grad_user) for array in ahead]
            reduce = scattered_direct if last and c + 1 == CHUNKS else scattered
            reduced.append(
                reduce(epoch, c, outs[c], arrived, members, (rows // 2, rows - rows // 2))
            )
        for c in range(CHUNKS - 1 if last else CHUNKS):
            terms_a, terms_b, found, sent = reduced[c]
            old = olds[c]
            if not last:
                old = tied(old, *reduced[min(c + 1, CHUNKS - 1)][3])
                old = tied(old, full_users)
            shard, gram = item_call(epoch, c, shard_rows, old, terms_a, terms_b, found or grams)
            if found:
                grams = [gram]
            shards.append(shard)
        if last:
            done = [moved(shard, 0) for shard in shards]
            own, side_a, side_b, sent = reduced[-1]
            grad_user = tied(grad_user, *sent)
            item_final = final_call(done, kept, own, side_a, side_b)
            full_users = user_call(epoch, block_rows, owners, full_users, grad_user, pieces)[0]
        else:
            users, own_gram = new_users[1:3], new_users[3]
            gathers = [gathered(shard, [shards[-1]]) for shard in shards]
            near = gathers[-1][1]
            gathers = [found for found, _ in gathers]
            (array, columns), *rest = gathers[0]
            gathers[0] = [(tied(array, *near), columns), *rest]
    return full_users, item_final


def solution(mesh):
    in_specs = (
        P(None, "blk", "grp", None, None, None),
        P(None, "blk", "grp", None),
        P(None, "blk", "grp", None),
        P(None, "blk", "grp", None, None),
        P(None, "blk", "grp"),
        P(None, "blk"),
        P(("blk", "grp"), None),
        P("blk", None),
    )
    out_specs = (P(("blk", "grp"), None), P(("blk", "grp"), None))
    return jax.shard_map(local, mesh=mesh, in_specs=in_specs, out_specs=out_specs, check_vma=False)
```

```python
import functools

import jax
import jax.numpy as jnp
from jax import lax
from jax.experimental import pallas as pl
from jax.experimental.pallas import tpu as pltpu
from jax.sharding import PartitionSpec as P

SUB = 2
LEARN = 0.004
GRAM = 256.0
RIDGE = 1.0
CHUNKS = 2
WIDE = 4
F32 = jnp.float32
BF16 = jnp.bfloat16
BIG = float(jnp.finfo(jnp.bfloat16).max)

ANY = pl.BlockSpec(memory_space=pl.ANY)
HBM = pl.BlockSpec(memory_space=pltpu.HBM)
VMEM = pl.BlockSpec(memory_space=pltpu.VMEM)


def params(mib):
    return pltpu.CompilerParams(vmem_limit_bytes=mib * 1024 * 1024)


def declared(name):
    costs = {"tiles": 16e9, "users": 10e9, "items": 1.2e9, "mid": 0.2e9, "mid_1_1_0": 1e9}
    flops = costs.get(name, costs[name.split("_")[0]])
    return pl.CostEstimate(flops=int(flops), bytes_accessed=1 << 16, transcendentals=0)


def over_rows(a, b):
    return lax.dot_general(a, b, (((1,), (1,)), ((), ())), preferred_element_type=F32)


def over_columns(a, b):
    return lax.dot_general(a, b, (((0,), (0,)), ((), ())), preferred_element_type=F32)


def ridge(rank):
    down = lax.broadcasted_iota(jnp.int32, (rank, rank), 0)
    across = lax.broadcasted_iota(jnp.int32, (rank, rank), 1)
    return jnp.where(down == across, RIDGE, 0.0)


def owned(gram, rows, owner):
    full = gram * (GRAM / rows) + ridge(gram.shape[0])
    return jnp.where(owner == lax.axis_index("grp"), full, 0.0).astype(BF16)


def without(members, bit):
    return [r for r in range(members) if not r & bit]


def chunk_columns(members, rows, direct):
    half = rows // 2
    found = []
    alone = []
    for bit, start, width in ((1, 0, half), (members // 2, half, rows - half)):
        names = [r for r in without(members, bit) if r or not direct]
        found.append([(r | bit, start, width) for r in names])
        found.append([(r, start, width) for r in names])
        alone.append([(bit, start, width)])
    return found + [*alone, [(0, 0, rows)]] if direct else found


def tile_kernel(epoch, chunk, direct, members, shard_tiles, tile, pieces, *refs):
    start_up = epoch == 0 and chunk == 0
    first = chunk == 0
    refs = list(refs)

    def take(n):
        out, refs[:n] = refs[:n], []
        return out

    row_hbm, col_hbm, count_hbm, owner_hbm, ratings, mask_hbm = take(6)
    users = take(1) if start_up else take(2)
    sources = take(len(pieces))
    grad_in = take(0 if first else 1)
    own_in = take(1 if first and epoch > 0 else 0)
    outs = take(7 if direct else 4)
    grad_user, = take(1)
    if epoch == 0:
        items, old = take(2)
    if start_up:
        user_bf, user_t = take(2)
    else:
        user_bf, user_t = users
    (row_ref, col_ref, count_ref, owner_ref, mask, parts, held, slots, slot_row, slot_place,
     sem_tile, sem_item, sem_small) = take(13)
    errors = take(WIDE)
    if epoch == 0:
        items_f, = take(1)
    else:
        items, = take(1)
    if start_up:
        users_f, = take(1)

    me = lax.axis_index("grp")
    chunk_tiles = shard_tiles // CHUNKS
    rows = chunk_tiles * tile
    half = rows // 2
    bits_tile = chunk_tiles.bit_length() - 1
    bits_shard = shard_tiles.bit_length() - 1

    pairs = [(row_hbm, row_ref), (col_hbm, col_ref), (count_hbm, count_ref),
             (owner_hbm, owner_ref), (mask_hbm.at[epoch, 0, 0], mask)]
    if not first:
        pairs.append((grad_in[0], grad_user))
    if start_up:
        pairs.append((users[0], users_f))
    small = [
        pltpu.make_async_copy(src, dst, sem_small.at[i]) for i, (src, dst) in enumerate(pairs)
    ]
    for copy in small:
        copy.start()
    copies = []
    if epoch == 0:
        for r in range(members):
            start = pl.multiple_of((me ^ r) * (shard_tiles * tile) + chunk * rows, rows)
            copies.append(
                pltpu.make_async_copy(
                    sources[0].at[pl.ds(start, rows)], items_f.at[pl.ds(r * rows, rows)], sem_item.at[r]
                )
            )
    else:
        for source, columns in zip(sources, pieces):
            at = 0
            for r, start, width in columns:
                copies.append(
                    pltpu.make_async_copy(
                        source.at[:, pl.ds(at, width)], items.at[:, pl.ds(r * rows + start, width)],
                        sem_item.at[len(copies)],
                    )
                )
                at += width
    for copy in copies:
        copy.start()
    for copy in small[:4]:
        copy.wait()

    count = count_ref[0, epoch]

    def pick(t, found):
        col = col_ref[epoch, 0, 0, t]
        slots[found] = t
        slot_row[found] = row_ref[epoch, 0, 0, t]
        slot_place[found] = ((col >> bits_shard) ^ me) * chunk_tiles + (col & (chunk_tiles - 1))
        here = ((col >> bits_tile) & (CHUNKS - 1)) == chunk
        return found + jnp.where(here & (t < count), 1, 0).astype(jnp.int32)

    total = lax.fori_loop(0, col_ref.shape[3], pick, jnp.int32(0), unroll=8)

    def fetch(i):
        return pltpu.make_async_copy(ratings.at[epoch, 0, 0, slots[i]], held.at[i], sem_tile.at[i])

    def begin(i, _):
        fetch(i).start()
        return 0

    lax.fori_loop(0, total, begin, 0)

    parts[...] = jnp.zeros_like(parts)
    if first:
        grad_user[...] = jnp.zeros_like(grad_user)
    for copy in small[4:]:
        copy.wait()

    def user_tile(j, _):
        spot = pl.ds(pl.multiple_of(j * tile, tile), tile)
        part = users_f[spot].astype(BF16)
        user_bf[spot] = part
        user_t[:, spot] = part.T
        return 0

    if start_up:
        lax.fori_loop(0, users_f.shape[0] // tile, user_tile, 0, unroll=2)

    def item_tile(own, j, _):
        spot = pl.ds(pl.multiple_of(j * tile, tile), tile)
        items[:, spot] = items_f[spot].astype(BF16).T
        if own:
            old[:, spot] = items_f[spot].T
        return 0

    for r, copy in enumerate(copies):
        copy.wait()
        if epoch == 0:
            lax.fori_loop(
                r * chunk_tiles, (r + 1) * chunk_tiles, functools.partial(item_tile, r == 0), 0,
                unroll=2,
            )

    def spots(i):
        row = pl.multiple_of(slot_row[i] * tile, tile)
        place = pl.multiple_of(slot_place[i] * tile, tile)
        return pl.ds(row, tile), pl.ds(place, tile)

    def ready(j):
        for k in range(WIDE):
            i = WIDE * j + k

            @pl.when(i < total)
            def _():
                fetch(i).wait()

    def front(j):
        for k in range(WIDE):
            i = jnp.minimum(WIDE * j + k, total - 1)
            row, place = spots(i)
            predicted = jnp.dot(user_bf[row], items[:, place], preferred_element_type=F32)
            error = (predicted - held[i].astype(F32)).astype(BF16)
            errors[k][j & 1] = jnp.clip(error, -BIG, BIG)

    def back(j):
        adds = []
        for k in range(WIDE):
            valid = WIDE * j + k < total
            i = jnp.minimum(WIDE * j + k, total - 1)
            row, place = spots(i)
            weight = mask[pl.ds(slots[i], 1), :].astype(F32)
            weight = jnp.where(valid, weight, 0.0)
            error = errors[k][j & 1]
            user_add = over_rows(items[:, place], error)
            item_add = jnp.dot(
                user_t[:, row] * weight.astype(BF16), error, preferred_element_type=F32
            )
            adds.append((row, place, jnp.where(weight > 0.5, user_add, 0.0), item_add))
        return adds

    def add(adds):
        for row, place, user_add, item_add in adds:
            grad_user[:, row] += user_add
            parts[:, place] += item_add

    groups = (total + WIDE - 1) // WIDE

    @pl.when(total > 0)
    def _():
        ready(0)
        front(0)

    def step(j, _):
        ready(j + 1)
        adds = back(j)
        front(j + 1)
        add(adds)
        return 0

    lax.fori_loop(0, groups, step, 0)

    for out, columns in zip(outs, chunk_columns(members, rows, direct)):
        at = 0
        for r, start, width in columns:
            out[:, at:at + width] = parts[:, pl.ds(r * rows + start, width)].astype(BF16)
            at += width
    if start_up:
        own = jnp.dot(user_t[...], user_bf[...], preferred_element_type=F32)
        own = owned(own, users_f.shape[0], owner_ref[0, epoch])
    elif first:
        own = own_in[0][...]
    if first:
        outs[0][:, members // 2 * half:] = own


def tile_call(
    epoch, chunk, direct, members, scalars, ratings, row_mask, users, sources, carried, own
):
    tile = ratings.shape[-1]
    slots = ratings.shape[3]
    start_up = epoch == 0 and chunk == 0
    first = chunk == 0
    user_rows, rank = users[0].shape
    pieces = [columns for _, columns in sources]
    sources = [array for array, _ in sources]
    if epoch == 0:
        block_rows = sources[0].shape[0]
    else:
        block_rows = sum(s.shape[1] for s in sources) * CHUNKS
    shard_tiles = block_rows // members // tile
    rows = shard_tiles // CHUNKS * tile
    sd = jax.ShapeDtypeStruct
    widths = [sum(w for _, _, w in columns) for columns in chunk_columns(members, rows, direct)]
    widths[0] += rank if first else 0
    out_shape = [sd((rank, width), BF16) for width in widths] + [sd((rank, user_rows), F32)]
    if epoch == 0:
        out_shape += [sd((rank, members * rows), BF16), sd((rank, rows), F32)]
    if start_up:
        out_shape += [sd((user_rows, rank), BF16), sd((rank, user_rows), BF16)]
    in_specs = [HBM] * 6 + ([HBM] if start_up else [VMEM] * 2)
    in_specs += [HBM if epoch == 0 else ANY] * len(sources)
    operands = [*scalars, ratings, row_mask, *users, *sources]
    if not first:
        in_specs += [ANY]
        operands += [carried]
    elif epoch > 0:
        in_specs += [VMEM]
        operands += [own]
    scratch = [
        *[pltpu.SMEM(s.shape, jnp.int32) for s in scalars],
        pltpu.VMEM((slots, tile), jnp.int32),
        pltpu.VMEM((rank, members * rows), F32),
        pltpu.VMEM((slots, tile, tile), BF16),
        *[pltpu.SMEM((slots + 1,), jnp.int32)] * 3,
        pltpu.SemaphoreType.DMA((slots,)),
        pltpu.SemaphoreType.DMA((2 * members,)),
        pltpu.SemaphoreType.DMA((7,)),
        *[pltpu.VMEM((2, tile, tile), BF16)] * WIDE,
    ]
    if epoch == 0:
        scratch.append(pltpu.VMEM((members * rows, rank), F32))
    else:
        scratch.append(pltpu.VMEM((rank, members * rows), BF16))
    if start_up:
        scratch.append(pltpu.VMEM((user_rows, rank), F32))
    return pl.pallas_call(
        functools.partial(
            tile_kernel, epoch, chunk, direct, members, shard_tiles, tile, pieces
        ),
        out_shape=out_shape,
        in_specs=in_specs,
        out_specs=[VMEM] * len(out_shape),
        scratch_shapes=scratch,
        compiler_params=params(40),
        cost_estimate=declared(f"tiles_{epoch}_{chunk}"),
        name=f"tiles_{epoch}_{chunk}",
    )(*operands)


def user_kernel(epoch, block_rows, owner_ref, users, grad, *refs):
    outs = 4 if epoch + 1 < SUB else 1
    pieces, outs = refs[:-outs], refs[-outs:]
    gram = over_rows(pieces[0][...], pieces[0][...])
    for piece in pieces[1:]:
        gram += over_rows(piece[...], piece[...])
    full = gram * (GRAM / block_rows) + ridge(users.shape[1])
    pull = jnp.dot(users[...], full, precision=lax.Precision.HIGHEST, preferred_element_type=F32)
    new = users[...] - LEARN * (grad[...].T + pull)
    outs[0][...] = new
    if len(outs) > 1:
        plain = new.astype(BF16)
        turned = new.T.astype(BF16)
        outs[1][...] = plain
        outs[2][...] = turned
        own = jnp.dot(turned, plain, preferred_element_type=F32)
        outs[3][...] = owned(own, users.shape[0], owner_ref[0, epoch + 1])


def user_call(epoch, block_rows, owners, users, grad, pieces):
    rows, rank = users.shape
    sd = jax.ShapeDtypeStruct
    out_shape = [sd(users.shape, F32)]
    if epoch + 1 < SUB:
        out_shape += [sd((rows, rank), BF16), sd((rank, rows), BF16), sd((rank, rank), BF16)]
    return pl.pallas_call(
        functools.partial(user_kernel, epoch, block_rows),
        out_shape=out_shape,
        in_specs=[pl.BlockSpec(memory_space=pltpu.SMEM)] + [VMEM] * (2 + len(pieces)),
        out_specs=[VMEM] * len(out_shape),
        compiler_params=params(40),
        cost_estimate=declared(f"users_{epoch}"),
        name=f"users_{epoch}",
    )(owners, users, grad, *pieces)


def summed(refs, names, r, width):
    total = None
    for ref, order in zip(refs, names):
        k = order.index(r)
        term = ref[:, k * width:(k + 1) * width].astype(F32)
        total = term if total is None else total + term
    return total


def mid_kernel(paths, grams, *refs):
    at = 0
    outs = refs[sum(len(names) for names, _, _ in paths) + grams:]
    gram_refs = refs[len(refs) - len(paths) - grams:len(refs) - len(paths)]
    for (names, going, width), out in zip(paths, outs):
        terms = refs[at:at + len(names)]
        at += len(names)
        for k, r in enumerate(going):
            out[:, k * width:(k + 1) * width] = summed(terms, names, r, width).astype(BF16)
    if grams:
        rank = outs[0].shape[0]
        total = gram_refs[0][:, gram_refs[0].shape[1] - rank:].astype(F32)
        for ref in gram_refs[1:]:
            total += ref[:, ref.shape[1] - rank:].astype(F32)
        outs[0][:, outs[0].shape[1] - rank:] = total.astype(BF16)


def mid_call(epoch, chunk, step, paths, grams):
    rank = paths[0][0][0][0].shape[0]
    specs, operands, out_shape = [], [], []
    for terms, going, width in paths:
        specs.append(([names for _, names in terms], going, width))
        operands += [array for array, _ in terms]
        extra = rank if grams and not out_shape else 0
        out_shape.append(jax.ShapeDtypeStruct((rank, len(going) * width + extra), BF16))
    operands += grams
    return pl.pallas_call(
        functools.partial(mid_kernel, specs, len(grams)),
        out_shape=out_shape,
        in_specs=[VMEM] * len(operands),
        out_specs=[VMEM] * len(out_shape),
        compiler_params=params(40),
        cost_estimate=declared(f"mid_{epoch}_{chunk}_{step}"),
        name=f"mid_{epoch}_{chunk}_{step}",
    )(*operands)


def item_kernel(epoch, count, rows, width, grams, items, *refs):
    terms_a, terms_b = refs[:count], refs[count:2 * count]
    gram_refs = refs[2 * count:2 * count + grams]
    refs = refs[2 * count + grams:]
    out = refs[0]
    rank = gram_refs[0].shape[0]
    gram = gram_refs[0][:, gram_refs[0].shape[1] - rank:]
    for ref in gram_refs[1:]:
        gram = (gram.astype(F32) + ref[:, ref.shape[1] - rank:].astype(F32)).astype(BF16)
    if grams > 1:
        refs[1][...] = gram
    zero = [[0]] * count
    grad = jnp.concatenate(
        [summed(terms_a, zero, 0, width), summed(terms_b, zero, 0, rows - width)], axis=1
    )
    if epoch == 0:
        high = items[...].astype(BF16)
        low = (items[...] - high.astype(F32)).astype(BF16)
        pull = over_columns(gram, high) + over_columns(gram, low)
    else:
        pull = over_columns(gram, items[...])
    new = items[...].astype(F32) - LEARN * (grad + pull)
    if epoch + 1 < SUB:
        out[...] = new.astype(BF16)
    else:
        out[:rows] = new.T.astype(BF16)
        if grams > 1:
            out[rows:] = gram


def item_call(epoch, chunk, shard_rows, items, terms_a, terms_b, grams):
    rank = grams[0].shape[0]
    rows = shard_rows // CHUNKS
    last = epoch + 1 == SUB
    tall = rows + (rank if len(grams) > 1 else 0)
    out_shape = [jax.ShapeDtypeStruct((tall, rank) if last else (rank, rows), BF16)]
    if len(grams) > 1:
        out_shape.append(jax.ShapeDtypeStruct((rank, rank), BF16))
    out = pl.pallas_call(
        functools.partial(
            item_kernel, epoch, len(terms_a), rows, rows // 2, len(grams)
        ),
        out_shape=out_shape,
        in_specs=[VMEM] * (1 + 2 * len(terms_a) + len(grams)),
        out_specs=[VMEM] * len(out_shape),
        compiler_params=params(40),
        cost_estimate=declared(f"items_{epoch}_{chunk}"),
        name=f"items_{epoch}_{chunk}",
    )(items, *terms_a, *terms_b, *grams)
    gram = out[1] if len(grams) > 1 else None
    return out[0], gram


def swapped(value, bit):
    length = lax.axis_size("grp")
    return lax.ppermute(value, "grp", [(i, i ^ bit) for i in range(length)])


def moved(value, bit, by=1):
    length, blocks = lax.axis_size("grp"), lax.axis_size("blk")
    pairs = [
        (b * length + i, (b + by) % blocks * length + (i ^ bit))
        for b in range(blocks)
        for i in range(length)
    ]
    return lax.ppermute(value, ("blk", "grp"), pairs)


def orders_of(members):
    bits = [1 << i for i in range(members.bit_length() - 1)]
    return bits, bits[::-1]


def exchanged(out, members):
    return [swapped(send, order[0]) for send, order in zip((out[0], out[2]), orders_of(members))]


def scattered(epoch, chunk, out, arrived, members, widths):
    send_a, keep_a, _, keep_b = out[:4]
    orders = orders_of(members)
    names = [without(members, order[0]) for order in orders]
    terms = [[(keep_a, names[0])], [(keep_b, names[1])]]
    grams = [send_a] if chunk == 0 else []
    sends = []
    for step in range(len(orders[0])):
        for p in range(2):
            terms[p].append((arrived[p], names[p]))
        if grams:
            grams.append(arrived[0])
        if step + 1 == len(orders[0]):
            break
        paths = []
        for p in range(2):
            bit = orders[p][step + 1]
            paths.append((terms[p], [r for r in names[p] if r & bit], widths[p]))
            names[p] = [r for r in names[p] if not r & bit]
        sends = mid_call(epoch, chunk, step, paths, grams)
        arrived = [swapped(sends[p], orders[p][step + 1]) for p in range(2)]
    return [a for a, _ in terms[0]], [a for a, _ in terms[1]], grams, sends


def scattered_direct(epoch, chunk, out, arrived, members, widths):
    _, keep_a, _, keep_b = out[:4]
    orders = orders_of(members)
    names = [[r for r in without(members, order[0]) if r] for order in orders]
    terms = [[(keep_a, names[0])], [(keep_b, names[1])]]
    ended = [[moved(out[4 + p], orders[p][0])] for p in range(2)]
    own = moved(out[6], 0)
    arrived = [tied(array, own) for array in arrived]
    sends = []
    for step in range(len(orders[0]) - 1):
        paths, kinds = [], []
        for p in range(2):
            terms[p].append((arrived[p], names[p]))
            bit = orders[p][step + 1]
            paths.append((terms[p], [bit], widths[p]))
            kinds.append((p, True))
            going = [r for r in names[p] if r & bit and r != bit]
            names[p] = [r for r in names[p] if not r & bit]
            if going:
                paths.append((terms[p], going, widths[p]))
                kinds.append((p, False))
        sends = mid_call(epoch, chunk, step, paths, [])
        arrived = [None, None]
        for (p, alone), send in zip(kinds, sends):
            bit = orders[p][step + 1]
            if alone:
                ended[p].append(moved(send, bit))
            else:
                arrived[p] = swapped(send, bit)
    return own, ended[0], ended[1], sends


def final_kernel(rows, width, others, count, *refs):
    done, refs = refs[:others], refs[others:]
    items, own = refs[:2]
    sides = refs[2:2 + count], refs[2 + count:2 + 2 * count]
    out, held, sem = refs[2 + 2 * count:]

    def leave(c):
        spot = pl.ds(c * rows, rows)
        return pltpu.make_async_copy(held.at[spot], out.at[spot], sem.at[c])

    for c, ref in enumerate(done):
        held[c * rows:(c + 1) * rows] = ref[:rows].astype(F32)
        leave(c).start()
    gram = done[0][rows:]
    totals = []
    for side, start, size in zip(sides, (0, width), (width, rows - width)):
        total = own[:, start:start + size].astype(F32)
        for ref in side:
            total += ref[...].astype(F32)
        totals.append(total)
    grad = jnp.concatenate(totals, axis=1)
    new = items[...].astype(F32) - LEARN * (grad + over_columns(gram, items[...]))
    held[others * rows:] = new.T
    leave(others).start()
    for c in range(others + 1):
        leave(c).wait()


def final_call(done, items, own, side_a, side_b):
    rank, rows = items.shape
    operands = [*done, items, own, *side_a, *side_b]
    return pl.pallas_call(
        functools.partial(final_kernel, rows, rows // 2, len(done), len(side_a)),
        out_shape=jax.ShapeDtypeStruct((CHUNKS * rows, rank), F32),
        in_specs=[VMEM] * len(operands),
        out_specs=HBM,
        scratch_shapes=[
            pltpu.VMEM((CHUNKS * rows, rank), F32), pltpu.SemaphoreType.DMA((CHUNKS,))
        ],
        compiler_params=params(40),
        cost_estimate=declared("items_final"),
        name="items_final",
    )(*operands)


def tied(value, *others):
    return lax.optimization_barrier((value, *others))[0]


def gathered(shard, after):
    length = lax.axis_size("grp")
    rows, half = shard.shape[1], shard.shape[1] // 2
    known = {0: [moved(tied(shard, *after), 0)]}
    for bit in orders_of(length)[0]:
        known[bit] = [moved(shard, bit)]
    near = [known[bit][0] for bit in orders_of(length)[0]]

    def cut(r, p):
        pieces = known[r]
        if len(pieces) == 2:
            return pieces[p]
        return pieces[0][:, half:] if p else pieces[0][:, :half]

    for r in range(1, length):
        if r not in known:
            low, high = r & -r, 1 << (r.bit_length() - 1)
            sent = [cut(r ^ high, 0), cut(r ^ low, 1)]
            sent = [tied(piece, *after) for piece in sent]
            known[r] = [swapped(sent[0], high), swapped(sent[1], low)]
    found = []
    for r, pieces in known.items():
        spots = [(0, rows)] if len(pieces) == 1 else [(0, half), (half, rows - half)]
        found += [(piece, [(r, *spot)]) for piece, spot in zip(pieces, spots)]
    return found, near


def local(ratings, row_index, col_index, row_mask, counts, owner_list, user_factors, item_factors):
    members = lax.axis_size("grp")
    block_rows = item_factors.shape[0]
    shard_rows = block_rows // members
    rows = shard_rows // CHUNKS
    owners = owner_list.reshape(1, -1)
    row_index, col_index, counts, owner_hbm, row_mask, first_users, ratings, item_factors = (
        pltpu.with_memory_space_constraint(array, pltpu.HBM)
        for array in (
            row_index, col_index, counts.reshape(1, -1), owners, row_mask, user_factors, ratings,
            item_factors,
        )
    )
    scalars = (row_index, col_index, counts, owner_hbm)
    full_users = user_factors
    users = [first_users]
    own_gram = None
    gathers = []
    for epoch in range(SUB):
        grad_user = None
        outs, olds, pieces = [], [], []
        for c in range(CHUNKS):
            if epoch == 0:
                sources = [(item_factors, None)]
            else:
                sources = gathers[c]
            direct = epoch + 1 == SUB and c + 1 == CHUNKS
            out = tile_call(
                epoch, c, direct, members, scalars, ratings, row_mask, users, sources, grad_user,
                own_gram,
            )
            grad_user = out[7 if direct else 4]
            outs.append(out)
            if epoch == 0:
                pieces.append(out[5])
                olds.append(out[6])
                if c == 0:
                    users = out[7:9]
            else:
                pieces += [array for array, _ in sources]
                olds.append(sources[0][0])
        last = epoch + 1 == SUB
        if not last:
            new_users = user_call(epoch, block_rows, owners, full_users, grad_user, pieces)
            full_users = new_users[0]
        shards = []
        grams = None
        reduced = []
        ahead = None
        for c in range(CHUNKS):
            arrived = ahead if ahead else exchanged(outs[c], members)
            arrived = [tied(array, grad_user if last else outs[-1][4]) for array in arrived]
            if last:
                if c == 0:
                    ahead = exchanged(outs[1], members)
                    arrived = [tied(array, kept) for array in arrived]
                else:
                    arrived = [tied(array, grad_user) for array in ahead]
            reduce = scattered_direct if last and c + 1 == CHUNKS else scattered
            reduced.append(
                reduce(epoch, c, outs[c], arrived, members, (rows // 2, rows - rows // 2))
            )
        for c in range(CHUNKS - 1 if last else CHUNKS):
            terms_a, terms_b, found, sent = reduced[c]
            old = olds[c]
            if not last:
                old = tied(old, *reduced[min(c + 1, CHUNKS - 1)][3])
                old = tied(old, full_users)
            shard, gram = item_call(epoch, c, shard_rows, old, terms_a, terms_b, found or grams)
            if found:
                grams = [gram]
            shards.append(shard)
        if last:
            done = [moved(shard, 0) for shard in shards]
            own, side_a, side_b, sent = reduced[-1]
            grad_user = tied(grad_user, *sent)
            item_final = final_call(done, kept, own, side_a, side_b)
            full_users = user_call(epoch, block_rows, owners, full_users, grad_user, pieces)[0]
        else:
            users, own_gram = new_users[1:3], new_users[3]
            gathers = [gathered(shard, [shards[-1]]) for shard in shards]
            near = gathers[-1][1]
            kept = moved(tied(shards[-1], *near), 0, 2)
            gathers = [found for found, _ in gathers]
            (array, columns), *rest = gathers[0]
            gathers[0] = [(tied(array, *near), columns), *rest]
    return full_users, item_final


def solution(mesh):
    in_specs = (
        P(None, "blk", "grp", None, None, None),
        P(None, "blk", "grp", None),
        P(None, "blk", "grp", None),
        P(None, "blk", "grp", None, None),
        P(None, "blk", "grp"),
        P(None, "blk"),
        P(("blk", "grp"), None),
        P("blk", None),
    )
    out_specs = (P(("blk", "grp"), None), P(("blk", "grp"), None))
    return jax.shard_map(local, mesh=mesh, in_specs=in_specs, out_specs=out_specs, check_vma=False)
```

```python
import functools

import jax
import jax.numpy as jnp
from jax import lax
from jax.experimental import pallas as pl
from jax.experimental.pallas import tpu as pltpu
from jax.sharding import PartitionSpec as P

SUB = 2
LEARN = 0.004
GRAM = 256.0
RIDGE = 1.0
CHUNKS = 2
WIDE = 4
F32 = jnp.float32
BF16 = jnp.bfloat16
BIG = float(jnp.finfo(jnp.bfloat16).max)

ANY = pl.BlockSpec(memory_space=pl.ANY)
HBM = pl.BlockSpec(memory_space=pltpu.HBM)
VMEM = pl.BlockSpec(memory_space=pltpu.VMEM)


def params(mib):
    return pltpu.CompilerParams(vmem_limit_bytes=mib * 1024 * 1024)


def declared(name):
    costs = {"tiles": 16e9, "users": 10e9, "items": 1.2e9, "mid": 0.2e9, "mid_1_1_0": 1e9}
    flops = costs.get(name, costs[name.split("_")[0]])
    return pl.CostEstimate(flops=int(flops), bytes_accessed=1 << 16, transcendentals=0)


def over_rows(a, b):
    return lax.dot_general(a, b, (((1,), (1,)), ((), ())), preferred_element_type=F32)


def over_columns(a, b):
    return lax.dot_general(a, b, (((0,), (0,)), ((), ())), preferred_element_type=F32)


def ridge(rank):
    down = lax.broadcasted_iota(jnp.int32, (rank, rank), 0)
    across = lax.broadcasted_iota(jnp.int32, (rank, rank), 1)
    return jnp.where(down == across, RIDGE, 0.0)


def owned(gram, rows, owner):
    full = gram * (GRAM / rows) + ridge(gram.shape[0])
    return jnp.where(owner == lax.axis_index("grp"), full, 0.0).astype(BF16)


def without(members, bit):
    return [r for r in range(members) if not r & bit]


def chunk_columns(members, rows, direct):
    half = rows // 2
    found = []
    alone = []
    for bit, start, width in ((1, 0, half), (members // 2, half, rows - half)):
        names = [r for r in without(members, bit) if r or not direct]
        found.append([(r | bit, start, width) for r in names])
        found.append([(r, start, width) for r in names])
        alone.append([(bit, start, width)])
    return found + [*alone, [(0, 0, rows)]] if direct else found


def tile_kernel(epoch, chunk, direct, members, shard_tiles, tile, pieces, *refs):
    start_up = epoch == 0 and chunk == 0
    first = chunk == 0
    refs = list(refs)

    def take(n):
        out, refs[:n] = refs[:n], []
        return out

    row_hbm, col_hbm, count_hbm, owner_hbm, ratings, mask_hbm = take(6)
    users = take(1) if start_up else take(2)
    sources = take(len(pieces))
    grad_in = take(0 if first else 1)
    own_in = take(1 if first and epoch > 0 else 0)
    outs = take(7 if direct else 4)
    grad_user, = take(1)
    if epoch == 0:
        items, old = take(2)
    if start_up:
        user_bf, user_t = take(2)
    else:
        user_bf, user_t = users
    (row_ref, col_ref, count_ref, owner_ref, mask, parts, held, slots, slot_row, slot_place,
     sem_tile, sem_item, sem_small) = take(13)
    errors = take(WIDE)
    if epoch == 0:
        items_f, = take(1)
    else:
        items, = take(1)
    if start_up:
        users_f, = take(1)

    me = lax.axis_index("grp")
    chunk_tiles = shard_tiles // CHUNKS
    rows = chunk_tiles * tile
    half = rows // 2
    bits_tile = chunk_tiles.bit_length() - 1
    bits_shard = shard_tiles.bit_length() - 1

    pairs = [(row_hbm, row_ref), (col_hbm, col_ref), (count_hbm, count_ref),
             (owner_hbm, owner_ref), (mask_hbm.at[epoch, 0, 0], mask)]
    if not first:
        pairs.append((grad_in[0], grad_user))
    if start_up:
        pairs.append((users[0], users_f))
    small = [
        pltpu.make_async_copy(src, dst, sem_small.at[i]) for i, (src, dst) in enumerate(pairs)
    ]
    for copy in small:
        copy.start()
    copies = []
    if epoch == 0:
        for r in range(members):
            start = pl.multiple_of((me ^ r) * (shard_tiles * tile) + chunk * rows, rows)
            copies.append(
                pltpu.make_async_copy(
                    sources[0].at[pl.ds(start, rows)], items_f.at[pl.ds(r * rows, rows)], sem_item.at[r]
                )
            )
    else:
        for source, columns in zip(sources, pieces):
            at = 0
            for r, start, width in columns:
                copies.append(
                    pltpu.make_async_copy(
                        source.at[:, pl.ds(at, width)], items.at[:, pl.ds(r * rows + start, width)],
                        sem_item.at[len(copies)],
                    )
                )
                at += width
    for copy in copies:
        copy.start()
    for copy in small[:4]:
        copy.wait()

    count = count_ref[0, epoch]

    def pick(t, found):
        col = col_ref[epoch, 0, 0, t]
        slots[found] = t
        slot_row[found] = row_ref[epoch, 0, 0, t]
        slot_place[found] = ((col >> bits_shard) ^ me) * chunk_tiles + (col & (chunk_tiles - 1))
        here = ((col >> bits_tile) & (CHUNKS - 1)) == chunk
        return found + jnp.where(here & (t < count), 1, 0).astype(jnp.int32)

    total = lax.fori_loop(0, col_ref.shape[3], pick, jnp.int32(0), unroll=8)

    def fetch(i):
        return pltpu.make_async_copy(ratings.at[epoch, 0, 0, slots[i]], held.at[i], sem_tile.at[i])

    def begin(i, _):
        fetch(i).start()
        return 0

    lax.fori_loop(0, total, begin, 0)

    parts[...] = jnp.zeros_like(parts)
    if first:
        grad_user[...] = jnp.zeros_like(grad_user)
    for copy in small[4:]:
        copy.wait()

    def user_tile(j, _):
        spot = pl.ds(pl.multiple_of(j * tile, tile), tile)
        part = users_f[spot].astype(BF16)
        user_bf[spot] = part
        user_t[:, spot] = part.T
        return 0

    if start_up:
        lax.fori_loop(0, users_f.shape[0] // tile, user_tile, 0, unroll=2)

    def item_tile(own, j, _):
        spot = pl.ds(pl.multiple_of(j * tile, tile), tile)
        items[:, spot] = items_f[spot].astype(BF16).T
        if own:
            old[:, spot] = items_f[spot].T
        return 0

    for r, copy in enumerate(copies):
        copy.wait()
        if epoch == 0:
            lax.fori_loop(
                r * chunk_tiles, (r + 1) * chunk_tiles, functools.partial(item_tile, r == 0), 0,
                unroll=2,
            )

    def spots(i):
        row = pl.multiple_of(slot_row[i] * tile, tile)
        place = pl.multiple_of(slot_place[i] * tile, tile)
        return pl.ds(row, tile), pl.ds(place, tile)

    def ready(j):
        for k in range(WIDE):
            i = WIDE * j + k

            @pl.when(i < total)
            def _():
                fetch(i).wait()

    def front(j):
        for k in range(WIDE):
            i = jnp.minimum(WIDE * j + k, total - 1)
            row, place = spots(i)
            predicted = jnp.dot(user_bf[row], items[:, place], preferred_element_type=F32)
            error = (predicted - held[i].astype(F32)).astype(BF16)
            errors[k][j & 1] = jnp.clip(error, -BIG, BIG)

    def back(j):
        adds = []
        for k in range(WIDE):
            valid = WIDE * j + k < total
            i = jnp.minimum(WIDE * j + k, total - 1)
            row, place = spots(i)
            weight = mask[pl.ds(slots[i], 1), :].astype(F32)
            weight = jnp.where(valid, weight, 0.0)
            error = errors[k][j & 1]
            user_add = over_rows(items[:, place], error)
            item_add = jnp.dot(
                user_t[:, row] * weight.astype(BF16), error, preferred_element_type=F32
            )
            adds.append((row, place, jnp.where(weight > 0.5, user_add, 0.0), item_add))
        return adds

    def add(adds):
        for row, place, user_add, item_add in adds:
            grad_user[:, row] += user_add
            parts[:, place] += item_add

    groups = (total + WIDE - 1) // WIDE

    @pl.when(total > 0)
    def _():
        ready(0)
        front(0)

    def step(j, _):
        ready(j + 1)
        adds = back(j)
        front(j + 1)
        add(adds)
        return 0

    lax.fori_loop(0, groups, step, 0)

    for out, columns in zip(outs, chunk_columns(members, rows, direct)):
        at = 0
        for r, start, width in columns:
            out[:, at:at + width] = parts[:, pl.ds(r * rows + start, width)].astype(BF16)
            at += width
    if start_up:
        own = jnp.dot(user_t[...], user_bf[...], preferred_element_type=F32)
        own = owned(own, users_f.shape[0], owner_ref[0, epoch])
    elif first:
        own = own_in[0][...]
    if first:
        outs[0][:, members // 2 * half:] = own


def tile_call(
    epoch, chunk, direct, members, scalars, ratings, row_mask, users, sources, carried, own
):
    tile = ratings.shape[-1]
    slots = ratings.shape[3]
    start_up = epoch == 0 and chunk == 0
    first = chunk == 0
    user_rows, rank = users[0].shape
    pieces = [columns for _, columns in sources]
    sources = [array for array, _ in sources]
    if epoch == 0:
        block_rows = sources[0].shape[0]
    else:
        block_rows = sum(s.shape[1] for s in sources) * CHUNKS
    shard_tiles = block_rows // members // tile
    rows = shard_tiles // CHUNKS * tile
    sd = jax.ShapeDtypeStruct
    widths = [sum(w for _, _, w in columns) for columns in chunk_columns(members, rows, direct)]
    widths[0] += rank if first else 0
    out_shape = [sd((rank, width), BF16) for width in widths] + [sd((rank, user_rows), F32)]
    if epoch == 0:
        out_shape += [sd((rank, members * rows), BF16), sd((rank, rows), F32)]
    if start_up:
        out_shape += [sd((user_rows, rank), BF16), sd((rank, user_rows), BF16)]
    in_specs = [HBM] * 6 + ([HBM] if start_up else [VMEM] * 2)
    in_specs += [HBM if epoch == 0 else ANY] * len(sources)
    operands = [*scalars, ratings, row_mask, *users, *sources]
    if not first:
        in_specs += [ANY]
        operands += [carried]
    elif epoch > 0:
        in_specs += [VMEM]
        operands += [own]
    scratch = [
        *[pltpu.SMEM(s.shape, jnp.int32) for s in scalars],
        pltpu.VMEM((slots, tile), jnp.int32),
        pltpu.VMEM((rank, members * rows), F32),
        pltpu.VMEM((slots, tile, tile), BF16),
        *[pltpu.SMEM((slots + 1,), jnp.int32)] * 3,
        pltpu.SemaphoreType.DMA((slots,)),
        pltpu.SemaphoreType.DMA((2 * members,)),
        pltpu.SemaphoreType.DMA((7,)),
        *[pltpu.VMEM((2, tile, tile), BF16)] * WIDE,
    ]
    if epoch == 0:
        scratch.append(pltpu.VMEM((members * rows, rank), F32))
    else:
        scratch.append(pltpu.VMEM((rank, members * rows), BF16))
    if start_up:
        scratch.append(pltpu.VMEM((user_rows, rank), F32))
    return pl.pallas_call(
        functools.partial(
            tile_kernel, epoch, chunk, direct, members, shard_tiles, tile, pieces
        ),
        out_shape=out_shape,
        in_specs=in_specs,
        out_specs=[VMEM] * len(out_shape),
        scratch_shapes=scratch,
        compiler_params=params(40),
        cost_estimate=declared(f"tiles_{epoch}_{chunk}"),
        name=f"tiles_{epoch}_{chunk}",
    )(*operands)


def user_kernel(epoch, block_rows, owner_ref, users, grad, *refs):
    outs = 4 if epoch + 1 < SUB else 1
    pieces, outs = refs[:-outs], refs[-outs:]
    gram = over_rows(pieces[0][...], pieces[0][...])
    for piece in pieces[1:]:
        gram += over_rows(piece[...], piece[...])
    full = gram * (GRAM / block_rows) + ridge(users.shape[1])
    pull = jnp.dot(users[...], full, precision=lax.Precision.HIGHEST, preferred_element_type=F32)
    new = users[...] - LEARN * (grad[...].T + pull)
    outs[0][...] = new
    if len(outs) > 1:
        plain = new.astype(BF16)
        turned = new.T.astype(BF16)
        outs[1][...] = plain
        outs[2][...] = turned
        own = jnp.dot(turned, plain, preferred_element_type=F32)
        outs[3][...] = owned(own, users.shape[0], owner_ref[0, epoch + 1])


def user_call(epoch, block_rows, owners, users, grad, pieces):
    rows, rank = users.shape
    sd = jax.ShapeDtypeStruct
    out_shape = [sd(users.shape, F32)]
    if epoch + 1 < SUB:
        out_shape += [sd((rows, rank), BF16), sd((rank, rows), BF16), sd((rank, rank), BF16)]
    return pl.pallas_call(
        functools.partial(user_kernel, epoch, block_rows),
        out_shape=out_shape,
        in_specs=[pl.BlockSpec(memory_space=pltpu.SMEM)] + [VMEM] * (2 + len(pieces)),
        out_specs=[VMEM] * len(out_shape),
        compiler_params=params(40),
        cost_estimate=declared(f"users_{epoch}"),
        name=f"users_{epoch}",
    )(owners, users, grad, *pieces)


def summed(refs, names, r, width):
    total = None
    for ref, order in zip(refs, names):
        k = order.index(r)
        term = ref[:, k * width:(k + 1) * width].astype(F32)
        total = term if total is None else total + term
    return total


def mid_kernel(paths, grams, *refs):
    at = 0
    outs = refs[sum(len(names) for names, _, _ in paths) + grams:]
    gram_refs = refs[len(refs) - len(paths) - grams:len(refs) - len(paths)]
    for (names, going, width), out in zip(paths, outs):
        terms = refs[at:at + len(names)]
        at += len(names)
        for k, r in enumerate(going):
            out[:, k * width:(k + 1) * width] = summed(terms, names, r, width).astype(BF16)
    if grams:
        rank = outs[0].shape[0]
        total = gram_refs[0][:, gram_refs[0].shape[1] - rank:].astype(F32)
        for ref in gram_refs[1:]:
            total += ref[:, ref.shape[1] - rank:].astype(F32)
        outs[0][:, outs[0].shape[1] - rank:] = total.astype(BF16)


def mid_call(epoch, chunk, step, paths, grams):
    rank = paths[0][0][0][0].shape[0]
    specs, operands, out_shape = [], [], []
    for terms, going, width in paths:
        specs.append(([names for _, names in terms], going, width))
        operands += [array for array, _ in terms]
        extra = rank if grams and not out_shape else 0
        out_shape.append(jax.ShapeDtypeStruct((rank, len(going) * width + extra), BF16))
    operands += grams
    return pl.pallas_call(
        functools.partial(mid_kernel, specs, len(grams)),
        out_shape=out_shape,
        in_specs=[VMEM] * len(operands),
        out_specs=[VMEM] * len(out_shape),
        compiler_params=params(40),
        cost_estimate=declared(f"mid_{epoch}_{chunk}_{step}"),
        name=f"mid_{epoch}_{chunk}_{step}",
    )(*operands)


def item_kernel(epoch, count, rows, width, grams, items, *refs):
    terms_a, terms_b = refs[:count], refs[count:2 * count]
    gram_refs = refs[2 * count:2 * count + grams]
    refs = refs[2 * count + grams:]
    out = refs[0]
    rank = gram_refs[0].shape[0]
    gram = gram_refs[0][:, gram_refs[0].shape[1] - rank:]
    for ref in gram_refs[1:]:
        gram = (gram.astype(F32) + ref[:, ref.shape[1] - rank:].astype(F32)).astype(BF16)
    if grams > 1:
        refs[1][...] = gram
    zero = [[0]] * count
    grad = jnp.concatenate(
        [summed(terms_a, zero, 0, width), summed(terms_b, zero, 0, rows - width)], axis=1
    )
    if epoch == 0:
        high = items[...].astype(BF16)
        low = (items[...] - high.astype(F32)).astype(BF16)
        pull = over_columns(gram, high) + over_columns(gram, low)
    else:
        pull = over_columns(gram, items[...])
    new = items[...].astype(F32) - LEARN * (grad + pull)
    if epoch + 1 < SUB:
        out[...] = new.astype(BF16)
    else:
        out[:rows] = new.T.astype(BF16)
        if grams > 1:
            out[rows:] = gram


def item_call(epoch, chunk, shard_rows, items, terms_a, terms_b, grams):
    rank = grams[0].shape[0]
    rows = shard_rows // CHUNKS
    last = epoch + 1 == SUB
    tall = rows + (rank if len(grams) > 1 else 0)
    out_shape = [jax.ShapeDtypeStruct((tall, rank) if last else (rank, rows), BF16)]
    if len(grams) > 1:
        out_shape.append(jax.ShapeDtypeStruct((rank, rank), BF16))
    out = pl.pallas_call(
        functools.partial(
            item_kernel, epoch, len(terms_a), rows, rows // 2, len(grams)
        ),
        out_shape=out_shape,
        in_specs=[VMEM] * (1 + 2 * len(terms_a) + len(grams)),
        out_specs=[VMEM] * len(out_shape),
        compiler_params=params(40),
        cost_estimate=declared(f"items_{epoch}_{chunk}"),
        name=f"items_{epoch}_{chunk}",
    )(items, *terms_a, *terms_b, *grams)
    gram = out[1] if len(grams) > 1 else None
    return out[0], gram


def swapped(value, bit):
    length = lax.axis_size("grp")
    return lax.ppermute(value, "grp", [(i, i ^ bit) for i in range(length)])


def moved(value, bit):
    length, blocks = lax.axis_size("grp"), lax.axis_size("blk")
    pairs = [
        (b * length + i, (b + 1) % blocks * length + (i ^ bit))
        for b in range(blocks)
        for i in range(length)
    ]
    return lax.ppermute(value, ("blk", "grp"), pairs)


def orders_of(members):
    bits = [1 << i for i in range(members.bit_length() - 1)]
    return bits, bits[::-1]


def exchanged(out, members):
    return [swapped(send, order[0]) for send, order in zip((out[0], out[2]), orders_of(members))]


def scattered(epoch, chunk, out, arrived, members, widths):
    send_a, keep_a, _, keep_b = out[:4]
    orders = orders_of(members)
    names = [without(members, order[0]) for order in orders]
    terms = [[(keep_a, names[0])], [(keep_b, names[1])]]
    grams = [send_a] if chunk == 0 else []
    sends = []
    for step in range(len(orders[0])):
        for p in range(2):
            terms[p].append((arrived[p], names[p]))
        if grams:
            grams.append(arrived[0])
        if step + 1 == len(orders[0]):
            break
        paths = []
        for p in range(2):
            bit = orders[p][step + 1]
            paths.append((terms[p], [r for r in names[p] if r & bit], widths[p]))
            names[p] = [r for r in names[p] if not r & bit]
        sends = mid_call(epoch, chunk, step, paths, grams)
        arrived = [swapped(sends[p], orders[p][step + 1]) for p in range(2)]
    return [a for a, _ in terms[0]], [a for a, _ in terms[1]], grams, sends


def scattered_direct(epoch, chunk, out, arrived, members, widths):
    _, keep_a, _, keep_b = out[:4]
    orders = orders_of(members)
    names = [[r for r in without(members, order[0]) if r] for order in orders]
    terms = [[(keep_a, names[0])], [(keep_b, names[1])]]
    ended = [[moved(out[4 + p], orders[p][0])] for p in range(2)]
    own = moved(out[6], 0)
    arrived = [tied(array, own) for array in arrived]
    sends = []
    for step in range(len(orders[0]) - 1):
        paths, kinds = [], []
        for p in range(2):
            terms[p].append((arrived[p], names[p]))
            bit = orders[p][step + 1]
            paths.append((terms[p], [bit], widths[p]))
            kinds.append((p, True))
            going = [r for r in names[p] if r & bit and r != bit]
            names[p] = [r for r in names[p] if not r & bit]
            if going:
                paths.append((terms[p], going, widths[p]))
                kinds.append((p, False))
        sends = mid_call(epoch, chunk, step, paths, [])
        arrived = [None, None]
        for (p, alone), send in zip(kinds, sends):
            bit = orders[p][step + 1]
            if alone:
                ended[p].append(moved(send, bit))
            else:
                arrived[p] = swapped(send, bit)
    return own, ended[0], ended[1], sends


def final_kernel(rows, width, others, count, *refs):
    done, refs = refs[:others], refs[others:]
    items, own = refs[:2]
    sides = refs[2:2 + count], refs[2 + count:2 + 2 * count]
    out, held, sem = refs[2 + 2 * count:]

    def leave(c):
        spot = pl.ds(c * rows, rows)
        return pltpu.make_async_copy(held.at[spot], out.at[spot], sem.at[c])

    for c, ref in enumerate(done):
        held[c * rows:(c + 1) * rows] = ref[:rows].astype(F32)
        leave(c).start()
    gram = done[0][rows:]
    totals = []
    for side, start, size in zip(sides, (0, width), (width, rows - width)):
        total = own[:, start:start + size].astype(F32)
        for ref in side:
            total += ref[...].astype(F32)
        totals.append(total)
    grad = jnp.concatenate(totals, axis=1)
    new = items[...].astype(F32) - LEARN * (grad + over_columns(gram, items[...]))
    held[others * rows:] = new.T
    leave(others).start()
    for c in range(others + 1):
        leave(c).wait()


def final_call(done, items, own, side_a, side_b):
    rank, rows = items.shape
    operands = [*done, items, own, *side_a, *side_b]
    return pl.pallas_call(
        functools.partial(final_kernel, rows, rows // 2, len(done), len(side_a)),
        out_shape=jax.ShapeDtypeStruct((CHUNKS * rows, rank), F32),
        in_specs=[VMEM] * len(operands),
        out_specs=HBM,
        scratch_shapes=[
            pltpu.VMEM((CHUNKS * rows, rank), F32), pltpu.SemaphoreType.DMA((CHUNKS,))
        ],
        compiler_params=params(40),
        cost_estimate=declared("items_final"),
        name="items_final",
    )(*operands)


def tied(value, *others):
    return lax.optimization_barrier((value, *others))[0]


def gathered(shard, after):
    length = lax.axis_size("grp")
    rows, half = shard.shape[1], shard.shape[1] // 2
    known = {0: [moved(tied(shard, *after), 0)]}
    for bit in orders_of(length)[0]:
        known[bit] = [moved(shard, bit)]
    near = [known[bit][0] for bit in orders_of(length)[0]]

    def cut(r, p):
        pieces = known[r]
        if len(pieces) == 2:
            return pieces[p]
        return pieces[0][:, half:] if p else pieces[0][:, :half]

    for r in range(1, length):
        if r not in known:
            low, high = r & -r, 1 << (r.bit_length() - 1)
            sent = [cut(r ^ high, 0), cut(r ^ low, 1)]
            sent = [tied(piece, *after) for piece in sent]
            known[r] = [swapped(sent[0], high), swapped(sent[1], low)]
    found = []
    for r, pieces in known.items():
        spots = [(0, rows)] if len(pieces) == 1 else [(0, half), (half, rows - half)]
        found += [(piece, [(r, *spot)]) for piece, spot in zip(pieces, spots)]
    return found, near


def local(ratings, row_index, col_index, row_mask, counts, owner_list, user_factors, item_factors):
    members = lax.axis_size("grp")
    block_rows = item_factors.shape[0]
    shard_rows = block_rows // members
    rows = shard_rows // CHUNKS
    owners = owner_list.reshape(1, -1)
    row_index, col_index, counts, owner_hbm, row_mask, first_users, ratings, item_factors = (
        pltpu.with_memory_space_constraint(array, pltpu.HBM)
        for array in (
            row_index, col_index, counts.reshape(1, -1), owners, row_mask, user_factors, ratings,
            item_factors,
        )
    )
    scalars = (row_index, col_index, counts, owner_hbm)
    full_users = user_factors
    users = [first_users]
    own_gram = None
    gathers = []
    for epoch in range(SUB):
        grad_user = None
        outs, olds, pieces = [], [], []
        for c in range(CHUNKS):
            if epoch == 0:
                sources = [(item_factors, None)]
            else:
                sources = gathers[c]
            direct = epoch + 1 == SUB and c + 1 == CHUNKS
            out = tile_call(
                epoch, c, direct, members, scalars, ratings, row_mask, users, sources, grad_user,
                own_gram,
            )
            grad_user = out[7 if direct else 4]
            outs.append(out)
            if epoch == 0:
                pieces.append(out[5])
                olds.append(out[6])
                if c == 0:
                    users = out[7:9]
            else:
                pieces += [array for array, _ in sources]
                olds.append(sources[0][0])
        last = epoch + 1 == SUB
        if last:
            kept = moved(tied(olds[-1], grad_user), 0)
        if not last:
            new_users = user_call(epoch, block_rows, owners, full_users, grad_user, pieces)
            full_users = new_users[0]
        shards = []
        grams = None
        reduced = []
        ahead = None
        for c in range(CHUNKS):
            arrived = ahead if ahead else exchanged(outs[c], members)
            arrived = [tied(array, grad_user if last else outs[-1][4]) for array in arrived]
            if last:
                if c == 0:
                    ahead = exchanged(outs[1], members)
                else:
                    arrived = [tied(array, grad_user, kept) for array in ahead]
            reduce = scattered_direct if last and c + 1 == CHUNKS else scattered
            reduced.append(
                reduce(epoch, c, outs[c], arrived, members, (rows // 2, rows - rows // 2))
            )
        for c in range(CHUNKS - 1 if last else CHUNKS):
            terms_a, terms_b, found, sent = reduced[c]
            old = olds[c]
            if not last:
                old = tied(old, *reduced[min(c + 1, CHUNKS - 1)][3])
                old = tied(old, full_users)
            shard, gram = item_call(epoch, c, shard_rows, old, terms_a, terms_b, found or grams)
            if found:
                grams = [gram]
            shards.append(shard)
        if last:
            done = [moved(shard, 0) for shard in shards]
            own, side_a, side_b, sent = reduced[-1]
            grad_user = tied(grad_user, *sent)
            item_final = final_call(done, kept, own, side_a, side_b)
            full_users = user_call(epoch, block_rows, owners, full_users, grad_user, pieces)[0]
        else:
            users, own_gram = new_users[1:3], new_users[3]
            gathers = [gathered(shard, [shards[-1]]) for shard in shards]
            near = gathers[-1][1]
            gathers = [found for found, _ in gathers]
            (array, columns), *rest = gathers[0]
            gathers[0] = [(tied(array, *near), columns), *rest]
    return full_users, item_final


def solution(mesh):
    in_specs = (
        P(None, "blk", "grp", None, None, None),
        P(None, "blk", "grp", None),
        P(None, "blk", "grp", None),
        P(None, "blk", "grp", None, None),
        P(None, "blk", "grp"),
        P(None, "blk"),
        P(("blk", "grp"), None),
        P("blk", None),
    )
    out_specs = (P(("blk", "grp"), None), P(("blk", "grp"), None))
    return jax.shard_map(local, mesh=mesh, in_specs=in_specs, out_specs=out_specs, check_vma=False)
```

```python
import functools

import jax
import jax.numpy as jnp
from jax import lax
from jax.experimental import pallas as pl
from jax.experimental.pallas import tpu as pltpu
from jax.sharding import PartitionSpec as P

SUB = 2
LEARN = 0.004
GRAM = 256.0
RIDGE = 1.0
CHUNKS = 2
WIDE = 4
F32 = jnp.float32
BF16 = jnp.bfloat16
BIG = float(jnp.finfo(jnp.bfloat16).max)

ANY = pl.BlockSpec(memory_space=pl.ANY)
HBM = pl.BlockSpec(memory_space=pltpu.HBM)
VMEM = pl.BlockSpec(memory_space=pltpu.VMEM)


def params(mib):
    return pltpu.CompilerParams(vmem_limit_bytes=mib * 1024 * 1024)


def declared(name):
    costs = {"tiles": 16e9, "users": 10e9, "items": 1.2e9, "mid": 0.2e9, "mid_1_1_0": 1e9}
    flops = costs.get(name, costs[name.split("_")[0]])
    return pl.CostEstimate(flops=int(flops), bytes_accessed=1 << 16, transcendentals=0)


def over_rows(a, b):
    return lax.dot_general(a, b, (((1,), (1,)), ((), ())), preferred_element_type=F32)


def over_columns(a, b):
    return lax.dot_general(a, b, (((0,), (0,)), ((), ())), preferred_element_type=F32)


def ridge(rank):
    down = lax.broadcasted_iota(jnp.int32, (rank, rank), 0)
    across = lax.broadcasted_iota(jnp.int32, (rank, rank), 1)
    return jnp.where(down == across, RIDGE, 0.0)


def owned(gram, rows, owner):
    full = gram * (GRAM / rows) + ridge(gram.shape[0])
    return jnp.where(owner == lax.axis_index("grp"), full, 0.0).astype(BF16)


def without(members, bit):
    return [r for r in range(members) if not r & bit]


def chunk_columns(members, rows, direct):
    half = rows // 2
    found = []
    alone = []
    for bit, start, width in ((1, 0, half), (members // 2, half, rows - half)):
        names = [r for r in without(members, bit) if r or not direct]
        found.append([(r | bit, start, width) for r in names])
        found.append([(r, start, width) for r in names])
        alone.append([(bit, start, width)])
    return found + [*alone, [(0, 0, rows)]] if direct else found


def tile_kernel(epoch, chunk, direct, members, shard_tiles, tile, pieces, *refs):
    start_up = epoch == 0 and chunk == 0
    first = chunk == 0
    refs = list(refs)

    def take(n):
        out, refs[:n] = refs[:n], []
        return out

    row_hbm, col_hbm, count_hbm, owner_hbm, ratings, mask_hbm = take(6)
    users = take(1) if start_up else take(2)
    sources = take(len(pieces))
    grad_in = take(0 if first else 1)
    own_in = take(1 if first and epoch > 0 else 0)
    outs = take(7 if direct else 4)
    grad_user, = take(1)
    if epoch == 0:
        items, old = take(2)
    if start_up:
        user_bf, user_t = take(2)
    else:
        user_bf, user_t = users
    (row_ref, col_ref, count_ref, owner_ref, mask, parts, held, slots, slot_row, slot_place,
     sem_tile, sem_item, sem_small) = take(13)
    errors = take(WIDE)
    if epoch == 0:
        items_f, = take(1)
    else:
        items, = take(1)
    if start_up:
        users_f, = take(1)

    me = lax.axis_index("grp")
    chunk_tiles = shard_tiles // CHUNKS
    rows = chunk_tiles * tile
    half = rows // 2
    bits_tile = chunk_tiles.bit_length() - 1
    bits_shard = shard_tiles.bit_length() - 1

    pairs = [(row_hbm, row_ref), (col_hbm, col_ref), (count_hbm, count_ref),
             (owner_hbm, owner_ref), (mask_hbm.at[epoch, 0, 0], mask)]
    if not first:
        pairs.append((grad_in[0], grad_user))
    if start_up:
        pairs.append((users[0], users_f))
    small = [
        pltpu.make_async_copy(src, dst, sem_small.at[i]) for i, (src, dst) in enumerate(pairs)
    ]
    for copy in small:
        copy.start()
    copies = []
    if epoch == 0:
        for r in range(members):
            start = pl.multiple_of((me ^ r) * (shard_tiles * tile) + chunk * rows, rows)
            copies.append(
                pltpu.make_async_copy(
                    sources[0].at[pl.ds(start, rows)], items_f.at[pl.ds(r * rows, rows)], sem_item.at[r]
                )
            )
    else:
        for source, columns in zip(sources, pieces):
            at = 0
            for r, start, width in columns:
                copies.append(
                    pltpu.make_async_copy(
                        source.at[:, pl.ds(at, width)], items.at[:, pl.ds(r * rows + start, width)],
                        sem_item.at[len(copies)],
                    )
                )
                at += width
    for copy in copies:
        copy.start()
    for copy in small[:4]:
        copy.wait()

    count = count_ref[0, epoch]

    def pick(t, found):
        col = col_ref[epoch, 0, 0, t]
        slots[found] = t
        slot_row[found] = row_ref[epoch, 0, 0, t]
        slot_place[found] = ((col >> bits_shard) ^ me) * chunk_tiles + (col & (chunk_tiles - 1))
        here = ((col >> bits_tile) & (CHUNKS - 1)) == chunk
        return found + jnp.where(here & (t < count), 1, 0).astype(jnp.int32)

    total = lax.fori_loop(0, col_ref.shape[3], pick, jnp.int32(0), unroll=8)

    def fetch(i):
        return pltpu.make_async_copy(ratings.at[epoch, 0, 0, slots[i]], held.at[i], sem_tile.at[i])

    def begin(i, _):
        fetch(i).start()
        return 0

    lax.fori_loop(0, total, begin, 0)

    parts[...] = jnp.zeros_like(parts)
    if first:
        grad_user[...] = jnp.zeros_like(grad_user)
    for copy in small[4:]:
        copy.wait()

    def user_tile(j, _):
        spot = pl.ds(pl.multiple_of(j * tile, tile), tile)
        part = users_f[spot].astype(BF16)
        user_bf[spot] = part
        user_t[:, spot] = part.T
        return 0

    if start_up:
        lax.fori_loop(0, users_f.shape[0] // tile, user_tile, 0, unroll=2)

    def item_tile(own, j, _):
        spot = pl.ds(pl.multiple_of(j * tile, tile), tile)
        items[:, spot] = items_f[spot].astype(BF16).T
        if own:
            old[:, spot] = items_f[spot].T
        return 0

    for r, copy in enumerate(copies):
        copy.wait()
        if epoch == 0:
            lax.fori_loop(
                r * chunk_tiles, (r + 1) * chunk_tiles, functools.partial(item_tile, r == 0), 0,
                unroll=2,
            )

    def spots(i):
        row = pl.multiple_of(slot_row[i] * tile, tile)
        place = pl.multiple_of(slot_place[i] * tile, tile)
        return pl.ds(row, tile), pl.ds(place, tile)

    def ready(j):
        for k in range(WIDE):
            i = WIDE * j + k

            @pl.when(i < total)
            def _():
                fetch(i).wait()

    def front(j):
        for k in range(WIDE):
            i = jnp.minimum(WIDE * j + k, total - 1)
            row, place = spots(i)
            predicted = jnp.dot(user_bf[row], items[:, place], preferred_element_type=F32)
            error = (predicted - held[i].astype(F32)).astype(BF16)
            errors[k][j & 1] = jnp.clip(error, -BIG, BIG)

    def back(j):
        adds = []
        for k in range(WIDE):
            valid = WIDE * j + k < total
            i = jnp.minimum(WIDE * j + k, total - 1)
            row, place = spots(i)
            weight = mask[pl.ds(slots[i], 1), :].astype(F32)
            weight = jnp.where(valid, weight, 0.0)
            error = errors[k][j & 1]
            user_add = over_rows(items[:, place], error)
            item_add = jnp.dot(
                user_t[:, row] * weight.astype(BF16), error, preferred_element_type=F32
            )
            adds.append((row, place, jnp.where(weight > 0.5, user_add, 0.0), item_add))
        return adds

    def add(adds):
        for row, place, user_add, item_add in adds:
            grad_user[:, row] += user_add
            parts[:, place] += item_add

    groups = (total + WIDE - 1) // WIDE

    @pl.when(total > 0)
    def _():
        ready(0)
        front(0)

    def step(j, _):
        ready(j + 1)
        adds = back(j)
        front(j + 1)
        add(adds)
        return 0

    lax.fori_loop(0, groups, step, 0)

    for out, columns in zip(outs, chunk_columns(members, rows, direct)):
        at = 0
        for r, start, width in columns:
            out[:, at:at + width] = parts[:, pl.ds(r * rows + start, width)].astype(BF16)
            at += width
    if start_up:
        own = jnp.dot(user_t[...], user_bf[...], preferred_element_type=F32)
        own = owned(own, users_f.shape[0], owner_ref[0, epoch])
    elif first:
        own = own_in[0][...]
    if first:
        outs[0][:, members // 2 * half:] = own


def tile_call(
    epoch, chunk, direct, members, scalars, ratings, row_mask, users, sources, carried, own
):
    tile = ratings.shape[-1]
    slots = ratings.shape[3]
    start_up = epoch == 0 and chunk == 0
    first = chunk == 0
    user_rows, rank = users[0].shape
    pieces = [columns for _, columns in sources]
    sources = [array for array, _ in sources]
    if epoch == 0:
        block_rows = sources[0].shape[0]
    else:
        block_rows = sum(s.shape[1] for s in sources) * CHUNKS
    shard_tiles = block_rows // members // tile
    rows = shard_tiles // CHUNKS * tile
    sd = jax.ShapeDtypeStruct
    widths = [sum(w for _, _, w in columns) for columns in chunk_columns(members, rows, direct)]
    widths[0] += rank if first else 0
    out_shape = [sd((rank, width), BF16) for width in widths] + [sd((rank, user_rows), F32)]
    if epoch == 0:
        out_shape += [sd((rank, members * rows), BF16), sd((rank, rows), F32)]
    if start_up:
        out_shape += [sd((user_rows, rank), BF16), sd((rank, user_rows), BF16)]
    in_specs = [HBM] * 6 + ([HBM] if start_up else [VMEM] * 2)
    in_specs += [HBM if epoch == 0 else ANY] * len(sources)
    operands = [*scalars, ratings, row_mask, *users, *sources]
    if not first:
        in_specs += [ANY]
        operands += [carried]
    elif epoch > 0:
        in_specs += [VMEM]
        operands += [own]
    scratch = [
        *[pltpu.SMEM(s.shape, jnp.int32) for s in scalars],
        pltpu.VMEM((slots, tile), jnp.int32),
        pltpu.VMEM((rank, members * rows), F32),
        pltpu.VMEM((slots, tile, tile), BF16),
        *[pltpu.SMEM((slots + 1,), jnp.int32)] * 3,
        pltpu.SemaphoreType.DMA((slots,)),
        pltpu.SemaphoreType.DMA((2 * members,)),
        pltpu.SemaphoreType.DMA((7,)),
        *[pltpu.VMEM((2, tile, tile), BF16)] * WIDE,
    ]
    if epoch == 0:
        scratch.append(pltpu.VMEM((members * rows, rank), F32))
    else:
        scratch.append(pltpu.VMEM((rank, members * rows), BF16))
    if start_up:
        scratch.append(pltpu.VMEM((user_rows, rank), F32))
    return pl.pallas_call(
        functools.partial(
            tile_kernel, epoch, chunk, direct, members, shard_tiles, tile, pieces
        ),
        out_shape=out_shape,
        in_specs=in_specs,
        out_specs=[VMEM] * len(out_shape),
        scratch_shapes=scratch,
        compiler_params=params(40),
        cost_estimate=declared(f"tiles_{epoch}_{chunk}"),
        name=f"tiles_{epoch}_{chunk}",
    )(*operands)


def user_kernel(epoch, block_rows, owner_ref, users, grad, *refs):
    outs = 4 if epoch + 1 < SUB else 1
    pieces, outs = refs[:-outs], refs[-outs:]
    gram = over_rows(pieces[0][...], pieces[0][...])
    for piece in pieces[1:]:
        gram += over_rows(piece[...], piece[...])
    full = gram * (GRAM / block_rows) + ridge(users.shape[1])
    pull = jnp.dot(users[...], full, precision=lax.Precision.HIGHEST, preferred_element_type=F32)
    new = users[...] - LEARN * (grad[...].T + pull)
    outs[0][...] = new
    if len(outs) > 1:
        plain = new.astype(BF16)
        turned = new.T.astype(BF16)
        outs[1][...] = plain
        outs[2][...] = turned
        own = jnp.dot(turned, plain, preferred_element_type=F32)
        outs[3][...] = owned(own, users.shape[0], owner_ref[0, epoch + 1])


def user_call(epoch, block_rows, owners, users, grad, pieces):
    rows, rank = users.shape
    sd = jax.ShapeDtypeStruct
    out_shape = [sd(users.shape, F32)]
    if epoch + 1 < SUB:
        out_shape += [sd((rows, rank), BF16), sd((rank, rows), BF16), sd((rank, rank), BF16)]
    return pl.pallas_call(
        functools.partial(user_kernel, epoch, block_rows),
        out_shape=out_shape,
        in_specs=[pl.BlockSpec(memory_space=pltpu.SMEM)] + [VMEM] * (2 + len(pieces)),
        out_specs=[VMEM] * len(out_shape),
        compiler_params=params(40),
        cost_estimate=declared(f"users_{epoch}"),
        name=f"users_{epoch}",
    )(owners, users, grad, *pieces)


def summed(refs, names, r, width):
    total = None
    for ref, order in zip(refs, names):
        k = order.index(r)
        term = ref[:, k * width:(k + 1) * width].astype(F32)
        total = term if total is None else total + term
    return total


def mid_kernel(paths, grams, *refs):
    at = 0
    outs = refs[sum(len(names) for names, _, _ in paths) + grams:]
    gram_refs = refs[len(refs) - len(paths) - grams:len(refs) - len(paths)]
    for (names, going, width), out in zip(paths, outs):
        terms = refs[at:at + len(names)]
        at += len(names)
        for k, r in enumerate(going):
            out[:, k * width:(k + 1) * width] = summed(terms, names, r, width).astype(BF16)
    if grams:
        rank = outs[0].shape[0]
        total = gram_refs[0][:, gram_refs[0].shape[1] - rank:].astype(F32)
        for ref in gram_refs[1:]:
            total += ref[:, ref.shape[1] - rank:].astype(F32)
        outs[0][:, outs[0].shape[1] - rank:] = total.astype(BF16)


def mid_call(epoch, chunk, step, paths, grams):
    rank = paths[0][0][0][0].shape[0]
    specs, operands, out_shape = [], [], []
    for terms, going, width in paths:
        specs.append(([names for _, names in terms], going, width))
        operands += [array for array, _ in terms]
        extra = rank if grams and not out_shape else 0
        out_shape.append(jax.ShapeDtypeStruct((rank, len(going) * width + extra), BF16))
    operands += grams
    return pl.pallas_call(
        functools.partial(mid_kernel, specs, len(grams)),
        out_shape=out_shape,
        in_specs=[VMEM] * len(operands),
        out_specs=[VMEM] * len(out_shape),
        compiler_params=params(40),
        cost_estimate=declared(f"mid_{epoch}_{chunk}_{step}"),
        name=f"mid_{epoch}_{chunk}_{step}",
    )(*operands)


def item_kernel(epoch, count, rows, width, grams, items, *refs):
    terms_a, terms_b = refs[:count], refs[count:2 * count]
    gram_refs = refs[2 * count:2 * count + grams]
    refs = refs[2 * count + grams:]
    out = refs[0]
    rank = gram_refs[0].shape[0]
    gram = gram_refs[0][:, gram_refs[0].shape[1] - rank:]
    for ref in gram_refs[1:]:
        gram = (gram.astype(F32) + ref[:, ref.shape[1] - rank:].astype(F32)).astype(BF16)
    if grams > 1:
        refs[1][...] = gram
    zero = [[0]] * count
    grad = jnp.concatenate(
        [summed(terms_a, zero, 0, width), summed(terms_b, zero, 0, rows - width)], axis=1
    )
    if epoch == 0:
        high = items[...].astype(BF16)
        low = (items[...] - high.astype(F32)).astype(BF16)
        pull = over_columns(gram, high) + over_columns(gram, low)
    else:
        pull = over_columns(gram, items[...])
    new = items[...].astype(F32) - LEARN * (grad + pull)
    if epoch + 1 < SUB:
        out[...] = new.astype(BF16)
    else:
        out[:rows] = new.T.astype(BF16)
        if grams > 1:
            out[rows:] = gram


def item_call(epoch, chunk, shard_rows, items, terms_a, terms_b, grams):
    rank = grams[0].shape[0]
    rows = shard_rows // CHUNKS
    last = epoch + 1 == SUB
    tall = rows + (rank if len(grams) > 1 else 0)
    out_shape = [jax.ShapeDtypeStruct((tall, rank) if last else (rank, rows), BF16)]
    if len(grams) > 1:
        out_shape.append(jax.ShapeDtypeStruct((rank, rank), BF16))
    out = pl.pallas_call(
        functools.partial(
            item_kernel, epoch, len(terms_a), rows, rows // 2, len(grams)
        ),
        out_shape=out_shape,
        in_specs=[VMEM] * (1 + 2 * len(terms_a) + len(grams)),
        out_specs=[VMEM] * len(out_shape),
        compiler_params=params(40),
        cost_estimate=declared(f"items_{epoch}_{chunk}"),
        name=f"items_{epoch}_{chunk}",
    )(items, *terms_a, *terms_b, *grams)
    gram = out[1] if len(grams) > 1 else None
    return out[0], gram


def swapped(value, bit):
    length = lax.axis_size("grp")
    return lax.ppermute(value, "grp", [(i, i ^ bit) for i in range(length)])


def moved(value, bit):
    length, blocks = lax.axis_size("grp"), lax.axis_size("blk")
    pairs = [
        (b * length + i, (b + 1) % blocks * length + (i ^ bit))
        for b in range(blocks)
        for i in range(length)
    ]
    return lax.ppermute(value, ("blk", "grp"), pairs)


def orders_of(members):
    bits = [1 << i for i in range(members.bit_length() - 1)]
    return bits, bits[::-1]


def exchanged(out, members):
    return [swapped(send, order[0]) for send, order in zip((out[0], out[2]), orders_of(members))]


def scattered(epoch, chunk, out, arrived, members, widths):
    send_a, keep_a, _, keep_b = out[:4]
    orders = orders_of(members)
    names = [without(members, order[0]) for order in orders]
    terms = [[(keep_a, names[0])], [(keep_b, names[1])]]
    grams = [send_a] if chunk == 0 else []
    sends = []
    for step in range(len(orders[0])):
        for p in range(2):
            terms[p].append((arrived[p], names[p]))
        if grams:
            grams.append(arrived[0])
        if step + 1 == len(orders[0]):
            break
        paths = []
        for p in range(2):
            bit = orders[p][step + 1]
            paths.append((terms[p], [r for r in names[p] if r & bit], widths[p]))
            names[p] = [r for r in names[p] if not r & bit]
        sends = mid_call(epoch, chunk, step, paths, grams)
        arrived = [swapped(sends[p], orders[p][step + 1]) for p in range(2)]
    return [a for a, _ in terms[0]], [a for a, _ in terms[1]], grams, sends


def scattered_direct(epoch, chunk, out, arrived, members, widths):
    _, keep_a, _, keep_b = out[:4]
    orders = orders_of(members)
    names = [[r for r in without(members, order[0]) if r] for order in orders]
    terms = [[(keep_a, names[0])], [(keep_b, names[1])]]
    ended = [[moved(out[4 + p], orders[p][0])] for p in range(2)]
    own = moved(out[6], 0)
    arrived = [tied(array, own) for array in arrived]
    sends = []
    for step in range(len(orders[0]) - 1):
        paths, kinds = [], []
        for p in range(2):
            terms[p].append((arrived[p], names[p]))
            bit = orders[p][step + 1]
            paths.append((terms[p], [bit], widths[p]))
            kinds.append((p, True))
            going = [r for r in names[p] if r & bit and r != bit]
            names[p] = [r for r in names[p] if not r & bit]
            if going:
                paths.append((terms[p], going, widths[p]))
                kinds.append((p, False))
        sends = mid_call(epoch, chunk, step, paths, [])
        arrived = [None, None]
        for (p, alone), send in zip(kinds, sends):
            bit = orders[p][step + 1]
            if alone:
                ended[p].append(moved(send, bit))
            else:
                arrived[p] = swapped(send, bit)
    return own, ended[0], ended[1], sends


def final_kernel(rows, width, others, count, *refs):
    done, refs = refs[:others], refs[others:]
    items, own = refs[:2]
    sides = refs[2:2 + count], refs[2 + count:2 + 2 * count]
    out, held, sem = refs[2 + 2 * count:]

    def leave(c):
        spot = pl.ds(c * rows, rows)
        return pltpu.make_async_copy(held.at[spot], out.at[spot], sem.at[c])

    for c, ref in enumerate(done):
        held[c * rows:(c + 1) * rows] = ref[:rows].astype(F32)
        leave(c).start()
    gram = done[0][rows:]
    totals = []
    for side, start, size in zip(sides, (0, width), (width, rows - width)):
        total = own[:, start:start + size].astype(F32)
        for ref in side:
            total += ref[...].astype(F32)
        totals.append(total)
    grad = jnp.concatenate(totals, axis=1)
    new = items[...].astype(F32) - LEARN * (grad + over_columns(gram, items[...]))
    held[others * rows:] = new.T
    leave(others).start()
    for c in range(others + 1):
        leave(c).wait()


def final_call(done, items, own, side_a, side_b):
    rank, rows = items.shape
    operands = [*done, items, own, *side_a, *side_b]
    return pl.pallas_call(
        functools.partial(final_kernel, rows, rows // 2, len(done), len(side_a)),
        out_shape=jax.ShapeDtypeStruct((CHUNKS * rows, rank), F32),
        in_specs=[VMEM] * len(operands),
        out_specs=HBM,
        scratch_shapes=[
            pltpu.VMEM((CHUNKS * rows, rank), F32), pltpu.SemaphoreType.DMA((CHUNKS,))
        ],
        compiler_params=params(40),
        cost_estimate=declared("items_final"),
        name="items_final",
    )(*operands)


def tied(value, *others):
    return lax.optimization_barrier((value, *others))[0]


def gathered(shard, after):
    length = lax.axis_size("grp")
    rows, half = shard.shape[1], shard.shape[1] // 2
    known = {0: [moved(tied(shard, *after), 0)]}
    for bit in orders_of(length)[0]:
        known[bit] = [moved(shard, bit)]
    near = [known[bit][0] for bit in orders_of(length)[0]]

    def cut(r, p):
        pieces = known[r]
        if len(pieces) == 2:
            return pieces[p]
        return pieces[0][:, half:] if p else pieces[0][:, :half]

    for r in range(1, length):
        if r not in known:
            low, high = r & -r, 1 << (r.bit_length() - 1)
            sent = [cut(r ^ high, 0), cut(r ^ low, 1)]
            sent = [tied(piece, *after) for piece in sent]
            known[r] = [swapped(sent[0], high), swapped(sent[1], low)]
    found = []
    for r, pieces in known.items():
        spots = [(0, rows)] if len(pieces) == 1 else [(0, half), (half, rows - half)]
        found += [(piece, [(r, *spot)]) for piece, spot in zip(pieces, spots)]
    return found, near


def local(ratings, row_index, col_index, row_mask, counts, owner_list, user_factors, item_factors):
    members = lax.axis_size("grp")
    block_rows = item_factors.shape[0]
    shard_rows = block_rows // members
    rows = shard_rows // CHUNKS
    owners = owner_list.reshape(1, -1)
    row_index, col_index, counts, owner_hbm, row_mask, first_users, ratings, item_factors = (
        pltpu.with_memory_space_constraint(array, pltpu.HBM)
        for array in (
            row_index, col_index, counts.reshape(1, -1), owners, row_mask, user_factors, ratings,
            item_factors,
        )
    )
    scalars = (row_index, col_index, counts, owner_hbm)
    full_users = user_factors
    users = [first_users]
    own_gram = None
    gathers = []
    for epoch in range(SUB):
        grad_user = None
        outs, olds, pieces = [], [], []
        for c in range(CHUNKS):
            if epoch == 0:
                sources = [(item_factors, None)]
            else:
                sources = gathers[c]
                if epoch + 1 == SUB and c + 1 == CHUNKS:
                    kept = moved(tied(sources[0][0], grad_user), 0)
            direct = epoch + 1 == SUB and c + 1 == CHUNKS
            out = tile_call(
                epoch, c, direct, members, scalars, ratings, row_mask, users, sources, grad_user,
                own_gram,
            )
            grad_user = out[7 if direct else 4]
            outs.append(out)
            if epoch == 0:
                pieces.append(out[5])
                olds.append(out[6])
                if c == 0:
                    users = out[7:9]
            else:
                pieces += [array for array, _ in sources]
                olds.append(sources[0][0])
        last = epoch + 1 == SUB
        if not last:
            new_users = user_call(epoch, block_rows, owners, full_users, grad_user, pieces)
            full_users = new_users[0]
        shards = []
        grams = None
        reduced = []
        ahead = None
        for c in range(CHUNKS):
            arrived = ahead if ahead else exchanged(outs[c], members)
            arrived = [tied(array, grad_user if last else outs[-1][4]) for array in arrived]
            if last:
                if c == 0:
                    ahead = exchanged(outs[1], members)
                    arrived = [tied(array, kept) for array in arrived]
                else:
                    arrived = [tied(array, grad_user) for array in ahead]
            reduce = scattered_direct if last and c + 1 == CHUNKS else scattered
            reduced.append(
                reduce(epoch, c, outs[c], arrived, members, (rows // 2, rows - rows // 2))
            )
        for c in range(CHUNKS - 1 if last else CHUNKS):
            terms_a, terms_b, found, sent = reduced[c]
            old = olds[c]
            if not last:
                old = tied(old, *reduced[min(c + 1, CHUNKS - 1)][3])
                old = tied(old, full_users)
            shard, gram = item_call(epoch, c, shard_rows, old, terms_a, terms_b, found or grams)
            if found:
                grams = [gram]
            shards.append(shard)
        if last:
            done = [moved(shard, 0) for shard in shards]
            own, side_a, side_b, sent = reduced[-1]
            grad_user = tied(grad_user, *sent)
            item_final = final_call(done, kept, own, side_a, side_b)
            full_users = user_call(epoch, block_rows, owners, full_users, grad_user, pieces)[0]
        else:
            users, own_gram = new_users[1:3], new_users[3]
            gathers = [gathered(shard, [shards[-1]]) for shard in shards]
            near = gathers[-1][1]
            gathers = [found for found, _ in gathers]
            (array, columns), *rest = gathers[0]
            gathers[0] = [(tied(array, *near), columns), *rest]
    return full_users, item_final


def solution(mesh):
    in_specs = (
        P(None, "blk", "grp", None, None, None),
        P(None, "blk", "grp", None),
        P(None, "blk", "grp", None),
        P(None, "blk", "grp", None, None),
        P(None, "blk", "grp"),
        P(None, "blk"),
        P(("blk", "grp"), None),
        P("blk", None),
    )
    out_specs = (P(("blk", "grp"), None), P(("blk", "grp"), None))
    return jax.shard_map(local, mesh=mesh, in_specs=in_specs, out_specs=out_specs, check_vma=False)
```

```python
import functools

import jax
import jax.numpy as jnp
from jax import lax
from jax.experimental import pallas as pl
from jax.experimental.pallas import tpu as pltpu
from jax.sharding import PartitionSpec as P

SUB = 2
LEARN = 0.004
GRAM = 256.0
RIDGE = 1.0
CHUNKS = 2
WIDE = 4
F32 = jnp.float32
BF16 = jnp.bfloat16
BIG = float(jnp.finfo(jnp.bfloat16).max)

ANY = pl.BlockSpec(memory_space=pl.ANY)
HBM = pl.BlockSpec(memory_space=pltpu.HBM)
VMEM = pl.BlockSpec(memory_space=pltpu.VMEM)


def params(mib):
    return pltpu.CompilerParams(vmem_limit_bytes=mib * 1024 * 1024)


def declared(name):
    costs = {"tiles": 16e9, "users": 10e9, "items": 1.2e9, "mid": 0.2e9, "mid_1_1_0": 1e9}
    flops = costs.get(name, costs[name.split("_")[0]])
    return pl.CostEstimate(flops=int(flops), bytes_accessed=1 << 16, transcendentals=0)


def over_rows(a, b):
    return lax.dot_general(a, b, (((1,), (1,)), ((), ())), preferred_element_type=F32)


def over_columns(a, b):
    return lax.dot_general(a, b, (((0,), (0,)), ((), ())), preferred_element_type=F32)


def ridge(rank):
    down = lax.broadcasted_iota(jnp.int32, (rank, rank), 0)
    across = lax.broadcasted_iota(jnp.int32, (rank, rank), 1)
    return jnp.where(down == across, RIDGE, 0.0)


def owned(gram, rows, owner):
    full = gram * (GRAM / rows) + ridge(gram.shape[0])
    return jnp.where(owner == lax.axis_index("grp"), full, 0.0).astype(BF16)


def without(members, bit):
    return [r for r in range(members) if not r & bit]


def chunk_columns(members, rows, direct):
    half = rows // 2
    found = []
    alone = []
    for bit, start, width in ((1, 0, half), (members // 2, half, rows - half)):
        names = [r for r in without(members, bit) if r or not direct]
        found.append([(r | bit, start, width) for r in names])
        found.append([(r, start, width) for r in names])
        alone.append([(bit, start, width)])
    return found + [*alone, [(0, 0, rows)]] if direct else found


def tile_kernel(epoch, chunk, direct, members, shard_tiles, tile, pieces, *refs):
    start_up = epoch == 0 and chunk == 0
    first = chunk == 0
    refs = list(refs)

    def take(n):
        out, refs[:n] = refs[:n], []
        return out

    row_hbm, col_hbm, count_hbm, owner_hbm, ratings, mask_hbm = take(6)
    users = take(1) if start_up else take(2)
    sources = take(len(pieces))
    grad_in = take(0 if first else 1)
    own_in = take(1 if first and epoch > 0 else 0)
    outs = take(7 if direct else 4)
    grad_user, = take(1)
    if epoch == 0:
        items, old = take(2)
    if start_up:
        user_bf, user_t = take(2)
    else:
        user_bf, user_t = users
    (row_ref, col_ref, count_ref, owner_ref, mask, parts, held, slots, slot_row, slot_place,
     sem_tile, sem_item, sem_small) = take(13)
    errors = take(WIDE)
    if epoch == 0:
        items_f, = take(1)
    else:
        items, = take(1)
    if start_up:
        users_f, = take(1)

    me = lax.axis_index("grp")
    chunk_tiles = shard_tiles // CHUNKS
    rows = chunk_tiles * tile
    half = rows // 2
    bits_tile = chunk_tiles.bit_length() - 1
    bits_shard = shard_tiles.bit_length() - 1

    pairs = [(row_hbm, row_ref), (col_hbm, col_ref), (count_hbm, count_ref),
             (owner_hbm, owner_ref), (mask_hbm.at[epoch, 0, 0], mask)]
    if not first:
        pairs.append((grad_in[0], grad_user))
    if start_up:
        pairs.append((users[0], users_f))
    small = [
        pltpu.make_async_copy(src, dst, sem_small.at[i]) for i, (src, dst) in enumerate(pairs)
    ]
    for copy in small:
        copy.start()
    copies = []
    if epoch == 0:
        for r in range(members):
            start = pl.multiple_of((me ^ r) * (shard_tiles * tile) + chunk * rows, rows)
            copies.append(
                pltpu.make_async_copy(
                    sources[0].at[pl.ds(start, rows)], items_f.at[pl.ds(r * rows, rows)], sem_item.at[r]
                )
            )
    else:
        for source, columns in zip(sources, pieces):
            at = 0
            for r, start, width in columns:
                copies.append(
                    pltpu.make_async_copy(
                        source.at[:, pl.ds(at, width)], items.at[:, pl.ds(r * rows + start, width)],
                        sem_item.at[len(copies)],
                    )
                )
                at += width
    for copy in copies:
        copy.start()
    for copy in small[:4]:
        copy.wait()

    count = count_ref[0, epoch]

    def pick(t, found):
        col = col_ref[epoch, 0, 0, t]
        slots[found] = t
        slot_row[found] = row_ref[epoch, 0, 0, t]
        slot_place[found] = ((col >> bits_shard) ^ me) * chunk_tiles + (col & (chunk_tiles - 1))
        here = ((col >> bits_tile) & (CHUNKS - 1)) == chunk
        return found + jnp.where(here & (t < count), 1, 0).astype(jnp.int32)

    total = lax.fori_loop(0, col_ref.shape[3], pick, jnp.int32(0), unroll=16)

    def fetch(i):
        return pltpu.make_async_copy(ratings.at[epoch, 0, 0, slots[i]], held.at[i], sem_tile.at[i])

    def begin(i, _):
        fetch(i).start()
        return 0

    lax.fori_loop(0, total, begin, 0)

    parts[...] = jnp.zeros_like(parts)
    if first:
        grad_user[...] = jnp.zeros_like(grad_user)
    for copy in small[4:]:
        copy.wait()

    def user_tile(j, _):
        spot = pl.ds(pl.multiple_of(j * tile, tile), tile)
        part = users_f[spot].astype(BF16)
        user_bf[spot] = part
        user_t[:, spot] = part.T
        return 0

    if start_up:
        lax.fori_loop(0, users_f.shape[0] // tile, user_tile, 0, unroll=2)

    def item_tile(own, j, _):
        spot = pl.ds(pl.multiple_of(j * tile, tile), tile)
        items[:, spot] = items_f[spot].astype(BF16).T
        if own:
            old[:, spot] = items_f[spot].T
        return 0

    for r, copy in enumerate(copies):
        copy.wait()
        if epoch == 0:
            lax.fori_loop(
                r * chunk_tiles, (r + 1) * chunk_tiles, functools.partial(item_tile, r == 0), 0,
                unroll=2,
            )

    def spots(i):
        row = pl.multiple_of(slot_row[i] * tile, tile)
        place = pl.multiple_of(slot_place[i] * tile, tile)
        return pl.ds(row, tile), pl.ds(place, tile)

    def ready(j):
        for k in range(WIDE):
            i = WIDE * j + k

            @pl.when(i < total)
            def _():
                fetch(i).wait()

    def front(j):
        for k in range(WIDE):
            i = jnp.minimum(WIDE * j + k, total - 1)
            row, place = spots(i)
            predicted = jnp.dot(user_bf[row], items[:, place], preferred_element_type=F32)
            error = (predicted - held[i].astype(F32)).astype(BF16)
            errors[k][j & 1] = jnp.clip(error, -BIG, BIG)

    def back(j):
        adds = []
        for k in range(WIDE):
            valid = WIDE * j + k < total
            i = jnp.minimum(WIDE * j + k, total - 1)
            row, place = spots(i)
            weight = mask[pl.ds(slots[i], 1), :].astype(F32)
            weight = jnp.where(valid, weight, 0.0)
            error = errors[k][j & 1]
            user_add = over_rows(items[:, place], error)
            item_add = jnp.dot(
                user_t[:, row] * weight.astype(BF16), error, preferred_element_type=F32
            )
            adds.append((row, place, jnp.where(weight > 0.5, user_add, 0.0), item_add))
        return adds

    def add(adds):
        for row, place, user_add, item_add in adds:
            grad_user[:, row] += user_add
            parts[:, place] += item_add

    groups = (total + WIDE - 1) // WIDE

    @pl.when(total > 0)
    def _():
        ready(0)
        front(0)

    def step(j, _):
        ready(j + 1)
        adds = back(j)
        front(j + 1)
        add(adds)
        return 0

    lax.fori_loop(0, groups - 1, step, 0)

    @pl.when(total > 0)
    def _():
        add(back(groups - 1))

    for out, columns in zip(outs, chunk_columns(members, rows, direct)):
        at = 0
        for r, start, width in columns:
            out[:, at:at + width] = parts[:, pl.ds(r * rows + start, width)].astype(BF16)
            at += width
    if start_up:
        own = jnp.dot(user_t[...], user_bf[...], preferred_element_type=F32)
        own = owned(own, users_f.shape[0], owner_ref[0, epoch])
    elif first:
        own = own_in[0][...]
    if first:
        outs[0][:, members // 2 * half:] = own


def tile_call(
    epoch, chunk, direct, members, scalars, ratings, row_mask, users, sources, carried, own
):
    tile = ratings.shape[-1]
    slots = ratings.shape[3]
    start_up = epoch == 0 and chunk == 0
    first = chunk == 0
    user_rows, rank = users[0].shape
    pieces = [columns for _, columns in sources]
    sources = [array for array, _ in sources]
    if epoch == 0:
        block_rows = sources[0].shape[0]
    else:
        block_rows = sum(s.shape[1] for s in sources) * CHUNKS
    shard_tiles = block_rows // members // tile
    rows = shard_tiles // CHUNKS * tile
    sd = jax.ShapeDtypeStruct
    widths = [sum(w for _, _, w in columns) for columns in chunk_columns(members, rows, direct)]
    widths[0] += rank if first else 0
    out_shape = [sd((rank, width), BF16) for width in widths] + [sd((rank, user_rows), F32)]
    if epoch == 0:
        out_shape += [sd((rank, members * rows), BF16), sd((rank, rows), F32)]
    if start_up:
        out_shape += [sd((user_rows, rank), BF16), sd((rank, user_rows), BF16)]
    in_specs = [HBM] * 6 + ([HBM] if start_up else [VMEM] * 2)
    in_specs += [HBM if epoch == 0 else ANY] * len(sources)
    operands = [*scalars, ratings, row_mask, *users, *sources]
    if not first:
        in_specs += [ANY]
        operands += [carried]
    elif epoch > 0:
        in_specs += [VMEM]
        operands += [own]
    scratch = [
        *[pltpu.SMEM(s.shape, jnp.int32) for s in scalars],
        pltpu.VMEM((slots, tile), jnp.int32),
        pltpu.VMEM((rank, members * rows), F32),
        pltpu.VMEM((slots, tile, tile), BF16),
        *[pltpu.SMEM((slots + 1,), jnp.int32)] * 3,
        pltpu.SemaphoreType.DMA((slots,)),
        pltpu.SemaphoreType.DMA((2 * members,)),
        pltpu.SemaphoreType.DMA((7,)),
        *[pltpu.VMEM((2, tile, tile), BF16)] * WIDE,
    ]
    if epoch == 0:
        scratch.append(pltpu.VMEM((members * rows, rank), F32))
    else:
        scratch.append(pltpu.VMEM((rank, members * rows), BF16))
    if start_up:
        scratch.append(pltpu.VMEM((user_rows, rank), F32))
    return pl.pallas_call(
        functools.partial(
            tile_kernel, epoch, chunk, direct, members, shard_tiles, tile, pieces
        ),
        out_shape=out_shape,
        in_specs=in_specs,
        out_specs=[VMEM] * len(out_shape),
        scratch_shapes=scratch,
        compiler_params=params(40),
        cost_estimate=declared(f"tiles_{epoch}_{chunk}"),
        name=f"tiles_{epoch}_{chunk}",
    )(*operands)


def user_kernel(epoch, block_rows, owner_ref, users, grad, *refs):
    outs = 4 if epoch + 1 < SUB else 1
    pieces, outs = refs[:-outs], refs[-outs:]
    gram = over_rows(pieces[0][...], pieces[0][...])
    for piece in pieces[1:]:
        gram += over_rows(piece[...], piece[...])
    full = gram * (GRAM / block_rows) + ridge(users.shape[1])
    pull = jnp.dot(users[...], full, precision=lax.Precision.HIGHEST, preferred_element_type=F32)
    new = users[...] - LEARN * (grad[...].T + pull)
    outs[0][...] = new
    if len(outs) > 1:
        plain = new.astype(BF16)
        turned = new.T.astype(BF16)
        outs[1][...] = plain
        outs[2][...] = turned
        own = jnp.dot(turned, plain, preferred_element_type=F32)
        outs[3][...] = owned(own, users.shape[0], owner_ref[0, epoch + 1])


def user_call(epoch, block_rows, owners, users, grad, pieces):
    rows, rank = users.shape
    sd = jax.ShapeDtypeStruct
    out_shape = [sd(users.shape, F32)]
    if epoch + 1 < SUB:
        out_shape += [sd((rows, rank), BF16), sd((rank, rows), BF16), sd((rank, rank), BF16)]
    return pl.pallas_call(
        functools.partial(user_kernel, epoch, block_rows),
        out_shape=out_shape,
        in_specs=[pl.BlockSpec(memory_space=pltpu.SMEM)] + [VMEM] * (2 + len(pieces)),
        out_specs=[VMEM] * len(out_shape),
        compiler_params=params(40),
        cost_estimate=declared(f"users_{epoch}"),
        name=f"users_{epoch}",
    )(owners, users, grad, *pieces)


def summed(refs, names, r, width):
    total = None
    for ref, order in zip(refs, names):
        k = order.index(r)
        term = ref[:, k * width:(k + 1) * width].astype(F32)
        total = term if total is None else total + term
    return total


def mid_kernel(paths, grams, *refs):
    at = 0
    outs = refs[sum(len(names) for names, _, _ in paths) + grams:]
    gram_refs = refs[len(refs) - len(paths) - grams:len(refs) - len(paths)]
    for (names, going, width), out in zip(paths, outs):
        terms = refs[at:at + len(names)]
        at += len(names)
        for k, r in enumerate(going):
            out[:, k * width:(k + 1) * width] = summed(terms, names, r, width).astype(BF16)
    if grams:
        rank = outs[0].shape[0]
        total = gram_refs[0][:, gram_refs[0].shape[1] - rank:].astype(F32)
        for ref in gram_refs[1:]:
            total += ref[:, ref.shape[1] - rank:].astype(F32)
        outs[0][:, outs[0].shape[1] - rank:] = total.astype(BF16)


def mid_call(epoch, chunk, step, paths, grams):
    rank = paths[0][0][0][0].shape[0]
    specs, operands, out_shape = [], [], []
    for terms, going, width in paths:
        specs.append(([names for _, names in terms], going, width))
        operands += [array for array, _ in terms]
        extra = rank if grams and not out_shape else 0
        out_shape.append(jax.ShapeDtypeStruct((rank, len(going) * width + extra), BF16))
    operands += grams
    return pl.pallas_call(
        functools.partial(mid_kernel, specs, len(grams)),
        out_shape=out_shape,
        in_specs=[VMEM] * len(operands),
        out_specs=[VMEM] * len(out_shape),
        compiler_params=params(40),
        cost_estimate=declared(f"mid_{epoch}_{chunk}_{step}"),
        name=f"mid_{epoch}_{chunk}_{step}",
    )(*operands)


def item_kernel(epoch, count, rows, width, grams, items, *refs):
    terms_a, terms_b = refs[:count], refs[count:2 * count]
    gram_refs = refs[2 * count:2 * count + grams]
    refs = refs[2 * count + grams:]
    out = refs[0]
    rank = gram_refs[0].shape[0]
    gram = gram_refs[0][:, gram_refs[0].shape[1] - rank:]
    for ref in gram_refs[1:]:
        gram = (gram.astype(F32) + ref[:, ref.shape[1] - rank:].astype(F32)).astype(BF16)
    if grams > 1:
        refs[1][...] = gram
    zero = [[0]] * count
    grad = jnp.concatenate(
        [summed(terms_a, zero, 0, width), summed(terms_b, zero, 0, rows - width)], axis=1
    )
    if epoch == 0:
        high = items[...].astype(BF16)
        low = (items[...] - high.astype(F32)).astype(BF16)
        pull = over_columns(gram, high) + over_columns(gram, low)
    else:
        pull = over_columns(gram, items[...])
    new = items[...].astype(F32) - LEARN * (grad + pull)
    if epoch + 1 < SUB:
        out[...] = new.astype(BF16)
    else:
        out[:rows] = new.T.astype(BF16)
        if grams > 1:
            out[rows:] = gram


def item_call(epoch, chunk, shard_rows, items, terms_a, terms_b, grams):
    rank = grams[0].shape[0]
    rows = shard_rows // CHUNKS
    last = epoch + 1 == SUB
    tall = rows + (rank if len(grams) > 1 else 0)
    out_shape = [jax.ShapeDtypeStruct((tall, rank) if last else (rank, rows), BF16)]
    if len(grams) > 1:
        out_shape.append(jax.ShapeDtypeStruct((rank, rank), BF16))
    out = pl.pallas_call(
        functools.partial(
            item_kernel, epoch, len(terms_a), rows, rows // 2, len(grams)
        ),
        out_shape=out_shape,
        in_specs=[VMEM] * (1 + 2 * len(terms_a) + len(grams)),
        out_specs=[VMEM] * len(out_shape),
        compiler_params=params(40),
        cost_estimate=declared(f"items_{epoch}_{chunk}"),
        name=f"items_{epoch}_{chunk}",
    )(items, *terms_a, *terms_b, *grams)
    gram = out[1] if len(grams) > 1 else None
    return out[0], gram


def swapped(value, bit):
    length = lax.axis_size("grp")
    return lax.ppermute(value, "grp", [(i, i ^ bit) for i in range(length)])


def moved(value, bit):
    length, blocks = lax.axis_size("grp"), lax.axis_size("blk")
    pairs = [
        (b * length + i, (b + 1) % blocks * length + (i ^ bit))
        for b in range(blocks)
        for i in range(length)
    ]
    return lax.ppermute(value, ("blk", "grp"), pairs)


def orders_of(members):
    bits = [1 << i for i in range(members.bit_length() - 1)]
    return bits, bits[::-1]


def exchanged(out, members):
    return [swapped(send, order[0]) for send, order in zip((out[0], out[2]), orders_of(members))]


def scattered(epoch, chunk, out, arrived, members, widths):
    send_a, keep_a, _, keep_b = out[:4]
    orders = orders_of(members)
    names = [without(members, order[0]) for order in orders]
    terms = [[(keep_a, names[0])], [(keep_b, names[1])]]
    grams = [send_a] if chunk == 0 else []
    sends = []
    for step in range(len(orders[0])):
        for p in range(2):
            terms[p].append((arrived[p], names[p]))
        if grams:
            grams.append(arrived[0])
        if step + 1 == len(orders[0]):
            break
        paths = []
        for p in range(2):
            bit = orders[p][step + 1]
            paths.append((terms[p], [r for r in names[p] if r & bit], widths[p]))
            names[p] = [r for r in names[p] if not r & bit]
        sends = mid_call(epoch, chunk, step, paths, grams)
        arrived = [swapped(sends[p], orders[p][step + 1]) for p in range(2)]
    return [a for a, _ in terms[0]], [a for a, _ in terms[1]], grams, sends


def scattered_direct(epoch, chunk, out, arrived, members, widths):
    _, keep_a, _, keep_b = out[:4]
    orders = orders_of(members)
    names = [[r for r in without(members, order[0]) if r] for order in orders]
    terms = [[(keep_a, names[0])], [(keep_b, names[1])]]
    ended = [[moved(out[4 + p], orders[p][0])] for p in range(2)]
    own = moved(out[6], 0)
    arrived = [tied(array, own) for array in arrived]
    sends = []
    for step in range(len(orders[0]) - 1):
        paths, kinds = [], []
        for p in range(2):
            terms[p].append((arrived[p], names[p]))
            bit = orders[p][step + 1]
            paths.append((terms[p], [bit], widths[p]))
            kinds.append((p, True))
            going = [r for r in names[p] if r & bit and r != bit]
            names[p] = [r for r in names[p] if not r & bit]
            if going:
                paths.append((terms[p], going, widths[p]))
                kinds.append((p, False))
        sends = mid_call(epoch, chunk, step, paths, [])
        arrived = [None, None]
        for (p, alone), send in zip(kinds, sends):
            bit = orders[p][step + 1]
            if alone:
                ended[p].append(moved(send, bit))
            else:
                arrived[p] = swapped(send, bit)
    return own, ended[0], ended[1], sends


def final_kernel(rows, width, others, count, *refs):
    done, refs = refs[:others], refs[others:]
    items, own = refs[:2]
    sides = refs[2:2 + count], refs[2 + count:2 + 2 * count]
    out, held, sem = refs[2 + 2 * count:]

    def leave(c):
        spot = pl.ds(c * rows, rows)
        return pltpu.make_async_copy(held.at[spot], out.at[spot], sem.at[c])

    for c, ref in enumerate(done):
        held[c * rows:(c + 1) * rows] = ref[:rows].astype(F32)
        leave(c).start()
    gram = done[0][rows:]
    totals = []
    for side, start, size in zip(sides, (0, width), (width, rows - width)):
        total = own[:, start:start + size].astype(F32)
        for ref in side:
            total += ref[...].astype(F32)
        totals.append(total)
    grad = jnp.concatenate(totals, axis=1)
    new = items[...].astype(F32) - LEARN * (grad + over_columns(gram, items[...]))
    held[others * rows:] = new.T
    leave(others).start()
    for c in range(others + 1):
        leave(c).wait()


def final_call(done, items, own, side_a, side_b):
    rank, rows = items.shape
    operands = [*done, items, own, *side_a, *side_b]
    return pl.pallas_call(
        functools.partial(final_kernel, rows, rows // 2, len(done), len(side_a)),
        out_shape=jax.ShapeDtypeStruct((CHUNKS * rows, rank), F32),
        in_specs=[VMEM] * len(operands),
        out_specs=HBM,
        scratch_shapes=[
            pltpu.VMEM((CHUNKS * rows, rank), F32), pltpu.SemaphoreType.DMA((CHUNKS,))
        ],
        compiler_params=params(40),
        cost_estimate=declared("items_final"),
        name="items_final",
    )(*operands)


def tied(value, *others):
    return lax.optimization_barrier((value, *others))[0]


def gathered(shard, after):
    length = lax.axis_size("grp")
    rows, half = shard.shape[1], shard.shape[1] // 2
    known = {0: [moved(tied(shard, *after), 0)]}
    for bit in orders_of(length)[0]:
        known[bit] = [moved(shard, bit)]
    near = [known[bit][0] for bit in orders_of(length)[0]]

    def cut(r, p):
        pieces = known[r]
        if len(pieces) == 2:
            return pieces[p]
        return pieces[0][:, half:] if p else pieces[0][:, :half]

    for r in range(1, length):
        if r not in known:
            low, high = r & -r, 1 << (r.bit_length() - 1)
            sent = [cut(r ^ high, 0), cut(r ^ low, 1)]
            sent = [tied(piece, *after) for piece in sent]
            known[r] = [swapped(sent[0], high), swapped(sent[1], low)]
    found = []
    for r, pieces in known.items():
        spots = [(0, rows)] if len(pieces) == 1 else [(0, half), (half, rows - half)]
        found += [(piece, [(r, *spot)]) for piece, spot in zip(pieces, spots)]
    return found, near


def local(ratings, row_index, col_index, row_mask, counts, owner_list, user_factors, item_factors):
    members = lax.axis_size("grp")
    block_rows = item_factors.shape[0]
    shard_rows = block_rows // members
    rows = shard_rows // CHUNKS
    owners = owner_list.reshape(1, -1)
    row_index, col_index, counts, owner_hbm, row_mask, first_users, ratings, item_factors = (
        pltpu.with_memory_space_constraint(array, pltpu.HBM)
        for array in (
            row_index, col_index, counts.reshape(1, -1), owners, row_mask, user_factors, ratings,
            item_factors,
        )
    )
    scalars = (row_index, col_index, counts, owner_hbm)
    full_users = user_factors
    users = [first_users]
    own_gram = None
    gathers = []
    for epoch in range(SUB):
        grad_user = None
        outs, olds, pieces = [], [], []
        for c in range(CHUNKS):
            if epoch == 0:
                sources = [(item_factors, None)]
            else:
                sources = gathers[c]
            direct = epoch + 1 == SUB and c + 1 == CHUNKS
            out = tile_call(
                epoch, c, direct, members, scalars, ratings, row_mask, users, sources, grad_user,
                own_gram,
            )
            grad_user = out[7 if direct else 4]
            outs.append(out)
            if epoch == 0:
                pieces.append(out[5])
                olds.append(out[6])
                if c == 0:
                    users = out[7:9]
            else:
                pieces += [array for array, _ in sources]
                olds.append(sources[0][0])
        last = epoch + 1 == SUB
        if last:
            kept = moved(tied(olds[-1], grad_user), 0)
        if not last:
            new_users = user_call(epoch, block_rows, owners, full_users, grad_user, pieces)
            full_users = new_users[0]
        shards = []
        grams = None
        reduced = []
        ahead = None
        for c in range(CHUNKS):
            arrived = ahead if ahead else exchanged(outs[c], members)
            arrived = [tied(array, grad_user if last else outs[-1][4]) for array in arrived]
            if last:
                if c == 0:
                    ahead = exchanged(outs[1], members)
                else:
                    arrived = [tied(array, grad_user, kept) for array in ahead]
            reduce = scattered_direct if last and c + 1 == CHUNKS else scattered
            reduced.append(
                reduce(epoch, c, outs[c], arrived, members, (rows // 2, rows - rows // 2))
            )
        for c in range(CHUNKS - 1 if last else CHUNKS):
            terms_a, terms_b, found, sent = reduced[c]
            old = olds[c]
            if not last:
                old = tied(old, *reduced[min(c + 1, CHUNKS - 1)][3])
                old = tied(old, full_users)
            shard, gram = item_call(epoch, c, shard_rows, old, terms_a, terms_b, found or grams)
            if found:
                grams = [gram]
            shards.append(shard)
        if last:
            done = [moved(shard, 0) for shard in shards]
            own, side_a, side_b, sent = reduced[-1]
            grad_user = tied(grad_user, *sent)
            item_final = final_call(done, kept, own, side_a, side_b)
            full_users = user_call(epoch, block_rows, owners, full_users, grad_user, pieces)[0]
        else:
            users, own_gram = new_users[1:3], new_users[3]
            gathers = [gathered(shard, [shards[-1]]) for shard in shards]
            near = gathers[-1][1]
            gathers = [found for found, _ in gathers]
            (array, columns), *rest = gathers[0]
            gathers[0] = [(tied(array, *near), columns), *rest]
    return full_users, item_final


def solution(mesh):
    in_specs = (
        P(None, "blk", "grp", None, None, None),
        P(None, "blk", "grp", None),
        P(None, "blk", "grp", None),
        P(None, "blk", "grp", None, None),
        P(None, "blk", "grp"),
        P(None, "blk"),
        P(("blk", "grp"), None),
        P("blk", None),
    )
    out_specs = (P(("blk", "grp"), None), P(("blk", "grp"), None))
    return jax.shard_map(local, mesh=mesh, in_specs=in_specs, out_specs=out_specs, check_vma=False)
```
